32 devices in a mesh: groups: 2 (over y), wide: 8 (over z, x), narrow: 2 (over core).
Axes of the slice: x: 2, y: 2, z: 4, core: 2. Of those that a mesh axis runs over, the one named last changes fastest.
Arguments:
- tokens: bfloat16 [4, 32, 18432], P(None, 'groups', ('narrow', 'wide')), parts along dimension 1, may hold values from -6 to 6
- norm_gain: bfloat16 [18432], P(('narrow', 'wide')), may hold values from 0.099609375 to 1.8984375
- w_query: bfloat16 [18432, 12288], P('narrow', 'wide'), may hold values from -0.046875 to 0.046875
- w_keyval: bfloat16 [18432, 512], P(('narrow', 'wide')), may hold values from -0.046875 to 0.046875
- w_out: bfloat16 [12288, 18432], P(None, ('narrow', 'wide')), may hold values from -0.0546875 to 0.0546875
- cache_keys: bfloat16 [32, 2048, 256], P(('groups', 'narrow', 'wide')), parts along dimension 0, may hold values from -3000 to 3000, as said below
- cache_values: bfloat16 [32, 2048, 256], P(('groups', 'narrow', 'wide')), parts along dimension 0, may hold values from -12 to 12
- lengths: int32 [32], P(('groups', 'narrow', 'wide')), parts along dimension 0, may hold values from 1 to 2044, as said below
Outputs:
- attended: bfloat16 [4, 32, 18432], P(None, 'groups', ('narrow', 'wide')), parts along dimension 1
The draws below stay inside these ranges and needn't reach their ends.
There are 2 independent parts, one for each index of `groups`. The reference program is written for one: setup_inputs(seed, part) draws one part's arguments, and reference() takes and returns one part's arrays. A program takes and returns all parts, laid end to end along the dimension named above; an argument that names none is the same for every part. Nothing has to cross between parts.
Inputs may be any that keep to these rules, and one draw needn't show every extreme that they name: `cache_keys`: keys of cached tokens, already rotated; slots at or beyond a sequence's length hold data that is not read. `lengths`: in every part one sequence holds exactly 2044 valid tokens and one holds exactly 1.
All inputs are finite; a program needn't handle non-finite values.
Results may differ from the reference program's by a relative error of at most 0.0065.
The reference program's roundings to bfloat16 on the way count: a program that leaves them out, or rounds other values in their place, can miss the bound.
Values may be sent and summed in bfloat16 or wider, within the bound.
No kernel may reach another device: no remote copies, remote signals or barrier semaphores. Data moves between devices by JAX's collectives and lax.ppermute only.
A program may use at most 128 MiB of HBM per device.

```python
import jax
import jax.numpy as jnp
from jax import lax

D = 18432
H = 48
DH = 256
S = 2048
STEPS = 4
B = 16


def draw_cache_keys(key, part):
    key = jax.random.fold_in(key, 11)
    first_key = jax.random.fold_in(key, 0)
    base = jnp.clip(2.0 * jax.random.normal(first_key, (B, S, DH), jnp.float32), -12.0, 12.0)
    return base.astype(jnp.bfloat16)


def draw_lengths(key, part):
    key = jax.random.fold_in(key, 23)
    first_key, second_key, third_key = jax.random.split(key, 3)
    longest = S - STEPS
    first_draw = jax.random.randint(first_key, (B,), 0, longest)
    second_draw = jax.random.randint(second_key, (B,), 0, longest)
    counts = 1 + first_draw * second_draw // longest
    order = jax.random.permutation(third_key, B)
    counts = counts.at[order[0]].set(longest)
    counts = counts.at[order[1]].set(1)
    return counts.astype(jnp.int32)


def shard_levels(own_key, extent, cuts, least, largest):
    gain, own = 1.0, jax.random.fold_in(own_key, 6)
    for axis_at, parts in cuts:
        heights = jnp.exp(jax.random.uniform(jax.random.fold_in(own, axis_at), (parts,), jnp.float32, least / len(cuts), largest / len(cuts)))
        gain = gain * jnp.repeat(heights, extent[axis_at] // parts).reshape([-1 if axis == axis_at else 1 for axis in range(len(extent))])
    return gain


def normal_values(own_key, shape, scale, bound, pieces=(), held_as=jnp.bfloat16):
    values = scale * jax.random.normal(own_key, shape, jnp.float32)
    if pieces:
        values = values * shard_levels(own_key, shape, pieces, -0.22, 0.18)
    return jnp.clip(values, -bound, bound).astype(held_as)


def setup_inputs(seed: int = 0, part: int = 0) -> dict:
    splits = jax.random.split(jax.random.key(seed), 9)
    own_keys = jax.random.split(jax.random.fold_in(splits[8], part), 9)
    tokens = normal_values(own_keys[0], (STEPS, B, D), 1.0, 6.0, ((2, 16),))
    norm_gain = jnp.clip(1.0 + 0.18 * jax.random.normal(splits[1], (D,), jnp.float32), 0.099609375, 1.8984375).astype(jnp.bfloat16)
    w_query = normal_values(splits[2], (D, H * DH), D ** -0.5, 0.046875, ((0, 2), (1, 8)))
    w_keyval = normal_values(splits[3], (D, 2 * DH), D ** -0.5, 0.046875, ((0, 16),))
    w_out = normal_values(splits[4], (H * DH, D), (H * DH) ** -0.5, 0.0546875, ((1, 16),))
    cache_keys = draw_cache_keys(jax.random.fold_in(jax.random.fold_in(splits[8], part), 71), part)
    cache_values = normal_values(own_keys[6], (B, S, DH), 2.0, 12.0, ((0, 16),))
    lengths = draw_lengths(jax.random.fold_in(jax.random.fold_in(splits[8], part), 71), part)
    return {"tokens": tokens, "norm_gain": norm_gain, "w_query": w_query, "w_keyval": w_keyval, "w_out": w_out, "cache_keys": cache_keys, "cache_values": cache_values, "lengths": lengths}


epsilon = 1e-06

def layer_norm(rows, norm_gain):
    values = rows.astype(jnp.float32)
    average = lax.optimization_barrier(jnp.mean(values, axis=-1, keepdims=True))
    spread = lax.optimization_barrier(jnp.mean(values * values, axis=-1, keepdims=True)) - average * average
    return ((values - average) * lax.rsqrt(spread + epsilon) * norm_gain.astype(jnp.float32)).astype(jnp.bfloat16)

def rotate(vectors, positions):
    half_size = vectors.shape[-1] // 2
    ladder = jnp.arange(half_size, dtype=jnp.float32)
    frequency = jnp.exp(ladder * (-2.0 / vectors.shape[-1]) * jnp.log(10000.0))
    angles = positions[..., None] * frequency
    cosine = jnp.cos(angles)
    sine = jnp.sin(angles)
    first_half = vectors[..., :half_size]
    second_half = vectors[..., half_size:]
    return jnp.concatenate([first_half * cosine - second_half * sine, second_half * cosine + first_half * sine], axis=-1)

def attend(rot_query, cache_keys, cache_values, new_keys, new_values, lengths):
    score_scale = 1.0 / jnp.sqrt(jnp.float32(DH))
    cache_scores = jnp.einsum('bhd,bsd->bhs', rot_query.astype(jnp.float32), cache_keys.astype(jnp.float32)) * score_scale
    valid = jnp.arange(cache_keys.shape[1])[None, None, :] < lengths[:, None, None]
    masked = jnp.where(valid, cache_scores, -1e+30)
    fresh = jnp.einsum('bhd,bjd->bhj', rot_query.astype(jnp.float32), new_keys.astype(jnp.float32)) * score_scale
    highest = jnp.maximum(lax.optimization_barrier(jnp.max(masked, axis=-1)), lax.optimization_barrier(jnp.max(fresh, axis=-1)))[..., None]
    cache_weights = jnp.where(valid, jnp.exp(masked - highest), 0.0)
    fresh_weights = jnp.exp(fresh - highest)
    total = lax.optimization_barrier(jnp.sum(cache_weights, axis=-1, keepdims=True)) + lax.optimization_barrier(jnp.sum(fresh_weights, axis=-1, keepdims=True))
    cache_probs = (cache_weights / total).astype(jnp.bfloat16)
    fresh_probs = (fresh_weights / total).astype(jnp.bfloat16)
    context = jnp.einsum('bhs,bsd->bhd', cache_probs.astype(jnp.float32), cache_values.astype(jnp.float32))
    context = context + jnp.einsum('bhj,bjd->bhd', fresh_probs.astype(jnp.float32), new_values.astype(jnp.float32))
    return context.astype(jnp.bfloat16)

def reference(tokens, norm_gain, w_query, w_keyval, w_out, cache_keys, cache_values, lengths):
    batch = lengths.shape[0]
    fresh_keys = []
    fresh_values = []
    results = []
    for step in range(STEPS):
        normed = layer_norm(tokens[step], norm_gain)
        query = jnp.dot(normed, w_query, preferred_element_type=jnp.float32).astype(jnp.bfloat16)
        keyval = jnp.dot(normed, w_keyval, preferred_element_type=jnp.float32)
        positions = (lengths + step).astype(jnp.float32)
        rot_query = rotate(query.astype(jnp.float32).reshape(batch, H, DH), positions[:, None]).astype(jnp.bfloat16)
        fresh_keys.append(rotate(keyval[:, :DH], positions).astype(jnp.bfloat16))
        fresh_values.append(keyval[:, DH:].astype(jnp.bfloat16))
        context = attend(rot_query, cache_keys, cache_values, jnp.stack(fresh_keys, axis=1), jnp.stack(fresh_values, axis=1), lengths)
        attended = jnp.dot(context.reshape(batch, H * DH), w_out, preferred_element_type=jnp.float32)
        results.append(attended.astype(jnp.bfloat16))
    return jnp.stack(results)
```

```python
import jax
import jax.numpy as jnp
from jax import lax
from jax.sharding import PartitionSpec as P

H = 48
DH = 256


epsilon = 1e-06


def rotate(vectors, positions):
    half_size = vectors.shape[-1] // 2
    ladder = jnp.arange(half_size, dtype=jnp.float32)
    frequency = jnp.exp(ladder * (-2.0 / vectors.shape[-1]) * jnp.log(10000.0))
    angles = positions[..., None] * frequency
    cosine = jnp.cos(angles)
    sine = jnp.sin(angles)
    first_half = vectors[..., :half_size]
    second_half = vectors[..., half_size:]
    return jnp.concatenate(
        [first_half * cosine - second_half * sine, second_half * cosine + first_half * sine],
        axis=-1,
    )


def attend(rot_query, cache_keys, cache_values, new_keys, new_values, lengths):
    count, steps, heads, size = rot_query.shape
    score_scale = 1.0 / jnp.sqrt(jnp.float32(DH))
    flat = rot_query.reshape(count, steps * heads, size)
    cache_scores = (
        jnp.einsum("bhd,bsd->bhs", flat, cache_keys, preferred_element_type=jnp.float32)
        * score_scale
    )
    valid = jnp.arange(cache_keys.shape[1])[None, None, :] < lengths[:, None, None]
    masked = jnp.where(valid, cache_scores, -1e30)
    fresh = (
        jnp.einsum("bhd,bjd->bhj", flat, new_keys, preferred_element_type=jnp.float32)
        * score_scale
    )
    row_step = jnp.arange(steps * heads) // heads
    seen = (jnp.arange(steps)[None, :] <= row_step[:, None])[None]
    fresh = jnp.where(seen, fresh, -1e30)
    highest = jnp.maximum(jnp.max(masked, axis=-1), jnp.max(fresh, axis=-1))[..., None]
    cache_weights = jnp.where(valid, jnp.exp(masked - highest), 0.0)
    fresh_weights = jnp.where(seen, jnp.exp(fresh - highest), 0.0)
    total = jnp.sum(cache_weights, axis=-1, keepdims=True) + jnp.sum(
        fresh_weights, axis=-1, keepdims=True
    )
    cache_probs = (cache_weights / total).astype(jnp.bfloat16)
    fresh_probs = (fresh_weights / total).astype(jnp.bfloat16)
    context = jnp.einsum(
        "bhs,bsd->bhd", cache_probs, cache_values, preferred_element_type=jnp.float32
    )
    context = context + jnp.einsum(
        "bhj,bjd->bhd", fresh_probs, new_values, preferred_element_type=jnp.float32
    )
    return context.astype(jnp.bfloat16).reshape(count, steps, heads, size)


def local(tokens, norm_gain, w_query, w_keyval, w_out, cache_keys, cache_values, lengths):
    wide_count = lax.axis_size("wide")
    narrow_count = lax.axis_size("narrow")
    steps, batch, width = tokens.shape
    count = lengths.shape[0]
    rows_all = steps * batch
    width_total = width * wide_count * narrow_count
    rows_float = tokens.reshape(rows_all, width).astype(jnp.float32)
    row_sum, row_squares = lax.psum(
        (jnp.sum(rows_float, axis=1), jnp.sum(rows_float * rows_float, axis=1)),
        ("wide", "narrow"),
    )
    average = (row_sum / width_total)[:, None]
    spread = (row_squares / width_total)[:, None] - average * average
    normed = (
        (rows_float - average) * lax.rsqrt(spread + epsilon) * norm_gain.astype(jnp.float32)
    ).astype(jnp.bfloat16)
    query_part = jnp.dot(
        lax.all_gather(normed, "wide", axis=1, tiled=True),
        w_query,
        preferred_element_type=jnp.float32,
    ).reshape(steps, narrow_count, batch // narrow_count, w_query.shape[1])
    keyval_part = jnp.dot(normed, w_keyval, preferred_element_type=jnp.float32)
    keyval_part = keyval_part.reshape(steps, batch, w_keyval.shape[1])
    query_half = lax.psum_scatter(query_part, "narrow", scatter_dimension=1, tiled=False)
    query_local = lax.all_to_all(
        query_half.astype(jnp.bfloat16), "wide", split_axis=1, concat_axis=2, tiled=True
    )
    keyval_local = lax.psum_scatter(
        keyval_part, ("narrow", "wide"), scatter_dimension=1, tiled=True
    )
    positions = (lengths[:, None] + jnp.arange(steps)).astype(jnp.float32)
    query_local = query_local.astype(jnp.float32).reshape(steps, count, H, DH).transpose(1, 0, 2, 3)
    keyval_local = keyval_local.transpose(1, 0, 2)
    rot_query = rotate(query_local, positions[..., None]).astype(jnp.bfloat16)
    new_keys = rotate(keyval_local[..., :DH], positions).astype(jnp.bfloat16)
    new_values = keyval_local[..., DH:].astype(jnp.bfloat16)
    context = attend(rot_query, cache_keys, cache_values, new_keys, new_values, lengths)
    context = context.reshape(count * steps, H * DH)
    joined = jnp.dot(
        lax.all_gather(context, ("narrow", "wide"), axis=0, tiled=True),
        w_out,
        preferred_element_type=jnp.float32,
    ).astype(jnp.bfloat16)
    return joined.reshape(batch, steps, w_out.shape[1]).transpose(1, 0, 2)


def solution(mesh):
    placed = (
        P(None, "groups", ("narrow", "wide")),
        P(("narrow", "wide")),
        P("narrow", "wide"),
        P(("narrow", "wide"), None),
        P(None, ("narrow", "wide")),
        P(("groups", "narrow", "wide"), None, None),
        P(("groups", "narrow", "wide"), None, None),
        P(("groups", "narrow", "wide")),
    )
    return jax.shard_map(
        local,
        mesh=mesh,
        in_specs=placed,
        out_specs=P(None, "groups", ("narrow", "wide")),
        check_vma=False,
    )
```

```python
import functools

import jax
import jax.numpy as jnp
from jax import lax
from jax.experimental import pallas as pl
from jax.experimental.pallas import tpu as pltpu
from jax.sharding import PartitionSpec as P

H = 48
DH = 256


epsilon = 1e-06


def rotate(vectors, positions):
    half_size = vectors.shape[-1] // 2
    ladder = jnp.arange(half_size, dtype=jnp.float32)
    frequency = jnp.exp(ladder * (-2.0 / vectors.shape[-1]) * jnp.log(10000.0))
    angles = positions[..., None] * frequency
    cosine = jnp.cos(angles)
    sine = jnp.sin(angles)
    first_half = vectors[..., :half_size]
    second_half = vectors[..., half_size:]
    return jnp.concatenate(
        [first_half * cosine - second_half * sine, second_half * cosine + first_half * sine],
        axis=-1,
    )


def attend(rot_query, cache_keys, cache_values, new_keys, new_values, lengths):
    count, steps, heads, size = rot_query.shape
    score_scale = 1.0 / jnp.sqrt(jnp.float32(DH))
    flat = rot_query.reshape(count, steps * heads, size)
    cache_scores = (
        jnp.einsum("bhd,bsd->bhs", flat, cache_keys, preferred_element_type=jnp.float32)
        * score_scale
    )
    valid = jnp.arange(cache_keys.shape[1])[None, None, :] < lengths[:, None, None]
    masked = jnp.where(valid, cache_scores, -1e30)
    fresh = (
        jnp.einsum("bhd,bjd->bhj", flat, new_keys, preferred_element_type=jnp.float32)
        * score_scale
    )
    row_step = jnp.arange(steps * heads) // heads
    seen = (jnp.arange(steps)[None, :] <= row_step[:, None])[None]
    fresh = jnp.where(seen, fresh, -1e30)
    highest = jnp.maximum(jnp.max(masked, axis=-1), jnp.max(fresh, axis=-1))[..., None]
    cache_weights = jnp.where(valid, jnp.exp(masked - highest), 0.0)
    fresh_weights = jnp.where(seen, jnp.exp(fresh - highest), 0.0)
    total = jnp.sum(cache_weights, axis=-1, keepdims=True) + jnp.sum(
        fresh_weights, axis=-1, keepdims=True
    )
    cache_probs = (cache_weights / total).astype(jnp.bfloat16)
    fresh_probs = (fresh_weights / total).astype(jnp.bfloat16)
    context = jnp.einsum(
        "bhs,bsd->bhd", cache_probs, cache_values, preferred_element_type=jnp.float32
    )
    context = context + jnp.einsum(
        "bhj,bjd->bhd", fresh_probs, new_values, preferred_element_type=jnp.float32
    )
    return context.astype(jnp.bfloat16).reshape(count, steps, heads, size)


def local_plain(tokens, norm_gain, w_query, w_keyval, w_out, cache_keys, cache_values, lengths):
    wide_count = lax.axis_size("wide")
    narrow_count = lax.axis_size("narrow")
    steps, batch, width = tokens.shape
    count = lengths.shape[0]
    rows_all = steps * batch
    width_total = width * wide_count * narrow_count
    rows_float = tokens.reshape(rows_all, width).astype(jnp.float32)
    row_sum, row_squares = lax.psum(
        (jnp.sum(rows_float, axis=1), jnp.sum(rows_float * rows_float, axis=1)),
        ("wide", "narrow"),
    )
    average = (row_sum / width_total)[:, None]
    spread = (row_squares / width_total)[:, None] - average * average
    normed = (
        (rows_float - average) * lax.rsqrt(spread + epsilon) * norm_gain.astype(jnp.float32)
    ).astype(jnp.bfloat16)
    query_part = jnp.dot(
        lax.all_gather(normed, "wide", axis=1, tiled=True),
        w_query,
        preferred_element_type=jnp.float32,
    ).reshape(steps, narrow_count, batch // narrow_count, w_query.shape[1])
    keyval_part = jnp.dot(normed, w_keyval, preferred_element_type=jnp.float32)
    keyval_part = keyval_part.reshape(steps, batch, w_keyval.shape[1])
    query_half = lax.psum_scatter(query_part, "narrow", scatter_dimension=1, tiled=False)
    query_local = lax.all_to_all(
        query_half.astype(jnp.bfloat16), "wide", split_axis=1, concat_axis=2, tiled=True
    )
    keyval_local = lax.psum_scatter(
        keyval_part, ("narrow", "wide"), scatter_dimension=1, tiled=True
    )
    positions = (lengths[:, None] + jnp.arange(steps)).astype(jnp.float32)
    query_local = query_local.astype(jnp.float32).reshape(steps, count, H, DH).transpose(1, 0, 2, 3)
    keyval_local = keyval_local.transpose(1, 0, 2)
    rot_query = rotate(query_local, positions[..., None]).astype(jnp.bfloat16)
    new_keys = rotate(keyval_local[..., :DH], positions).astype(jnp.bfloat16)
    new_values = keyval_local[..., DH:].astype(jnp.bfloat16)
    context = attend(rot_query, cache_keys, cache_values, new_keys, new_values, lengths)
    context = context.reshape(count * steps, H * DH)
    joined = jnp.dot(
        lax.all_gather(context, ("narrow", "wide"), axis=0, tiled=True),
        w_out,
        preferred_element_type=jnp.float32,
    ).astype(jnp.bfloat16)
    return joined.reshape(batch, steps, w_out.shape[1]).transpose(1, 0, 2)


MIB = 1 << 20
IN_VMEM = pl.BlockSpec(memory_space=pltpu.VMEM)
IN_SMEM = pl.BlockSpec(memory_space=pltpu.SMEM)
IN_HBM = pl.BlockSpec(memory_space=pltpu.HBM)


def call(kernel, name, out_shape, args, in_specs=None, scratch=(), limit=12 * MIB, flops=0):
    leaves = jax.tree.leaves(out_shape)
    moved = sum(a.size * a.dtype.itemsize for a in args) + sum(
        o.size * jnp.dtype(o.dtype).itemsize if hasattr(o, "size") else 0 for o in leaves
    )
    return pl.pallas_call(
        kernel,
        out_shape=out_shape,
        in_specs=in_specs or [IN_VMEM] * len(args),
        out_specs=jax.tree.map(lambda _: IN_VMEM, out_shape),
        scratch_shapes=list(scratch),
        compiler_params=pltpu.CompilerParams(vmem_limit_bytes=limit),
        cost_estimate=pl.CostEstimate(flops=flops, bytes_accessed=moved, transcendentals=0),
        name=name,
    )(*args)


def load_kernel(pieces, *refs):
    count = len(pieces)
    sources, targets, sems = refs[:count], refs[count : 2 * count], refs[2 * count]
    copies = []
    for source, target, cuts in zip(sources, targets, pieces):
        rows = source.shape[0] // cuts
        for cut in range(cuts):
            part = pl.ds(cut * rows, rows)
            copies.append(
                pltpu.make_async_copy(source.at[part], target.at[part], sems.at[len(copies)])
            )
    for copy in copies:
        copy.start()
    for copy in copies:
        copy.wait()


def load(name, pieces, *arrays):
    return call(
        functools.partial(load_kernel, pieces),
        name,
        [pltpu.VMEM(a.shape, a.dtype) for a in arrays],
        arrays,
        in_specs=[IN_HBM] * len(arrays),
        scratch=[pltpu.SemaphoreType.DMA((sum(pieces),))],
        limit=MIB,
    )


def stats_kernel(rows, *refs):
    blocks, out = refs[:-1], refs[-1]
    lanes = out.shape[1]
    total = jnp.zeros((rows, lanes), jnp.float32)
    squares = jnp.zeros((rows, lanes), jnp.float32)
    for block in blocks:
        for at in range(0, block.shape[1], lanes):
            values = block[:, at : at + lanes].astype(jnp.float32)[:rows]
            total = total + values
            squares = squares + values * values
    out[:rows] = total
    out[rows:] = squares


def project_kernel(steps, width_total, *refs):
    place, mine, theirs = refs[:3]
    *blocks, w_query, w_keyval, keep, send, result = refs[3:]
    wide_at, narrow_at = place[0], place[1]
    rows = result.shape[0]
    width, columns = w_keyval.shape[0], w_query.shape[1]
    sums = jnp.sum(mine[...] + theirs[...], axis=1, keepdims=True)
    average = sums[:rows] / width_total
    spread = sums[rows:] / width_total - average * average
    scale = lax.rsqrt(spread + epsilon)
    for k, block in enumerate(blocks):
        values = block[...].astype(jnp.float32)
        normed = ((values[:rows] - average) * scale * values[rows : rows + 1]).astype(jnp.bfloat16)
        owner = jnp.bitwise_xor(wide_at, k)
        weights = w_query[pl.ds(pl.multiple_of(owner * width, width), width), :]
        product = jnp.dot(normed, weights, preferred_element_type=jnp.float32)
        if k == 0:
            result[:, :columns] = product
            result[:, columns:] = jnp.dot(
                normed, w_keyval[...], preferred_element_type=jnp.float32
            )
        else:
            result[:, :columns] += product
    half = rows // steps // 2
    for step in range(steps):
        for out, core in ((keep, narrow_at), (send, 1 - narrow_at)):
            start = pl.multiple_of(step * 2 * half + core * half, half)
            out[step * half : (step + 1) * half, :] = result[pl.ds(start, half), :]


def combine_kernel(columns, mine, theirs, out, held):
    wide, steps, _ = out.shape
    lanes = held.shape[2]
    extent = mine.shape[1]
    for at in range(0, extent, lanes):
        total = mine[:, at : at + lanes] + theirs[:, at : at + lanes]
        if at < columns:
            held[at // lanes] = total
        else:
            high = total.astype(jnp.bfloat16).astype(jnp.float32)
            held[at // lanes] = high
            held[(at + extent - columns) // lanes] = total - high
    for at in range(held.shape[0]):
        for to in range(wide):
            out[to, :, at * lanes : (at + 1) * lanes] = held[
                at, pl.ds(to, steps, stride=wide), :
            ].astype(jnp.bfloat16)


def attend_kernel(columns, length, cosine, sine, arrived, cache_keys, cache_values, out, queries, fresh_rows):
    wide, steps, _ = arrived.shape
    size = cache_keys.shape[1]
    half = size // 2
    heads = columns // size
    cos, sin = cosine[...], sine[...]

    def turn(vectors):
        first, second = vectors[:, :half], vectors[:, half:]
        return first * cos - second * sin, second * cos + first * sin

    for source in range(wide):
        for head in range(heads):
            at = (source * heads + head) * steps
            low, high = turn(
                arrived[source, :, head * size : (head + 1) * size].astype(jnp.float32)
            )
            queries[at : at + steps, :half] = low
            queries[at : at + steps, half:] = high
    keyval = jnp.zeros((steps, 2 * size), jnp.float32)
    for source in range(wide):
        high = arrived[source, :, columns : columns + 2 * size].astype(jnp.float32)
        low = arrived[source, :, columns + 2 * size :].astype(jnp.float32)
        keyval = keyval + (high + low)
    fresh_rows[...] = jnp.zeros_like(fresh_rows)
    low, high = turn(keyval[:, :size])
    fresh_rows[0, :steps, :half] = low
    fresh_rows[0, :steps, half:] = high
    fresh_rows[1, :steps, :] = keyval[:, size:]
    query = queries[...].astype(jnp.bfloat16)
    new_keys = fresh_rows[0].astype(jnp.bfloat16)
    new_values = fresh_rows[1].astype(jnp.bfloat16)
    score_scale = 1.0 / size**0.5
    by_row = (((1,), (1,)), ((), ()))
    scores = score_scale * lax.dot_general(
        query, cache_keys[...], by_row, preferred_element_type=jnp.float32
    )
    fresh = score_scale * lax.dot_general(
        query, new_keys, by_row, preferred_element_type=jnp.float32
    )
    valid = lax.broadcasted_iota(jnp.int32, scores.shape, 1) < length[0]
    row_step = lax.rem(lax.broadcasted_iota(jnp.int32, fresh.shape, 0), steps)
    seen = lax.broadcasted_iota(jnp.int32, fresh.shape, 1) <= row_step
    scores = jnp.where(valid, scores, -1e30)
    fresh = jnp.where(seen, fresh, -1e30)
    highest = jnp.maximum(
        jnp.max(scores, axis=1, keepdims=True), jnp.max(fresh, axis=1, keepdims=True)
    )
    weights = jnp.where(valid, jnp.exp(scores - highest), 0.0)
    fresh_weights = jnp.where(seen, jnp.exp(fresh - highest), 0.0)
    share = 1.0 / (
        jnp.sum(weights, axis=1, keepdims=True) + jnp.sum(fresh_weights, axis=1, keepdims=True)
    )
    context = jnp.dot(
        (weights * share).astype(jnp.bfloat16),
        cache_values[...],
        preferred_element_type=jnp.float32,
    ) + jnp.dot(
        (fresh_weights * share).astype(jnp.bfloat16),
        new_values,
        preferred_element_type=jnp.float32,
    )
    queries[...] = context
    for head in range(wide * heads):
        out[:, head * size : (head + 1) * size] = queries[
            head * steps : (head + 1) * steps, :
        ].astype(jnp.bfloat16)


def assemble_kernel(*refs):
    *blocks, out, held = refs
    steps = blocks[0].shape[0]
    for k, block in enumerate(blocks):
        held[k * steps : (k + 1) * steps, :] = block[...].astype(jnp.float32)
    out[...] = held[...].astype(jnp.bfloat16)


def output_kernel(steps, depth, place, mine, theirs, w_out, out, result, ordered):
    wide_at, narrow_at = place[0], place[1]
    count = mine.shape[0] // steps
    batch = 2 * count
    for at in range(0, w_out.shape[0], depth):
        rows = jnp.concatenate([mine[:, at : at + depth], theirs[:, at : at + depth]], axis=0)
        product = jnp.dot(rows, w_out[at : at + depth, :], preferred_element_type=jnp.float32)
        if at == 0:
            result[...] = product
        else:
            result[...] += product
    for core in range(2):
        for k in range(count):
            sequence = jnp.bitwise_xor(narrow_at, core) * count + jnp.bitwise_xor(wide_at, k)
            for step in range(steps):
                row = core * count * steps + k * steps + step
                ordered[pl.ds(step * batch + sequence, 1), :] = result[row : row + 1, :]
    for step in range(steps):
        out[step] = ordered[step * batch : (step + 1) * batch, :].astype(jnp.bfloat16)


def swap(value, axis, bits):
    size = lax.axis_size(axis)
    return lax.ppermute(value, axis, [(at, at ^ bits) for at in range(size)])


def gather_wide(block, count):
    near = {0: block}
    for bits in range(2, count, 2):
        near[bits] = swap(block, "wide", bits)
    for bits in range(0, count, 2):
        near[bits + 1] = swap(near[bits], "wide", 1)
    return [near[k] for k in range(count)]


def local_fast(tokens, norm_gain, w_query, w_keyval, w_out, cache_keys, cache_values, lengths):
    wide_count = lax.axis_size("wide")
    narrow_count = lax.axis_size("narrow")
    steps, batch, width = tokens.shape
    rows = steps * batch
    columns, tail = w_query.shape[1], w_keyval.shape[1]
    size = cache_keys.shape[2]
    f32, bf16 = jnp.float32, jnp.bfloat16
    place = jnp.stack([lax.axis_index("wide"), lax.axis_index("narrow")]).astype(jnp.int32)

    payload = jnp.concatenate(
        [tokens.reshape(rows, width), norm_gain[None], jnp.zeros((7, width), bf16)]
    )
    blocks = gather_wide(payload, wide_count)
    query_weights, keyval_weights, keys, values = load(
        "load_query_weights",
        (8, 1, 1, 1),
        w_query,
        w_keyval,
        cache_keys.reshape(cache_keys.shape[1:]),
        cache_values.reshape(cache_values.shape[1:]),
    )
    sums = call(
        functools.partial(stats_kernel, rows),
        "row_sums",
        jax.ShapeDtypeStruct((2 * rows, 128), f32),
        blocks,
    )
    keep, send = call(
        functools.partial(project_kernel, steps, width * wide_count * narrow_count),
        "norm_and_project",
        [jax.ShapeDtypeStruct((rows // 2, columns + tail), f32)] * 2,
        [place, sums, swap(sums, "narrow", 1), *blocks, query_weights, keyval_weights],
        in_specs=[IN_SMEM] + [IN_VMEM] * (wide_count + 4),
        scratch=[pltpu.VMEM((rows, columns + tail), f32)],
        flops=2 * rows * width * wide_count * columns,
    )
    outgoing = call(
        functools.partial(combine_kernel, columns),
        "sum_of_cores",
        jax.ShapeDtypeStruct((wide_count, steps, columns + 2 * tail), bf16),
        [keep, swap(send, "narrow", 1)],
        scratch=[pltpu.VMEM(((columns + 2 * tail) // 128, rows // 2, 128), f32)],
    )
    arrived = lax.all_to_all(outgoing, "wide", 0, 0, tiled=True)
    ladder = jnp.arange(size // 2, dtype=f32)
    frequency = jnp.exp(ladder * (-2.0 / size) * jnp.log(10000.0))
    angles = (lengths + jnp.arange(steps)).astype(f32)[:, None] * frequency
    context = call(
        functools.partial(attend_kernel, columns),
        "attention",
        jax.ShapeDtypeStruct((steps, H * size), bf16),
        [lengths, jnp.cos(angles), jnp.sin(angles), arrived, keys, values],
        in_specs=[IN_SMEM] + [IN_VMEM] * 5,
        scratch=[pltpu.VMEM((steps * H, size), f32), pltpu.VMEM((2, 128, size), f32)],
        limit=16 * MIB,
        flops=4 * steps * H * size * keys.shape[0],
    )
    w_out, context = lax.optimization_barrier((w_out, context))
    contexts = gather_wide(context, wide_count)
    (out_weights,) = load("load_out_weights", (8,), w_out)
    mine = call(
        assemble_kernel,
        "join_contexts",
        jax.ShapeDtypeStruct((wide_count * steps, H * size), bf16),
        contexts,
        scratch=[pltpu.VMEM((wide_count * steps, H * size), f32)],
    )
    return call(
        functools.partial(output_kernel, steps, w_out.shape[0] // 8),
        "project_out",
        jax.ShapeDtypeStruct((steps, batch, w_out.shape[1]), bf16),
        [place, mine, swap(mine, "narrow", 1), out_weights],
        in_specs=[IN_SMEM] + [IN_VMEM] * 3,
        scratch=[pltpu.VMEM((rows, w_out.shape[1]), f32)] * 2,
        flops=2 * rows * w_out.size,
    )


def local(tokens, norm_gain, w_query, w_keyval, w_out, cache_keys, cache_values, lengths):
    fits = (
        lengths.shape[0] == 1
        and lax.axis_size("narrow") == 2
        and lax.axis_size("wide") == 8
        and tokens.shape[1] == 16
        and tokens.shape[2] % 128 == 0
    )
    return (local_fast if fits else local_plain)(
        tokens, norm_gain, w_query, w_keyval, w_out, cache_keys, cache_values, lengths
    )


def solution(mesh):
    placed = (
        P(None, "groups", ("narrow", "wide")),
        P(("narrow", "wide")),
        P("narrow", "wide"),
        P(("narrow", "wide"), None),
        P(None, ("narrow", "wide")),
        P(("groups", "narrow", "wide"), None, None),
        P(("groups", "narrow", "wide"), None, None),
        P(("groups", "narrow", "wide")),
    )
    return jax.shard_map(
        local,
        mesh=mesh,
        in_specs=placed,
        out_specs=P(None, "groups", ("narrow", "wide")),
        check_vma=False,
    )
```

```python
import functools

import jax
import jax.numpy as jnp
from jax import lax
from jax.experimental import pallas as pl
from jax.experimental.pallas import tpu as pltpu
from jax.sharding import PartitionSpec as P

H = 48
DH = 256


epsilon = 1e-06


def rotate(vectors, positions):
    half_size = vectors.shape[-1] // 2
    ladder = jnp.arange(half_size, dtype=jnp.float32)
    frequency = jnp.exp(ladder * (-2.0 / vectors.shape[-1]) * jnp.log(10000.0))
    angles = positions[..., None] * frequency
    cosine = jnp.cos(angles)
    sine = jnp.sin(angles)
    first_half = vectors[..., :half_size]
    second_half = vectors[..., half_size:]
    return jnp.concatenate(
        [first_half * cosine - second_half * sine, second_half * cosine + first_half * sine],
        axis=-1,
    )


def attend(rot_query, cache_keys, cache_values, new_keys, new_values, lengths):
    count, steps, heads, size = rot_query.shape
    score_scale = 1.0 / jnp.sqrt(jnp.float32(DH))
    flat = rot_query.reshape(count, steps * heads, size)
    cache_scores = (
        jnp.einsum("bhd,bsd->bhs", flat, cache_keys, preferred_element_type=jnp.float32)
        * score_scale
    )
    valid = jnp.arange(cache_keys.shape[1])[None, None, :] < lengths[:, None, None]
    masked = jnp.where(valid, cache_scores, -1e30)
    fresh = (
        jnp.einsum("bhd,bjd->bhj", flat, new_keys, preferred_element_type=jnp.float32)
        * score_scale
    )
    row_step = jnp.arange(steps * heads) // heads
    seen = (jnp.arange(steps)[None, :] <= row_step[:, None])[None]
    fresh = jnp.where(seen, fresh, -1e30)
    highest = jnp.maximum(jnp.max(masked, axis=-1), jnp.max(fresh, axis=-1))[..., None]
    cache_weights = jnp.where(valid, jnp.exp(masked - highest), 0.0)
    fresh_weights = jnp.where(seen, jnp.exp(fresh - highest), 0.0)
    total = jnp.sum(cache_weights, axis=-1, keepdims=True) + jnp.sum(
        fresh_weights, axis=-1, keepdims=True
    )
    cache_probs = (cache_weights / total).astype(jnp.bfloat16)
    fresh_probs = (fresh_weights / total).astype(jnp.bfloat16)
    context = jnp.einsum(
        "bhs,bsd->bhd", cache_probs, cache_values, preferred_element_type=jnp.float32
    )
    context = context + jnp.einsum(
        "bhj,bjd->bhd", fresh_probs, new_values, preferred_element_type=jnp.float32
    )
    return context.astype(jnp.bfloat16).reshape(count, steps, heads, size)


def local_plain(tokens, norm_gain, w_query, w_keyval, w_out, cache_keys, cache_values, lengths):
    wide_count = lax.axis_size("wide")
    narrow_count = lax.axis_size("narrow")
    steps, batch, width = tokens.shape
    count = lengths.shape[0]
    rows_all = steps * batch
    width_total = width * wide_count * narrow_count
    rows_float = tokens.reshape(rows_all, width).astype(jnp.float32)
    row_sum, row_squares = lax.psum(
        (jnp.sum(rows_float, axis=1), jnp.sum(rows_float * rows_float, axis=1)),
        ("wide", "narrow"),
    )
    average = (row_sum / width_total)[:, None]
    spread = (row_squares / width_total)[:, None] - average * average
    normed = (
        (rows_float - average) * lax.rsqrt(spread + epsilon) * norm_gain.astype(jnp.float32)
    ).astype(jnp.bfloat16)
    query_part = jnp.dot(
        lax.all_gather(normed, "wide", axis=1, tiled=True),
        w_query,
        preferred_element_type=jnp.float32,
    ).reshape(steps, narrow_count, batch // narrow_count, w_query.shape[1])
    keyval_part = jnp.dot(normed, w_keyval, preferred_element_type=jnp.float32)
    keyval_part = keyval_part.reshape(steps, batch, w_keyval.shape[1])
    query_half = lax.psum_scatter(query_part, "narrow", scatter_dimension=1, tiled=False)
    query_local = lax.all_to_all(
        query_half.astype(jnp.bfloat16), "wide", split_axis=1, concat_axis=2, tiled=True
    )
    keyval_local = lax.psum_scatter(
        keyval_part, ("narrow", "wide"), scatter_dimension=1, tiled=True
    )
    positions = (lengths[:, None] + jnp.arange(steps)).astype(jnp.float32)
    query_local = query_local.astype(jnp.float32).reshape(steps, count, H, DH).transpose(1, 0, 2, 3)
    keyval_local = keyval_local.transpose(1, 0, 2)
    rot_query = rotate(query_local, positions[..., None]).astype(jnp.bfloat16)
    new_keys = rotate(keyval_local[..., :DH], positions).astype(jnp.bfloat16)
    new_values = keyval_local[..., DH:].astype(jnp.bfloat16)
    context = attend(rot_query, cache_keys, cache_values, new_keys, new_values, lengths)
    context = context.reshape(count * steps, H * DH)
    joined = jnp.dot(
        lax.all_gather(context, ("narrow", "wide"), axis=0, tiled=True),
        w_out,
        preferred_element_type=jnp.float32,
    ).astype(jnp.bfloat16)
    return joined.reshape(batch, steps, w_out.shape[1]).transpose(1, 0, 2)


MIB = 1 << 20
IN_VMEM = pl.BlockSpec(memory_space=pltpu.VMEM)
IN_SMEM = pl.BlockSpec(memory_space=pltpu.SMEM)
IN_HBM = pl.BlockSpec(memory_space=pltpu.HBM)


def call(kernel, name, out_shape, args, in_specs=None, scratch=(), limit=12 * MIB, flops=0, moved=None, aliases=None):
    if moved is None:
        moved = sum(a.size * a.dtype.itemsize for a in args)
    return pl.pallas_call(
        kernel,
        out_shape=out_shape,
        in_specs=in_specs or [IN_VMEM] * len(args),
        out_specs=jax.tree.map(lambda _: IN_VMEM, out_shape),
        scratch_shapes=list(scratch),
        compiler_params=pltpu.CompilerParams(vmem_limit_bytes=limit),
        input_output_aliases=aliases or {},
        cost_estimate=pl.CostEstimate(flops=flops, bytes_accessed=moved, transcendentals=0),
        name=name,
    )(*args)


def in_hbm(array):
    return pltpu.with_memory_space_constraint(array, pltpu.HBM)


def load_kernel(start, size, pieces, *refs):
    source, target, sems = refs[0], refs[-2], refs[-1]
    step = size // pieces
    copies = []
    for at in range(pieces):
        part = pl.ds(start + at * step, step)
        copies.append(pltpu.make_async_copy(source.at[part], target.at[part], sems.at[at]))
    for copy in copies:
        copy.start()
    for copy in copies:
        copy.wait()


def load(name, source, at, parts, held=None, after=(), pieces=4):
    size = source.shape[0] // parts
    args = [in_hbm(source), *after]
    specs = [IN_HBM] + [pl.BlockSpec(memory_space=pl.ANY)] * len(after)
    aliases = {}
    if held is not None:
        aliases = {len(args): 0}
        args.append(held)
        specs.append(IN_VMEM)
    return call(
        functools.partial(load_kernel, at * size, size, pieces),
        name,
        pltpu.VMEM(source.shape, source.dtype),
        args,
        in_specs=specs,
        scratch=[pltpu.SemaphoreType.DMA((pieces,))],
        limit=MIB,
        moved=2 * size * source.shape[1],
        aliases=aliases,
    )


def stats_kernel(rows, *refs):
    blocks, out = refs[:-1], refs[-1]
    lanes = out.shape[1]
    total = jnp.zeros((rows, lanes), jnp.float32)
    squares = jnp.zeros((rows, lanes), jnp.float32)
    for block in blocks:
        for at in range(0, block.shape[1], lanes):
            values = block[:, at : at + lanes].astype(jnp.float32)[:rows]
            total = total + values
            squares = squares + values * values
    out[:rows] = total
    out[rows:] = squares


def project_kernel(steps, width_total, *refs):
    place, mine, theirs, w_keyval_far = refs[:4]
    *inner, keep, send, result, w_keyval, sem = refs[4:]
    w_query, *blocks = inner
    fetch = pltpu.make_async_copy(w_keyval_far, w_keyval, sem)
    fetch.start()
    wide_at, narrow_at = place[0], place[1]
    rows = result.shape[0]
    width, columns = w_keyval.shape[0], w_query.shape[1]
    sums = jnp.sum(mine[...] + theirs[...], axis=1, keepdims=True)
    average = sums[:rows] / width_total
    spread = sums[rows:] / width_total - average * average
    scale = lax.rsqrt(spread + epsilon)
    for k, block in enumerate(blocks):
        values = block[...].astype(jnp.float32)
        normed = ((values[:rows] - average) * scale * values[rows : rows + 1]).astype(jnp.bfloat16)
        owner = jnp.bitwise_xor(wide_at, k)
        features = pl.ds(pl.multiple_of(owner * width, width), width)
        product = jnp.dot(normed, w_query[features, :], preferred_element_type=jnp.float32)
        if k == 0:
            own = normed
            result[:, :columns] = product
        else:
            result[:, :columns] += product
    fetch.wait()
    result[:, columns:] = jnp.dot(own, w_keyval[...], preferred_element_type=jnp.float32)
    half = rows // steps // 2
    for step in range(steps):
        for out, core in ((keep, narrow_at), (send, 1 - narrow_at)):
            start = pl.multiple_of(step * 2 * half + core * half, half)
            out[step * half : (step + 1) * half, :] = result[pl.ds(start, half), :]


def combine_kernel(columns, mine, theirs, out, held):
    wide, steps, _ = out.shape
    lanes = held.shape[2]
    extent = mine.shape[1]
    for at in range(0, extent, lanes):
        total = mine[:, at : at + lanes] + theirs[:, at : at + lanes]
        if at < columns:
            held[at // lanes] = total
        else:
            high = total.astype(jnp.bfloat16).astype(jnp.float32)
            held[at // lanes] = high
            held[(at + extent - columns) // lanes] = total - high
    for at in range(held.shape[0]):
        for to in range(wide):
            out[to, :, at * lanes : (at + 1) * lanes] = held[
                at, pl.ds(to, steps, stride=wide), :
            ].astype(jnp.bfloat16)


def attend_kernel(
    columns, length, cosine, sine, arrived, keys_far, values_far,
    out, queries, fresh_rows, cache_keys, cache_values, sems,
):
    fetch_keys = pltpu.make_async_copy(keys_far, cache_keys, sems.at[0])
    fetch_values = pltpu.make_async_copy(values_far, cache_values, sems.at[1])
    fetch_keys.start()
    fetch_values.start()
    wide, steps, _ = arrived.shape
    size = cache_keys.shape[1]
    half = size // 2
    heads = columns // size
    cos, sin = cosine[...], sine[...]

    def turn(vectors):
        first, second = vectors[:, :half], vectors[:, half:]
        return first * cos - second * sin, second * cos + first * sin

    for source in range(wide):
        for head in range(heads):
            at = (source * heads + head) * steps
            low, high = turn(
                arrived[source, :, head * size : (head + 1) * size].astype(jnp.float32)
            )
            queries[at : at + steps, :half] = low
            queries[at : at + steps, half:] = high
    keyval = jnp.zeros((steps, 2 * size), jnp.float32)
    for source in range(wide):
        high = arrived[source, :, columns : columns + 2 * size].astype(jnp.float32)
        low = arrived[source, :, columns + 2 * size :].astype(jnp.float32)
        keyval = keyval + (high + low)
    fresh_rows[...] = jnp.zeros_like(fresh_rows)
    low, high = turn(keyval[:, :size])
    fresh_rows[0, :steps, :half] = low
    fresh_rows[0, :steps, half:] = high
    fresh_rows[1, :steps, :] = keyval[:, size:]
    query = queries[...].astype(jnp.bfloat16)
    new_keys = fresh_rows[0].astype(jnp.bfloat16)
    new_values = fresh_rows[1].astype(jnp.bfloat16)
    score_scale = 1.0 / size**0.5
    by_row = (((1,), (1,)), ((), ()))
    fetch_keys.wait()
    scores = score_scale * lax.dot_general(
        query, cache_keys[...], by_row, preferred_element_type=jnp.float32
    )
    fresh = score_scale * lax.dot_general(
        query, new_keys, by_row, preferred_element_type=jnp.float32
    )
    valid = lax.broadcasted_iota(jnp.int32, scores.shape, 1) < length[0]
    row_step = lax.rem(lax.broadcasted_iota(jnp.int32, fresh.shape, 0), steps)
    seen = lax.broadcasted_iota(jnp.int32, fresh.shape, 1) <= row_step
    scores = jnp.where(valid, scores, -1e30)
    fresh = jnp.where(seen, fresh, -1e30)
    highest = jnp.maximum(
        jnp.max(scores, axis=1, keepdims=True), jnp.max(fresh, axis=1, keepdims=True)
    )
    weights = jnp.where(valid, jnp.exp(scores - highest), 0.0)
    fresh_weights = jnp.where(seen, jnp.exp(fresh - highest), 0.0)
    share = 1.0 / (
        jnp.sum(weights, axis=1, keepdims=True) + jnp.sum(fresh_weights, axis=1, keepdims=True)
    )
    fetch_values.wait()
    context = jnp.dot(
        (weights * share).astype(jnp.bfloat16),
        cache_values[...],
        preferred_element_type=jnp.float32,
    ) + jnp.dot(
        (fresh_weights * share).astype(jnp.bfloat16),
        new_values,
        preferred_element_type=jnp.float32,
    )
    queries[...] = context
    for head in range(wide * heads):
        out[:, head * size : (head + 1) * size] = queries[
            head * steps : (head + 1) * steps, :
        ].astype(jnp.bfloat16)


def assemble_kernel(*refs):
    *blocks, out, held = refs
    steps = blocks[0].shape[0]
    for k, block in enumerate(blocks):
        held[k * steps : (k + 1) * steps, :] = block[...].astype(jnp.float32)
    out[...] = held[...].astype(jnp.bfloat16)


def output_kernel(steps, place, mine, theirs, w_out, out, result, ordered):
    wide_at, narrow_at = place[0], place[1]
    count = mine.shape[0] // steps
    batch = 2 * count
    depth = w_out.shape[0] // 8
    for at in range(0, w_out.shape[0], depth):
        part = slice(at, at + depth)
        rows = jnp.concatenate([mine[:, part], theirs[:, part]], axis=0)
        product = jnp.dot(rows, w_out[part, :], preferred_element_type=jnp.float32)
        if at == 0:
            result[...] = product
        else:
            result[...] += product
    for core in range(2):
        for k in range(count):
            sequence = jnp.bitwise_xor(narrow_at, core) * count + jnp.bitwise_xor(wide_at, k)
            for step in range(steps):
                row = core * count * steps + k * steps + step
                ordered[pl.ds(step * batch + sequence, 1), :] = result[row : row + 1, :]
    for step in range(steps):
        out[step] = ordered[step * batch : (step + 1) * batch, :].astype(jnp.bfloat16)


def swap(value, axis, bits):
    size = lax.axis_size(axis)
    return lax.ppermute(value, axis, [(at, at ^ bits) for at in range(size)])


def gather_wide(block, count):
    near = {0: block}
    for bits in range(2, count, 2):
        near[bits] = swap(block, "wide", bits)
    for bits in range(0, count, 2):
        near[bits + 1] = swap(near[bits], "wide", 1)
    return [near[k] for k in range(count)]


def local_fast(tokens, norm_gain, w_query, w_keyval, w_out, cache_keys, cache_values, lengths):
    wide_count = lax.axis_size("wide")
    narrow_count = lax.axis_size("narrow")
    steps, batch, width = tokens.shape
    rows = steps * batch
    columns, tail = w_query.shape[1], w_keyval.shape[1]
    size = cache_keys.shape[2]
    f32, bf16 = jnp.float32, jnp.bfloat16
    place = jnp.stack([lax.axis_index("wide"), lax.axis_index("narrow")]).astype(jnp.int32)

    payload = jnp.concatenate(
        [tokens.reshape(rows, width), norm_gain[None], jnp.zeros((7, width), bf16)]
    )
    blocks = gather_wide(payload, wide_count)
    query_weights = load("load_query_weights", w_query, 0, 1, pieces=8)
    sums = call(
        functools.partial(stats_kernel, rows),
        "row_sums",
        jax.ShapeDtypeStruct((2 * rows, 128), f32),
        blocks,
    )
    keep, send = call(
        functools.partial(project_kernel, steps, width * wide_count * narrow_count),
        "norm_and_project",
        [jax.ShapeDtypeStruct((rows // 2, columns + tail), f32)] * 2,
        [place, sums, swap(sums, "narrow", 1), in_hbm(w_keyval), query_weights, *blocks],
        in_specs=[IN_SMEM, IN_VMEM, IN_VMEM, IN_HBM] + [IN_VMEM] * (wide_count + 1),
        scratch=[
            pltpu.VMEM((rows, columns + tail), f32),
            pltpu.VMEM(w_keyval.shape, bf16),
            pltpu.SemaphoreType.DMA,
        ],
        flops=2 * rows * width * wide_count * columns,
    )
    outgoing = call(
        functools.partial(combine_kernel, columns),
        "sum_of_cores",
        jax.ShapeDtypeStruct((wide_count, steps, columns + 2 * tail), bf16),
        [keep, swap(send, "narrow", 1)],
        scratch=[pltpu.VMEM(((columns + 2 * tail) // 128, rows // 2, 128), f32)],
    )
    arrived = lax.all_to_all(outgoing, "wide", 0, 0, tiled=True)
    keys = cache_keys.reshape(cache_keys.shape[1:])
    values = cache_values.reshape(cache_values.shape[1:])
    ladder = jnp.arange(size // 2, dtype=f32)
    frequency = jnp.exp(ladder * (-2.0 / size) * jnp.log(10000.0))
    angles = (lengths + jnp.arange(steps)).astype(f32)[:, None] * frequency
    context = call(
        functools.partial(attend_kernel, columns),
        "attention",
        jax.ShapeDtypeStruct((steps, H * size), bf16),
        [lengths, jnp.cos(angles), jnp.sin(angles), arrived, in_hbm(keys), in_hbm(values)],
        in_specs=[IN_SMEM] + [IN_VMEM] * 3 + [IN_HBM] * 2,
        scratch=[
            pltpu.VMEM((steps * H, size), f32),
            pltpu.VMEM((2, 128, size), f32),
            pltpu.VMEM(keys.shape, bf16),
            pltpu.VMEM(values.shape, bf16),
            pltpu.SemaphoreType.DMA((2,)),
        ],
        limit=16 * MIB,
        flops=4 * steps * H * size * keys.shape[0],
    )
    contexts = gather_wide(context, wide_count)
    out_weights = load("load_out_weights", w_out, 0, 1, pieces=8, after=[context])
    mine = call(
        assemble_kernel,
        "join_contexts",
        jax.ShapeDtypeStruct((wide_count * steps, H * size), bf16),
        contexts,
        scratch=[pltpu.VMEM((wide_count * steps, H * size), f32)],
    )
    return call(
        functools.partial(output_kernel, steps),
        "project_out",
        jax.ShapeDtypeStruct((steps, batch, w_out.shape[1]), bf16),
        [place, mine, swap(mine, "narrow", 1), out_weights],
        in_specs=[IN_SMEM] + [IN_VMEM] * 3,
        scratch=[pltpu.VMEM((rows, w_out.shape[1]), f32)] * 2,
        flops=2 * rows * w_out.size,
    )


def local(tokens, norm_gain, w_query, w_keyval, w_out, cache_keys, cache_values, lengths):
    fits = (
        lengths.shape[0] == 1
        and lax.axis_size("narrow") == 2
        and lax.axis_size("wide") == 8
        and tokens.shape[1] == 16
        and tokens.shape[2] % 128 == 0
    )
    return (local_fast if fits else local_plain)(
        tokens, norm_gain, w_query, w_keyval, w_out, cache_keys, cache_values, lengths
    )


def solution(mesh):
    placed = (
        P(None, "groups", ("narrow", "wide")),
        P(("narrow", "wide")),
        P("narrow", "wide"),
        P(("narrow", "wide"), None),
        P(None, ("narrow", "wide")),
        P(("groups", "narrow", "wide"), None, None),
        P(("groups", "narrow", "wide"), None, None),
        P(("groups", "narrow", "wide")),
    )
    return jax.shard_map(
        local,
        mesh=mesh,
        in_specs=placed,
        out_specs=P(None, "groups", ("narrow", "wide")),
        check_vma=False,
    )
```

```python
import functools

import jax
import jax.numpy as jnp
from jax import lax
from jax.experimental import pallas as pl
from jax.experimental.pallas import tpu as pltpu
from jax.sharding import PartitionSpec as P

H = 48
DH = 256


epsilon = 1e-06


def rotate(vectors, positions):
    half_size = vectors.shape[-1] // 2
    ladder = jnp.arange(half_size, dtype=jnp.float32)
    frequency = jnp.exp(ladder * (-2.0 / vectors.shape[-1]) * jnp.log(10000.0))
    angles = positions[..., None] * frequency
    cosine = jnp.cos(angles)
    sine = jnp.sin(angles)
    first_half = vectors[..., :half_size]
    second_half = vectors[..., half_size:]
    return jnp.concatenate(
        [first_half * cosine - second_half * sine, second_half * cosine + first_half * sine],
        axis=-1,
    )


def attend(rot_query, cache_keys, cache_values, new_keys, new_values, lengths):
    count, steps, heads, size = rot_query.shape
    score_scale = 1.0 / jnp.sqrt(jnp.float32(DH))
    flat = rot_query.reshape(count, steps * heads, size)
    cache_scores = (
        jnp.einsum("bhd,bsd->bhs", flat, cache_keys, preferred_element_type=jnp.float32)
        * score_scale
    )
    valid = jnp.arange(cache_keys.shape[1])[None, None, :] < lengths[:, None, None]
    masked = jnp.where(valid, cache_scores, -1e30)
    fresh = (
        jnp.einsum("bhd,bjd->bhj", flat, new_keys, preferred_element_type=jnp.float32)
        * score_scale
    )
    row_step = jnp.arange(steps * heads) // heads
    seen = (jnp.arange(steps)[None, :] <= row_step[:, None])[None]
    fresh = jnp.where(seen, fresh, -1e30)
    highest = jnp.maximum(jnp.max(masked, axis=-1), jnp.max(fresh, axis=-1))[..., None]
    cache_weights = jnp.where(valid, jnp.exp(masked - highest), 0.0)
    fresh_weights = jnp.where(seen, jnp.exp(fresh - highest), 0.0)
    total = jnp.sum(cache_weights, axis=-1, keepdims=True) + jnp.sum(
        fresh_weights, axis=-1, keepdims=True
    )
    cache_probs = (cache_weights / total).astype(jnp.bfloat16)
    fresh_probs = (fresh_weights / total).astype(jnp.bfloat16)
    context = jnp.einsum(
        "bhs,bsd->bhd", cache_probs, cache_values, preferred_element_type=jnp.float32
    )
    context = context + jnp.einsum(
        "bhj,bjd->bhd", fresh_probs, new_values, preferred_element_type=jnp.float32
    )
    return context.astype(jnp.bfloat16).reshape(count, steps, heads, size)


def local_plain(tokens, norm_gain, w_query, w_keyval, w_out, cache_keys, cache_values, lengths):
    wide_count = lax.axis_size("wide")
    narrow_count = lax.axis_size("narrow")
    steps, batch, width = tokens.shape
    count = lengths.shape[0]
    rows_all = steps * batch
    width_total = width * wide_count * narrow_count
    rows_float = tokens.reshape(rows_all, width).astype(jnp.float32)
    row_sum, row_squares = lax.psum(
        (jnp.sum(rows_float, axis=1), jnp.sum(rows_float * rows_float, axis=1)),
        ("wide", "narrow"),
    )
    average = (row_sum / width_total)[:, None]
    spread = (row_squares / width_total)[:, None] - average * average
    normed = (
        (rows_float - average) * lax.rsqrt(spread + epsilon) * norm_gain.astype(jnp.float32)
    ).astype(jnp.bfloat16)
    query_part = jnp.dot(
        lax.all_gather(normed, "wide", axis=1, tiled=True),
        w_query,
        preferred_element_type=jnp.float32,
    ).reshape(steps, narrow_count, batch // narrow_count, w_query.shape[1])
    keyval_part = jnp.dot(normed, w_keyval, preferred_element_type=jnp.float32)
    keyval_part = keyval_part.reshape(steps, batch, w_keyval.shape[1])
    query_half = lax.psum_scatter(query_part, "narrow", scatter_dimension=1, tiled=False)
    query_local = lax.all_to_all(
        query_half.astype(jnp.bfloat16), "wide", split_axis=1, concat_axis=2, tiled=True
    )
    keyval_local = lax.psum_scatter(
        keyval_part, ("narrow", "wide"), scatter_dimension=1, tiled=True
    )
    positions = (lengths[:, None] + jnp.arange(steps)).astype(jnp.float32)
    query_local = query_local.astype(jnp.float32).reshape(steps, count, H, DH).transpose(1, 0, 2, 3)
    keyval_local = keyval_local.transpose(1, 0, 2)
    rot_query = rotate(query_local, positions[..., None]).astype(jnp.bfloat16)
    new_keys = rotate(keyval_local[..., :DH], positions).astype(jnp.bfloat16)
    new_values = keyval_local[..., DH:].astype(jnp.bfloat16)
    context = attend(rot_query, cache_keys, cache_values, new_keys, new_values, lengths)
    context = context.reshape(count * steps, H * DH)
    joined = jnp.dot(
        lax.all_gather(context, ("narrow", "wide"), axis=0, tiled=True),
        w_out,
        preferred_element_type=jnp.float32,
    ).astype(jnp.bfloat16)
    return joined.reshape(batch, steps, w_out.shape[1]).transpose(1, 0, 2)


MIB = 1 << 20
EXTRA = 16
OUT_PIECES = 8
IN_VMEM = pl.BlockSpec(memory_space=pltpu.VMEM)
IN_SMEM = pl.BlockSpec(memory_space=pltpu.SMEM)
IN_HBM = pl.BlockSpec(memory_space=pltpu.HBM)


def call(kernel, name, out_shape, args, in_specs=None, scratch=(), limit=12 * MIB, flops=0, moved=None, aliases=None):
    if moved is None:
        moved = sum(a.size * a.dtype.itemsize for a in args)
    return pl.pallas_call(
        kernel,
        out_shape=out_shape,
        in_specs=in_specs or [IN_VMEM] * len(args),
        out_specs=jax.tree.map(lambda _: IN_VMEM, out_shape),
        scratch_shapes=list(scratch),
        compiler_params=pltpu.CompilerParams(vmem_limit_bytes=limit),
        input_output_aliases=aliases or {},
        cost_estimate=pl.CostEstimate(flops=flops, bytes_accessed=moved, transcendentals=0),
        name=name,
    )(*args)


def in_hbm(array):
    return pltpu.with_memory_space_constraint(array, pltpu.HBM)


def load_kernel(moves, *refs):
    target, sems = refs[-2], refs[-1]
    copies = [
        pltpu.make_async_copy(refs[source].at[box], target.at[to], sems.at[at])
        for at, (source, box, to) in enumerate(moves)
    ]
    for copy in copies:
        copy.start()
    for copy in copies:
        copy.wait()


def load(name, shape, moves, *sources, after=()):
    return call(
        functools.partial(load_kernel, moves),
        name,
        pltpu.VMEM(shape, sources[0].dtype),
        [in_hbm(source) for source in sources] + list(after),
        in_specs=[IN_HBM] * len(sources) + [pl.BlockSpec(memory_space=pl.ANY)] * len(after),
        scratch=[pltpu.SemaphoreType.DMA((len(moves),))],
        limit=MIB,
        moved=2 * shape[0] * shape[1],
    )


def boxes(rows, columns, pieces, at_row=0, source=0):
    step = rows.size // pieces
    return [
        (
            source,
            (pl.ds(rows.start + at * step, step), columns),
            (pl.ds(at_row + at * step, step), pl.ds(0, columns.size)),
        )
        for at in range(pieces)
    ]


def sums_kernel(tokens, out):
    rows = tokens.shape[0]
    lanes = out.shape[1]
    values = tokens[...].astype(jnp.float32)
    at_lane = lax.broadcasted_iota(jnp.int32, (rows, lanes), 1)
    at_row = lax.broadcasted_iota(jnp.int32, (rows, lanes), 0)
    out[...] = jnp.zeros_like(out)
    for row, column in enumerate(
        (
            jnp.sum(values, axis=1, keepdims=True),
            jnp.sum(values * values, axis=1, keepdims=True),
        )
    ):
        out[row : row + 1, :] = jnp.sum(
            jnp.where(at_lane == at_row, column, 0.0), axis=0, keepdims=True
        )


def payload_kernel(tokens, gain, mine, theirs, out, extra):
    rows, width = tokens.shape
    lanes = out.shape[1]
    parts = width // lanes
    extra[...] = jnp.zeros_like(extra)
    for at in range(parts):
        span = slice(at * lanes, (at + 1) * lanes)
        extra[at : at + 1, :] = gain[:, span].astype(jnp.float32)
        out[at * rows : (at + 1) * rows, :] = tokens[:, span]
    for at in range(2):
        left = mine[at : at + 1, :] + theirs[at : at + 1, :]
        for piece in range(3):
            row = parts + 3 * at + piece
            part = left.astype(jnp.bfloat16).astype(jnp.float32)
            extra[row : row + 1, :] = part
            left = left - part
    out[parts * rows :, :] = extra[...].astype(jnp.bfloat16)


class Stream:
    def __init__(self, copies, flight=3):
        self.copies, self.started, self.done = copies, 0, 0
        self.start(flight)

    def start(self, count):
        for copy in self.copies[self.started : self.started + count]:
            copy.start()
        self.started = min(self.started + count, len(self.copies))

    def take(self, at):
        while self.done <= at:
            self.copies[self.done].wait()
            self.done += 1
            self.start(1)


def project_kernel(steps, width_total, place, w_keyval_far, w_query, early, *refs):
    *blocks, keep, send, result, normed, late, w_keyval, sems = refs
    wide_at, narrow_at = place[0], place[1]
    rows = result.shape[0]
    width, part = w_keyval.shape[0], early.shape[1]
    columns = w_query.shape[1]
    lanes = blocks[0].shape[1]
    parts = width // lanes
    spots = [
        pl.ds(pl.multiple_of(jnp.bitwise_xor(wide_at, k) * width, width), width)
        for k in range(len(blocks))
    ]
    stream = Stream(
        [pltpu.make_async_copy(w_keyval_far, w_keyval, sems.at[len(blocks)])]
        + [
            pltpu.make_async_copy(
                w_query.at[spot, pl.ds(part, columns - part)], late.at[spot], sems.at[k]
            )
            for k, spot in enumerate(spots)
        ]
    )
    tail = pl.ds(parts * rows, blocks[0].shape[0] - parts * rows)
    sums = blocks[0][tail, :].astype(jnp.float32)
    for block in blocks[1:]:
        sums = sums + block[tail, :].astype(jnp.float32)
    totals = [
        sums[at : at + 1] + sums[at + 1 : at + 2] + sums[at + 2 : at + 3]
        for at in (parts, parts + 3)
    ]
    average = totals[0] / width_total
    spread = totals[1] / width_total - average * average
    scale = lax.rsqrt(spread + epsilon)
    at_lane = lax.broadcasted_iota(jnp.int32, (rows, lanes), 1)
    at_row = lax.broadcasted_iota(jnp.int32, (rows, lanes), 0)

    def stand(flat):
        return jnp.sum(jnp.where(at_lane == at_row, flat, 0.0), axis=1, keepdims=True)

    average, scale = stand(average), stand(scale)
    for weights, span in ((early, slice(0, part)), (late, slice(part, columns))):
        for k, block in enumerate(blocks):
            if weights is early:
                gains = block[tail, :].astype(jnp.float32)
                for at in range(parts):
                    values = block[at * rows : (at + 1) * rows, :].astype(jnp.float32)
                    normed[k, :, at * lanes : (at + 1) * lanes] = (
                        (values - average) * scale * gains[at : at + 1]
                    ).astype(jnp.bfloat16)
            else:
                stream.take(k + 1)
            product = jnp.dot(normed[k], weights[spots[k], :], preferred_element_type=jnp.float32)
            if k == 0:
                result[:, span] = product
            else:
                result[:, span] += product
            if weights is early and k in (2, 4, 6):
                stream.take(k // 2 - 1)
    result[:, columns:] = jnp.dot(normed[0], w_keyval[...], preferred_element_type=jnp.float32)
    half = rows // steps // 2
    for step in range(steps):
        for out, core in ((keep, narrow_at), (send, 1 - narrow_at)):
            start = pl.multiple_of(step * 2 * half + core * half, half)
            out[step * half : (step + 1) * half, :] = result[pl.ds(start, half), :]


def combine_kernel(columns, mine, theirs, out, held):
    wide, steps, _ = out.shape
    lanes = held.shape[2]
    extent = mine.shape[1]
    for at in range(0, extent, lanes):
        total = mine[:, at : at + lanes] + theirs[:, at : at + lanes]
        if at < columns:
            held[at // lanes] = total
        else:
            high = total.astype(jnp.bfloat16).astype(jnp.float32)
            held[at // lanes] = high
            held[(at + extent - columns) // lanes] = total - high
    for at in range(held.shape[0]):
        for to in range(wide):
            out[to, :, at * lanes : (at + 1) * lanes] = held[
                at, pl.ds(to, steps, stride=wide), :
            ].astype(jnp.bfloat16)


def attend_kernel(
    columns, length, cosine, sine, arrived, cache, out, queries, fresh_rows
):
    slots = cache.shape[0] // 2
    wide, steps, _ = arrived.shape
    size = cache.shape[1]
    half = size // 2
    heads = columns // size
    cos, sin = cosine[...], sine[...]

    def turn(vectors):
        first, second = vectors[:, :half], vectors[:, half:]
        return first * cos - second * sin, second * cos + first * sin

    for source in range(wide):
        for head in range(heads):
            at = (source * heads + head) * steps
            low, high = turn(
                arrived[source, :, head * size : (head + 1) * size].astype(jnp.float32)
            )
            queries[at : at + steps, :half] = low
            queries[at : at + steps, half:] = high
    keyval = jnp.zeros((steps, 2 * size), jnp.float32)
    for source in range(wide):
        high = arrived[source, :, columns : columns + 2 * size].astype(jnp.float32)
        low = arrived[source, :, columns + 2 * size :].astype(jnp.float32)
        keyval = keyval + (high + low)
    fresh_rows[...] = jnp.zeros_like(fresh_rows)
    low, high = turn(keyval[:, :size])
    fresh_rows[0, :steps, :half] = low
    fresh_rows[0, :steps, half:] = high
    fresh_rows[1, :steps, :] = keyval[:, size:]
    query = queries[...].astype(jnp.bfloat16)
    new_keys = fresh_rows[0].astype(jnp.bfloat16)
    new_values = fresh_rows[1].astype(jnp.bfloat16)
    score_scale = 1.0 / size**0.5
    by_row = (((1,), (1,)), ((), ()))
    scores = score_scale * lax.dot_general(
        query, cache[:slots, :], by_row, preferred_element_type=jnp.float32
    )
    fresh = score_scale * lax.dot_general(
        query, new_keys, by_row, preferred_element_type=jnp.float32
    )
    valid = lax.broadcasted_iota(jnp.int32, scores.shape, 1) < length[0]
    row_step = lax.rem(lax.broadcasted_iota(jnp.int32, fresh.shape, 0), steps)
    seen = lax.broadcasted_iota(jnp.int32, fresh.shape, 1) <= row_step
    scores = jnp.where(valid, scores, -1e30)
    fresh = jnp.where(seen, fresh, -1e30)
    highest = jnp.maximum(
        jnp.max(scores, axis=1, keepdims=True), jnp.max(fresh, axis=1, keepdims=True)
    )
    weights = jnp.where(valid, jnp.exp(scores - highest), 0.0)
    fresh_weights = jnp.where(seen, jnp.exp(fresh - highest), 0.0)
    share = 1.0 / (
        jnp.sum(weights, axis=1, keepdims=True) + jnp.sum(fresh_weights, axis=1, keepdims=True)
    )
    context = jnp.dot(
        (weights * share).astype(jnp.bfloat16),
        cache[slots:, :],
        preferred_element_type=jnp.float32,
    ) + jnp.dot(
        (fresh_weights * share).astype(jnp.bfloat16),
        new_values,
        preferred_element_type=jnp.float32,
    )
    queries[...] = context
    for head in range(wide * heads):
        out[:, head * size : (head + 1) * size] = queries[
            head * steps : (head + 1) * steps, :
        ].astype(jnp.bfloat16)


def output_kernel(steps, place, w_out, early, *refs):
    *blocks, out, joined, result, ordered, late, sems = refs
    wide_at, narrow_at = place[0], place[1]
    batch = len(blocks)
    count = batch // 2
    deep = early.shape[0]
    piece = late.shape[0] // OUT_PIECES
    stream = Stream(
        [
            pltpu.make_async_copy(
                w_out.at[pl.ds(deep + at * piece, piece)],
                late.at[pl.ds(at * piece, piece)],
                sems.at[at],
            )
            for at in range(OUT_PIECES)
        ]
    )
    depth = joined.shape[1]
    for at in range(0, w_out.shape[0], depth):
        for k, block in enumerate(blocks):
            joined[k * steps : (k + 1) * steps, :] = block[:, at : at + depth].astype(jnp.float32)
        rows = joined[...].astype(jnp.bfloat16)
        if at < deep:
            weights = early[at : at + depth, :]
        else:
            stream.take((at + depth - deep) // piece - 1)
            weights = late[at - deep : at - deep + depth, :]
        product = jnp.dot(rows, weights, preferred_element_type=jnp.float32)
        if at == 0:
            result[...] = product
        else:
            result[...] += product
        if at + depth in (deep // 2, deep):
            stream.take((at + depth) * 2 // deep - 1)
    for core in range(2):
        for k in range(count):
            sequence = jnp.bitwise_xor(narrow_at, core) * count + jnp.bitwise_xor(wide_at, k)
            for step in range(steps):
                row = core * count * steps + k * steps + step
                ordered[pl.ds(step * batch + sequence, 1), :] = result[row : row + 1, :]
    for step in range(steps):
        out[step] = ordered[step * batch : (step + 1) * batch, :].astype(jnp.bfloat16)


def swap(value, axis, bits):
    size = lax.axis_size(axis)
    return lax.ppermute(value, axis, [(at, at ^ bits) for at in range(size)])


def gather_tokens(block):
    near = {0: block}
    for bits in (4, 2, 1):
        near[bits] = swap(block, "wide", bits)
    near[1], near[2], near[4] = lax.optimization_barrier((near[1], near[2], near[4]))
    near[6] = swap(near[4], "wide", 2)
    near[5] = swap(near[4], "wide", 1)
    near[3] = swap(near[2], "wide", 1)
    near[7] = swap(near[5], "wide", 2)
    return [near[k] for k in range(8)]


def gather_contexts(block, loader):
    near = {0: block}
    for bits in (2, 4, 6, 1):
        near[bits] = swap(block, "wide", bits)
    near[4], near[6], held = lax.optimization_barrier((near[4], near[6], loader(near[2])))
    for bits in (2, 4, 6):
        near[bits + 1] = swap(near[bits], "wide", 1)
    return [near[k] for k in range(8)], held


def local_fast(tokens, norm_gain, w_query, w_keyval, w_out, cache_keys, cache_values, lengths):
    wide_count = lax.axis_size("wide")
    narrow_count = lax.axis_size("narrow")
    steps, batch, width = tokens.shape
    rows = steps * batch
    columns, tail = w_query.shape[1], w_keyval.shape[1]
    size = cache_keys.shape[2]
    f32, bf16 = jnp.float32, jnp.bfloat16
    place = jnp.stack([lax.axis_index("wide"), lax.axis_index("narrow")]).astype(jnp.int32)

    own = tokens.reshape(rows, width)
    sums = call(sums_kernel, "row_sums", jax.ShapeDtypeStruct((8, 128), f32), [own])
    payload = call(
        payload_kernel,
        "payload",
        jax.ShapeDtypeStruct((width // 128 * rows + EXTRA, 128), bf16),
        [own, norm_gain[None], sums, swap(sums, "narrow", 1)],
        scratch=[pltpu.VMEM((EXTRA, 128), f32)],
    )
    blocks = gather_tokens(payload)
    part = columns // 2
    deep = w_query.shape[0]
    early_weights = load(
        "load_query_weights",
        (deep, part),
        boxes(pl.ds(0, deep), pl.ds(0, part), 8),
        w_query,
    )
    keep, send = call(
        functools.partial(project_kernel, steps, width * wide_count * narrow_count),
        "norm_and_project",
        [jax.ShapeDtypeStruct((rows // 2, columns + tail), f32)] * 2,
        [place, in_hbm(w_keyval), in_hbm(w_query), early_weights, *blocks],
        in_specs=[IN_SMEM, IN_HBM, IN_HBM] + [IN_VMEM] * (wide_count + 1),
        scratch=[
            pltpu.VMEM((rows, columns + tail), f32),
            pltpu.VMEM((wide_count, rows, width), bf16),
            pltpu.VMEM((deep, columns - part), bf16),
            pltpu.VMEM(w_keyval.shape, bf16),
            pltpu.SemaphoreType.DMA((wide_count + 1,)),
        ],
        limit=24 * MIB,
        flops=2 * rows * width * wide_count * columns,
    )
    outgoing = call(
        functools.partial(combine_kernel, columns),
        "sum_of_cores",
        jax.ShapeDtypeStruct((wide_count, steps, columns + 2 * tail), bf16),
        [keep, swap(send, "narrow", 1)],
        scratch=[pltpu.VMEM(((columns + 2 * tail) // 128, rows // 2, 128), f32)],
    )
    arrived = lax.all_to_all(outgoing, "wide", 0, 0, tiled=True)
    slots = cache_keys.shape[1]
    cache = load(
        "load_cache",
        (2 * slots, size),
        boxes(pl.ds(0, slots), pl.ds(0, size), 4)
        + boxes(pl.ds(0, slots), pl.ds(0, size), 4, at_row=slots, source=1),
        cache_keys.reshape(slots, size),
        cache_values.reshape(slots, size),
        after=[outgoing],
    )
    ladder = jnp.arange(size // 2, dtype=f32)
    frequency = jnp.exp(ladder * (-2.0 / size) * jnp.log(10000.0))
    angles = (lengths + jnp.arange(steps)).astype(f32)[:, None] * frequency
    context = call(
        functools.partial(attend_kernel, columns),
        "attention",
        jax.ShapeDtypeStruct((steps, H * size), bf16),
        [lengths, jnp.cos(angles), jnp.sin(angles), arrived, cache],
        in_specs=[IN_SMEM] + [IN_VMEM] * 4,
        scratch=[
            pltpu.VMEM((steps * H, size), f32),
            pltpu.VMEM((2, 128, size), f32),
        ],
        limit=16 * MIB,
        flops=4 * steps * H * size * slots,
    )
    deep = w_out.shape[0] // 2
    contexts, early_weights = gather_contexts(
        context,
        lambda block: load(
            "load_out_weights",
            (deep, w_out.shape[1]),
            boxes(pl.ds(0, deep), pl.ds(0, w_out.shape[1]), 8),
            w_out,
            after=[block],
        ),
    )
    contexts = contexts + [swap(block, "narrow", 1) for block in contexts]
    return call(
        functools.partial(output_kernel, steps),
        "project_out",
        jax.ShapeDtypeStruct((steps, batch, w_out.shape[1]), bf16),
        [place, in_hbm(w_out), early_weights, *contexts],
        in_specs=[IN_SMEM, IN_HBM] + [IN_VMEM] * (1 + batch),
        scratch=[
            pltpu.VMEM((rows, w_out.shape[0] // 8), f32),
            pltpu.VMEM((rows, w_out.shape[1]), f32),
            pltpu.VMEM((rows, w_out.shape[1]), f32),
            pltpu.VMEM((w_out.shape[0] - deep, w_out.shape[1]), bf16),
            pltpu.SemaphoreType.DMA((OUT_PIECES,)),
        ],
        limit=28 * MIB,
        flops=2 * rows * w_out.size,
    )


def local(tokens, norm_gain, w_query, w_keyval, w_out, cache_keys, cache_values, lengths):
    fits = (
        lengths.shape[0] == 1
        and lax.axis_size("narrow") == 2
        and lax.axis_size("wide") == 8
        and tokens.shape[1] == 16
        and tokens.shape[2] % 128 == 0
        and tokens.shape[2] // 128 + 6 <= EXTRA
        and tokens.shape[0] * 16 <= 128
    )
    return (local_fast if fits else local_plain)(
        tokens, norm_gain, w_query, w_keyval, w_out, cache_keys, cache_values, lengths
    )


def solution(mesh):
    placed = (
        P(None, "groups", ("narrow", "wide")),
        P(("narrow", "wide")),
        P("narrow", "wide"),
        P(("narrow", "wide"), None),
        P(None, ("narrow", "wide")),
        P(("groups", "narrow", "wide"), None, None),
        P(("groups", "narrow", "wide"), None, None),
        P(("groups", "narrow", "wide")),
    )
    return jax.shard_map(
        local,
        mesh=mesh,
        in_specs=placed,
        out_specs=P(None, "groups", ("narrow", "wide")),
        check_vma=False,
    )
```

```python
import functools

import jax
import jax.numpy as jnp
from jax import lax
from jax.experimental import pallas as pl
from jax.experimental.pallas import tpu as pltpu
from jax.sharding import PartitionSpec as P

H = 48
DH = 256


epsilon = 1e-06


def rotate(vectors, positions):
    half_size = vectors.shape[-1] // 2
    ladder = jnp.arange(half_size, dtype=jnp.float32)
    frequency = jnp.exp(ladder * (-2.0 / vectors.shape[-1]) * jnp.log(10000.0))
    angles = positions[..., None] * frequency
    cosine = jnp.cos(angles)
    sine = jnp.sin(angles)
    first_half = vectors[..., :half_size]
    second_half = vectors[..., half_size:]
    return jnp.concatenate(
        [first_half * cosine - second_half * sine, second_half * cosine + first_half * sine],
        axis=-1,
    )


def attend(rot_query, cache_keys, cache_values, new_keys, new_values, lengths):
    count, steps, heads, size = rot_query.shape
    score_scale = 1.0 / jnp.sqrt(jnp.float32(DH))
    flat = rot_query.reshape(count, steps * heads, size)
    cache_scores = (
        jnp.einsum("bhd,bsd->bhs", flat, cache_keys, preferred_element_type=jnp.float32)
        * score_scale
    )
    valid = jnp.arange(cache_keys.shape[1])[None, None, :] < lengths[:, None, None]
    masked = jnp.where(valid, cache_scores, -1e30)
    fresh = (
        jnp.einsum("bhd,bjd->bhj", flat, new_keys, preferred_element_type=jnp.float32)
        * score_scale
    )
    row_step = jnp.arange(steps * heads) // heads
    seen = (jnp.arange(steps)[None, :] <= row_step[:, None])[None]
    fresh = jnp.where(seen, fresh, -1e30)
    highest = jnp.maximum(jnp.max(masked, axis=-1), jnp.max(fresh, axis=-1))[..., None]
    cache_weights = jnp.where(valid, jnp.exp(masked - highest), 0.0)
    fresh_weights = jnp.where(seen, jnp.exp(fresh - highest), 0.0)
    total = jnp.sum(cache_weights, axis=-1, keepdims=True) + jnp.sum(
        fresh_weights, axis=-1, keepdims=True
    )
    cache_probs = (cache_weights / total).astype(jnp.bfloat16)
    fresh_probs = (fresh_weights / total).astype(jnp.bfloat16)
    context = jnp.einsum(
        "bhs,bsd->bhd", cache_probs, cache_values, preferred_element_type=jnp.float32
    )
    context = context + jnp.einsum(
        "bhj,bjd->bhd", fresh_probs, new_values, preferred_element_type=jnp.float32
    )
    return context.astype(jnp.bfloat16).reshape(count, steps, heads, size)


def local_plain(tokens, norm_gain, w_query, w_keyval, w_out, cache_keys, cache_values, lengths):
    wide_count = lax.axis_size("wide")
    narrow_count = lax.axis_size("narrow")
    steps, batch, width = tokens.shape
    count = lengths.shape[0]
    rows_all = steps * batch
    width_total = width * wide_count * narrow_count
    rows_float = tokens.reshape(rows_all, width).astype(jnp.float32)
    row_sum, row_squares = lax.psum(
        (jnp.sum(rows_float, axis=1), jnp.sum(rows_float * rows_float, axis=1)),
        ("wide", "narrow"),
    )
    average = (row_sum / width_total)[:, None]
    spread = (row_squares / width_total)[:, None] - average * average
    normed = (
        (rows_float - average) * lax.rsqrt(spread + epsilon) * norm_gain.astype(jnp.float32)
    ).astype(jnp.bfloat16)
    query_part = jnp.dot(
        lax.all_gather(normed, "wide", axis=1, tiled=True),
        w_query,
        preferred_element_type=jnp.float32,
    ).reshape(steps, narrow_count, batch // narrow_count, w_query.shape[1])
    keyval_part = jnp.dot(normed, w_keyval, preferred_element_type=jnp.float32)
    keyval_part = keyval_part.reshape(steps, batch, w_keyval.shape[1])
    query_half = lax.psum_scatter(query_part, "narrow", scatter_dimension=1, tiled=False)
    query_local = lax.all_to_all(
        query_half.astype(jnp.bfloat16), "wide", split_axis=1, concat_axis=2, tiled=True
    )
    keyval_local = lax.psum_scatter(
        keyval_part, ("narrow", "wide"), scatter_dimension=1, tiled=True
    )
    positions = (lengths[:, None] + jnp.arange(steps)).astype(jnp.float32)
    query_local = query_local.astype(jnp.float32).reshape(steps, count, H, DH).transpose(1, 0, 2, 3)
    keyval_local = keyval_local.transpose(1, 0, 2)
    rot_query = rotate(query_local, positions[..., None]).astype(jnp.bfloat16)
    new_keys = rotate(keyval_local[..., :DH], positions).astype(jnp.bfloat16)
    new_values = keyval_local[..., DH:].astype(jnp.bfloat16)
    context = attend(rot_query, cache_keys, cache_values, new_keys, new_values, lengths)
    context = context.reshape(count * steps, H * DH)
    joined = jnp.dot(
        lax.all_gather(context, ("narrow", "wide"), axis=0, tiled=True),
        w_out,
        preferred_element_type=jnp.float32,
    ).astype(jnp.bfloat16)
    return joined.reshape(batch, steps, w_out.shape[1]).transpose(1, 0, 2)


MIB = 1 << 20
EXTRA = 16
OUT_PIECES = 8
IN_VMEM = pl.BlockSpec(memory_space=pltpu.VMEM)
IN_SMEM = pl.BlockSpec(memory_space=pltpu.SMEM)
IN_HBM = pl.BlockSpec(memory_space=pltpu.HBM)


def call(kernel, name, out_shape, args, in_specs=None, scratch=(), limit=12 * MIB, flops=0, moved=None, aliases=None):
    if moved is None:
        moved = sum(a.size * a.dtype.itemsize for a in args)
    return pl.pallas_call(
        kernel,
        out_shape=out_shape,
        in_specs=in_specs or [IN_VMEM] * len(args),
        out_specs=jax.tree.map(lambda _: IN_VMEM, out_shape),
        scratch_shapes=list(scratch),
        compiler_params=pltpu.CompilerParams(vmem_limit_bytes=limit),
        input_output_aliases=aliases or {},
        cost_estimate=pl.CostEstimate(flops=flops, bytes_accessed=moved, transcendentals=0),
        name=name,
    )(*args)


def in_hbm(array):
    return pltpu.with_memory_space_constraint(array, pltpu.HBM)


def load_kernel(moves, *refs):
    target, sems = refs[-2], refs[-1]
    copies = [
        pltpu.make_async_copy(refs[source].at[box], target.at[to], sems.at[at])
        for at, (source, box, to) in enumerate(moves)
    ]
    for copy in copies:
        copy.start()
    for copy in copies:
        copy.wait()


def load(name, shape, moves, *sources, after=()):
    return call(
        functools.partial(load_kernel, moves),
        name,
        pltpu.VMEM(shape, sources[0].dtype),
        [in_hbm(source) for source in sources] + list(after),
        in_specs=[IN_HBM] * len(sources) + [pl.BlockSpec(memory_space=pl.ANY)] * len(after),
        scratch=[pltpu.SemaphoreType.DMA((len(moves),))],
        limit=MIB,
        moved=2 * shape[0] * shape[1],
    )


def boxes(rows, columns, pieces, at_row=0, source=0):
    step = rows.size // pieces
    return [
        (
            source,
            (pl.ds(rows.start + at * step, step), columns),
            (pl.ds(at_row + at * step, step), pl.ds(0, columns.size)),
        )
        for at in range(pieces)
    ]


def sums_kernel(tokens, out):
    rows = tokens.shape[0]
    lanes = out.shape[1]
    values = tokens[...].astype(jnp.float32)
    at_lane = lax.broadcasted_iota(jnp.int32, (rows, lanes), 1)
    at_row = lax.broadcasted_iota(jnp.int32, (rows, lanes), 0)
    out[...] = jnp.zeros_like(out)
    for row, column in enumerate(
        (
            jnp.sum(values, axis=1, keepdims=True),
            jnp.sum(values * values, axis=1, keepdims=True),
        )
    ):
        out[row : row + 1, :] = jnp.sum(
            jnp.where(at_lane == at_row, column, 0.0), axis=0, keepdims=True
        )


def payload_kernel(tokens, gain, mine, theirs, out, extra):
    rows, width = tokens.shape
    lanes = out.shape[1]
    parts = width // lanes
    extra[...] = jnp.zeros_like(extra)
    for at in range(parts):
        span = slice(at * lanes, (at + 1) * lanes)
        extra[at : at + 1, :] = gain[:, span].astype(jnp.float32)
        out[at * rows : (at + 1) * rows, :] = tokens[:, span]
    for at in range(2):
        left = mine[at : at + 1, :] + theirs[at : at + 1, :]
        for piece in range(3):
            row = parts + 3 * at + piece
            part = left.astype(jnp.bfloat16).astype(jnp.float32)
            extra[row : row + 1, :] = part
            left = left - part
    out[parts * rows :, :] = extra[...].astype(jnp.bfloat16)


class Stream:
    def __init__(self, copies, flight=5):
        self.copies, self.started, self.done = copies, 0, 0
        self.start(flight)

    def start(self, count):
        for copy in self.copies[self.started : self.started + count]:
            copy.start()
        self.started = min(self.started + count, len(self.copies))

    def take(self, at):
        while self.done <= at:
            self.copies[self.done].wait()
            self.done += 1
            self.start(1)


def project_kernel(steps, width_total, place, w_keyval_far, w_query, early, *refs):
    *blocks, keep, send, result, normed, late, w_keyval, sems = refs
    wide_at, narrow_at = place[0], place[1]
    rows = result.shape[0]
    width, part = w_keyval.shape[0], early.shape[1]
    columns = w_query.shape[1]
    lanes = blocks[0].shape[1]
    parts = width // lanes
    spots = [
        pl.ds(pl.multiple_of(jnp.bitwise_xor(wide_at, k) * width, width), width)
        for k in range(len(blocks))
    ]
    stream = Stream(
        [pltpu.make_async_copy(w_keyval_far, w_keyval, sems.at[len(blocks)])]
        + [
            pltpu.make_async_copy(
                w_query.at[spot, pl.ds(part, columns - part)], late.at[spot], sems.at[k]
            )
            for k, spot in enumerate(spots)
        ]
    )
    tail = pl.ds(parts * rows, blocks[0].shape[0] - parts * rows)
    sums = blocks[0][tail, :].astype(jnp.float32)
    for block in blocks[1:]:
        sums = sums + block[tail, :].astype(jnp.float32)
    totals = [
        sums[at : at + 1] + sums[at + 1 : at + 2] + sums[at + 2 : at + 3]
        for at in (parts, parts + 3)
    ]
    average = totals[0] / width_total
    spread = totals[1] / width_total - average * average
    scale = lax.rsqrt(spread + epsilon)
    at_lane = lax.broadcasted_iota(jnp.int32, (rows, lanes), 1)
    at_row = lax.broadcasted_iota(jnp.int32, (rows, lanes), 0)

    def stand(flat):
        return jnp.sum(jnp.where(at_lane == at_row, flat, 0.0), axis=1, keepdims=True)

    average, scale = stand(average), stand(scale)
    for weights, span in ((early, slice(0, part)), (late, slice(part, columns))):
        for k, block in enumerate(blocks):
            if weights is early:
                gains = block[tail, :].astype(jnp.float32)
                for at in range(parts):
                    values = block[at * rows : (at + 1) * rows, :].astype(jnp.float32)
                    normed[k, :, at * lanes : (at + 1) * lanes] = (
                        (values - average) * scale * gains[at : at + 1]
                    ).astype(jnp.bfloat16)
            else:
                stream.take(k + 1)
            product = jnp.dot(normed[k], weights[spots[k], :], preferred_element_type=jnp.float32)
            if k == 0:
                result[:, span] = product
            else:
                result[:, span] += product
            if weights is early and k in (2, 4, 6):
                stream.take(k // 2 - 1)
    result[:, columns:] = jnp.dot(normed[0], w_keyval[...], preferred_element_type=jnp.float32)
    half = rows // steps // 2
    for step in range(steps):
        for out, core in ((keep, narrow_at), (send, 1 - narrow_at)):
            start = pl.multiple_of(step * 2 * half + core * half, half)
            out[step * half : (step + 1) * half, :] = result[pl.ds(start, half), :]


def combine_kernel(columns, mine, theirs, out, held):
    wide, steps, _ = out.shape
    lanes = held.shape[2]
    extent = mine.shape[1]
    for at in range(0, extent, lanes):
        total = mine[:, at : at + lanes] + theirs[:, at : at + lanes]
        if at < columns:
            held[at // lanes] = total
        else:
            high = total.astype(jnp.bfloat16).astype(jnp.float32)
            held[at // lanes] = high
            held[(at + extent - columns) // lanes] = total - high
    for at in range(held.shape[0]):
        for to in range(wide):
            out[to, :, at * lanes : (at + 1) * lanes] = held[
                at, pl.ds(to, steps, stride=wide), :
            ].astype(jnp.bfloat16)


def attend_kernel(
    columns, length, cosine, sine, arrived, cache, out, queries, fresh_rows
):
    slots = cache.shape[0] // 2
    wide, steps, _ = arrived.shape
    size = cache.shape[1]
    half = size // 2
    heads = columns // size
    cos, sin = cosine[...], sine[...]

    def turn(vectors):
        first, second = vectors[:, :half], vectors[:, half:]
        return first * cos - second * sin, second * cos + first * sin

    for source in range(wide):
        for head in range(heads):
            at = (source * heads + head) * steps
            low, high = turn(
                arrived[source, :, head * size : (head + 1) * size].astype(jnp.float32)
            )
            queries[at : at + steps, :half] = low
            queries[at : at + steps, half:] = high
    keyval = jnp.zeros((steps, 2 * size), jnp.float32)
    for source in range(wide):
        high = arrived[source, :, columns : columns + 2 * size].astype(jnp.float32)
        low = arrived[source, :, columns + 2 * size :].astype(jnp.float32)
        keyval = keyval + (high + low)
    fresh_rows[...] = jnp.zeros_like(fresh_rows)
    low, high = turn(keyval[:, :size])
    fresh_rows[0, :steps, :half] = low
    fresh_rows[0, :steps, half:] = high
    fresh_rows[1, :steps, :] = keyval[:, size:]
    query = queries[...].astype(jnp.bfloat16)
    new_keys = fresh_rows[0].astype(jnp.bfloat16)
    new_values = fresh_rows[1].astype(jnp.bfloat16)
    score_scale = 1.0 / size**0.5
    by_row = (((1,), (1,)), ((), ()))
    scores = score_scale * lax.dot_general(
        query, cache[:slots, :], by_row, preferred_element_type=jnp.float32
    )
    fresh = score_scale * lax.dot_general(
        query, new_keys, by_row, preferred_element_type=jnp.float32
    )
    valid = lax.broadcasted_iota(jnp.int32, scores.shape, 1) < length[0]
    row_step = lax.rem(lax.broadcasted_iota(jnp.int32, fresh.shape, 0), steps)
    seen = lax.broadcasted_iota(jnp.int32, fresh.shape, 1) <= row_step
    scores = jnp.where(valid, scores, -1e30)
    fresh = jnp.where(seen, fresh, -1e30)
    highest = jnp.maximum(
        jnp.max(scores, axis=1, keepdims=True), jnp.max(fresh, axis=1, keepdims=True)
    )
    weights = jnp.where(valid, jnp.exp(scores - highest), 0.0)
    fresh_weights = jnp.where(seen, jnp.exp(fresh - highest), 0.0)
    share = 1.0 / (
        jnp.sum(weights, axis=1, keepdims=True) + jnp.sum(fresh_weights, axis=1, keepdims=True)
    )
    context = jnp.dot(
        (weights * share).astype(jnp.bfloat16),
        cache[slots:, :],
        preferred_element_type=jnp.float32,
    ) + jnp.dot(
        (fresh_weights * share).astype(jnp.bfloat16),
        new_values,
        preferred_element_type=jnp.float32,
    )
    queries[...] = context
    for head in range(wide * heads):
        out[:, head * size : (head + 1) * size] = queries[
            head * steps : (head + 1) * steps, :
        ].astype(jnp.bfloat16)


def output_kernel(steps, place, w_out, *refs):
    *blocks, out, joined, result, ordered, late, sems = refs
    parts, blocks = [*blocks[:2], late], blocks[2:]
    wide_at, narrow_at = place[0], place[1]
    batch = len(blocks)
    count = batch // 2
    deep, depth = late.shape[0], joined.shape[1]
    piece = deep // OUT_PIECES
    stream = Stream(
        [
            pltpu.make_async_copy(
                w_out.at[pl.ds(2 * deep + at * piece, piece)],
                late.at[pl.ds(at * piece, piece)],
                sems.at[at],
            )
            for at in range(OUT_PIECES)
        ]
    )
    for at in range(0, 3 * deep, depth):
        for k, block in enumerate(blocks):
            joined[k * steps : (k + 1) * steps, :] = block[:, at : at + depth].astype(jnp.float32)
        rows = joined[...].astype(jnp.bfloat16)
        inside = at % deep
        if at >= 2 * deep:
            stream.take((inside + depth) // piece - 1)
        product = jnp.dot(
            rows,
            parts[at // deep][inside : inside + depth, :],
            preferred_element_type=jnp.float32,
        )
        if at == 0:
            result[...] = product
        else:
            result[...] += product
        if at in (3 * depth, 5 * depth, 7 * depth):
            stream.take(at // depth // 2 - 1)
    for core in range(2):
        for k in range(count):
            sequence = jnp.bitwise_xor(narrow_at, core) * count + jnp.bitwise_xor(wide_at, k)
            for step in range(steps):
                row = core * count * steps + k * steps + step
                ordered[pl.ds(step * batch + sequence, 1), :] = result[row : row + 1, :]
    for step in range(steps):
        out[step] = ordered[step * batch : (step + 1) * batch, :].astype(jnp.bfloat16)


def swap(value, axis, bits):
    size = lax.axis_size(axis)
    return lax.ppermute(value, axis, [(at, at ^ bits) for at in range(size)])


def gather_tokens(block):
    near = {0: block}
    for bits in (4, 2, 1):
        near[bits] = swap(block, "wide", bits)
    near[1], near[2], near[4] = lax.optimization_barrier((near[1], near[2], near[4]))
    near[6] = swap(near[4], "wide", 2)
    near[5] = swap(near[4], "wide", 1)
    near[3] = swap(near[2], "wide", 1)
    near[7] = swap(near[5], "wide", 2)
    return [near[k] for k in range(8)]


def gather_contexts(block, loader):
    near = {0: block}
    for bits in (4, 2, 1):
        near[bits] = swap(block, "wide", bits)
    first = loader(0, block)
    near[1], near[2], near[4], first = lax.optimization_barrier((near[1], near[2], near[4], first))
    near[6] = swap(near[4], "wide", 2)
    near[5] = swap(near[4], "wide", 1)
    near[3] = swap(near[2], "wide", 1)
    near[7] = swap(near[5], "wide", 2)
    second = loader(1, near[4])
    near[3], near[6], near[7], second = lax.optimization_barrier(
        (near[3], near[6], near[7], second)
    )
    return [near[k] for k in range(8)], [first, second]


def local_fast(tokens, norm_gain, w_query, w_keyval, w_out, cache_keys, cache_values, lengths):
    wide_count = lax.axis_size("wide")
    narrow_count = lax.axis_size("narrow")
    steps, batch, width = tokens.shape
    rows = steps * batch
    columns, tail = w_query.shape[1], w_keyval.shape[1]
    size = cache_keys.shape[2]
    f32, bf16 = jnp.float32, jnp.bfloat16
    place = jnp.stack([lax.axis_index("wide"), lax.axis_index("narrow")]).astype(jnp.int32)

    own = tokens.reshape(rows, width)
    sums = call(sums_kernel, "row_sums", jax.ShapeDtypeStruct((8, 128), f32), [own])
    payload = call(
        payload_kernel,
        "payload",
        jax.ShapeDtypeStruct((width // 128 * rows + EXTRA, 128), bf16),
        [own, norm_gain[None], sums, swap(sums, "narrow", 1)],
        scratch=[pltpu.VMEM((EXTRA, 128), f32)],
    )
    blocks = gather_tokens(payload)
    part = columns // 3 * 2
    deep = w_query.shape[0]
    early_weights = load(
        "load_query_weights",
        (deep, part),
        boxes(pl.ds(0, deep), pl.ds(0, part), 8),
        w_query,
    )
    keep, send = call(
        functools.partial(project_kernel, steps, width * wide_count * narrow_count),
        "norm_and_project",
        [jax.ShapeDtypeStruct((rows // 2, columns + tail), f32)] * 2,
        [place, in_hbm(w_keyval), in_hbm(w_query), early_weights, *blocks],
        in_specs=[IN_SMEM, IN_HBM, IN_HBM] + [IN_VMEM] * (wide_count + 1),
        scratch=[
            pltpu.VMEM((rows, columns + tail), f32),
            pltpu.VMEM((wide_count, rows, width), bf16),
            pltpu.VMEM((deep, columns - part), bf16),
            pltpu.VMEM(w_keyval.shape, bf16),
            pltpu.SemaphoreType.DMA((wide_count + 1,)),
        ],
        limit=24 * MIB,
        flops=2 * rows * width * wide_count * columns,
    )
    outgoing = call(
        functools.partial(combine_kernel, columns),
        "sum_of_cores",
        jax.ShapeDtypeStruct((wide_count, steps, columns + 2 * tail), bf16),
        [keep, swap(send, "narrow", 1)],
        scratch=[pltpu.VMEM(((columns + 2 * tail) // 128, rows // 2, 128), f32)],
    )
    arrived = lax.all_to_all(outgoing, "wide", 0, 0, tiled=True)
    slots = cache_keys.shape[1]
    cache = load(
        "load_cache",
        (2 * slots, size),
        boxes(pl.ds(0, slots), pl.ds(0, size), 4)
        + boxes(pl.ds(0, slots), pl.ds(0, size), 4, at_row=slots, source=1),
        cache_keys.reshape(slots, size),
        cache_values.reshape(slots, size),
        after=[outgoing],
    )
    ladder = jnp.arange(size // 2, dtype=f32)
    frequency = jnp.exp(ladder * (-2.0 / size) * jnp.log(10000.0))
    angles = (lengths + jnp.arange(steps)).astype(f32)[:, None] * frequency
    context = call(
        functools.partial(attend_kernel, columns),
        "attention",
        jax.ShapeDtypeStruct((steps, H * size), bf16),
        [lengths, jnp.cos(angles), jnp.sin(angles), arrived, cache],
        in_specs=[IN_SMEM] + [IN_VMEM] * 4,
        scratch=[
            pltpu.VMEM((steps * H, size), f32),
            pltpu.VMEM((2, 128, size), f32),
        ],
        limit=16 * MIB,
        flops=4 * steps * H * size * slots,
    )
    deep = w_out.shape[0] // 3
    contexts, early_weights = gather_contexts(
        context,
        lambda at, block: load(
            "load_out_weights",
            (deep, w_out.shape[1]),
            boxes(pl.ds(at * deep, deep), pl.ds(0, w_out.shape[1]), 8),
            w_out,
            after=[block],
        ),
    )
    contexts = contexts + [swap(block, "narrow", 1) for block in contexts]
    return call(
        functools.partial(output_kernel, steps),
        "project_out",
        jax.ShapeDtypeStruct((steps, batch, w_out.shape[1]), bf16),
        [place, in_hbm(w_out), *early_weights, *contexts],
        in_specs=[IN_SMEM, IN_HBM] + [IN_VMEM] * (2 + batch),
        scratch=[
            pltpu.VMEM((rows, deep // 4), f32),
            pltpu.VMEM((rows, w_out.shape[1]), f32),
            pltpu.VMEM((rows, w_out.shape[1]), f32),
            pltpu.VMEM((deep, w_out.shape[1]), bf16),
            pltpu.SemaphoreType.DMA((OUT_PIECES,)),
        ],
        limit=28 * MIB,
        flops=2 * rows * w_out.size,
    )


def local(tokens, norm_gain, w_query, w_keyval, w_out, cache_keys, cache_values, lengths):
    fits = (
        lengths.shape[0] == 1
        and lax.axis_size("narrow") == 2
        and lax.axis_size("wide") == 8
        and tokens.shape[1] == 16
        and tokens.shape[2] % 128 == 0
        and tokens.shape[2] // 128 + 6 <= EXTRA
        and tokens.shape[0] * 16 <= 128
    )
    return (local_fast if fits else local_plain)(
        tokens, norm_gain, w_query, w_keyval, w_out, cache_keys, cache_values, lengths
    )


def solution(mesh):
    placed = (
        P(None, "groups", ("narrow", "wide")),
        P(("narrow", "wide")),
        P("narrow", "wide"),
        P(("narrow", "wide"), None),
        P(None, ("narrow", "wide")),
        P(("groups", "narrow", "wide"), None, None),
        P(("groups", "narrow", "wide"), None, None),
        P(("groups", "narrow", "wide")),
    )
    return jax.shard_map(
        local,
        mesh=mesh,
        in_specs=placed,
        out_specs=P(None, "groups", ("narrow", "wide")),
        check_vma=False,
    )
```

```python
import functools

import jax
import jax.numpy as jnp
from jax import lax
from jax.experimental import pallas as pl
from jax.experimental.pallas import tpu as pltpu
from jax.sharding import PartitionSpec as P

H = 48
DH = 256


epsilon = 1e-06


def rotate(vectors, positions):
    half_size = vectors.shape[-1] // 2
    ladder = jnp.arange(half_size, dtype=jnp.float32)
    frequency = jnp.exp(ladder * (-2.0 / vectors.shape[-1]) * jnp.log(10000.0))
    angles = positions[..., None] * frequency
    cosine = jnp.cos(angles)
    sine = jnp.sin(angles)
    first_half = vectors[..., :half_size]
    second_half = vectors[..., half_size:]
    return jnp.concatenate(
        [first_half * cosine - second_half * sine, second_half * cosine + first_half * sine],
        axis=-1,
    )


def attend(rot_query, cache_keys, cache_values, new_keys, new_values, lengths):
    count, steps, heads, size = rot_query.shape
    score_scale = 1.0 / jnp.sqrt(jnp.float32(DH))
    flat = rot_query.reshape(count, steps * heads, size)
    cache_scores = (
        jnp.einsum("bhd,bsd->bhs", flat, cache_keys, preferred_element_type=jnp.float32)
        * score_scale
    )
    valid = jnp.arange(cache_keys.shape[1])[None, None, :] < lengths[:, None, None]
    masked = jnp.where(valid, cache_scores, -1e30)
    fresh = (
        jnp.einsum("bhd,bjd->bhj", flat, new_keys, preferred_element_type=jnp.float32)
        * score_scale
    )
    row_step = jnp.arange(steps * heads) // heads
    seen = (jnp.arange(steps)[None, :] <= row_step[:, None])[None]
    fresh = jnp.where(seen, fresh, -1e30)
    highest = jnp.maximum(jnp.max(masked, axis=-1), jnp.max(fresh, axis=-1))[..., None]
    cache_weights = jnp.where(valid, jnp.exp(masked - highest), 0.0)
    fresh_weights = jnp.where(seen, jnp.exp(fresh - highest), 0.0)
    total = jnp.sum(cache_weights, axis=-1, keepdims=True) + jnp.sum(
        fresh_weights, axis=-1, keepdims=True
    )
    cache_probs = (cache_weights / total).astype(jnp.bfloat16)
    fresh_probs = (fresh_weights / total).astype(jnp.bfloat16)
    context = jnp.einsum(
        "bhs,bsd->bhd", cache_probs, cache_values, preferred_element_type=jnp.float32
    )
    context = context + jnp.einsum(
        "bhj,bjd->bhd", fresh_probs, new_values, preferred_element_type=jnp.float32
    )
    return context.astype(jnp.bfloat16).reshape(count, steps, heads, size)


def local_plain(tokens, norm_gain, w_query, w_keyval, w_out, cache_keys, cache_values, lengths):
    wide_count = lax.axis_size("wide")
    narrow_count = lax.axis_size("narrow")
    steps, batch, width = tokens.shape
    count = lengths.shape[0]
    rows_all = steps * batch
    width_total = width * wide_count * narrow_count
    rows_float = tokens.reshape(rows_all, width).astype(jnp.float32)
    row_sum, row_squares = lax.psum(
        (jnp.sum(rows_float, axis=1), jnp.sum(rows_float * rows_float, axis=1)),
        ("wide", "narrow"),
    )
    average = (row_sum / width_total)[:, None]
    spread = (row_squares / width_total)[:, None] - average * average
    normed = (
        (rows_float - average) * lax.rsqrt(spread + epsilon) * norm_gain.astype(jnp.float32)
    ).astype(jnp.bfloat16)
    query_part = jnp.dot(
        lax.all_gather(normed, "wide", axis=1, tiled=True),
        w_query,
        preferred_element_type=jnp.float32,
    ).reshape(steps, narrow_count, batch // narrow_count, w_query.shape[1])
    keyval_part = jnp.dot(normed, w_keyval, preferred_element_type=jnp.float32)
    keyval_part = keyval_part.reshape(steps, batch, w_keyval.shape[1])
    query_half = lax.psum_scatter(query_part, "narrow", scatter_dimension=1, tiled=False)
    query_local = lax.all_to_all(
        query_half.astype(jnp.bfloat16), "wide", split_axis=1, concat_axis=2, tiled=True
    )
    keyval_local = lax.psum_scatter(
        keyval_part, ("narrow", "wide"), scatter_dimension=1, tiled=True
    )
    positions = (lengths[:, None] + jnp.arange(steps)).astype(jnp.float32)
    query_local = query_local.astype(jnp.float32).reshape(steps, count, H, DH).transpose(1, 0, 2, 3)
    keyval_local = keyval_local.transpose(1, 0, 2)
    rot_query = rotate(query_local, positions[..., None]).astype(jnp.bfloat16)
    new_keys = rotate(keyval_local[..., :DH], positions).astype(jnp.bfloat16)
    new_values = keyval_local[..., DH:].astype(jnp.bfloat16)
    context = attend(rot_query, cache_keys, cache_values, new_keys, new_values, lengths)
    context = context.reshape(count * steps, H * DH)
    joined = jnp.dot(
        lax.all_gather(context, ("narrow", "wide"), axis=0, tiled=True),
        w_out,
        preferred_element_type=jnp.float32,
    ).astype(jnp.bfloat16)
    return joined.reshape(batch, steps, w_out.shape[1]).transpose(1, 0, 2)


MIB = 1 << 20
EXTRA = 16
OUT_PIECES = 8
IN_VMEM = pl.BlockSpec(memory_space=pltpu.VMEM)
IN_SMEM = pl.BlockSpec(memory_space=pltpu.SMEM)
IN_HBM = pl.BlockSpec(memory_space=pltpu.HBM)


def call(kernel, name, out_shape, args, in_specs=None, scratch=(), limit=12 * MIB, flops=0, moved=None, aliases=None):
    if moved is None:
        moved = sum(a.size * a.dtype.itemsize for a in args)
    return pl.pallas_call(
        kernel,
        out_shape=out_shape,
        in_specs=in_specs or [IN_VMEM] * len(args),
        out_specs=jax.tree.map(lambda _: IN_VMEM, out_shape),
        scratch_shapes=list(scratch),
        compiler_params=pltpu.CompilerParams(vmem_limit_bytes=limit),
        input_output_aliases=aliases or {},
        cost_estimate=pl.CostEstimate(flops=flops, bytes_accessed=moved, transcendentals=0),
        name=name,
    )(*args)


def in_hbm(array):
    return pltpu.with_memory_space_constraint(array, pltpu.HBM)


def load_kernel(moves, *refs):
    target, sems = refs[-2], refs[-1]
    copies = [
        pltpu.make_async_copy(refs[source].at[box], target.at[to], sems.at[at])
        for at, (source, box, to) in enumerate(moves)
    ]
    for copy in copies:
        copy.start()
    for copy in copies:
        copy.wait()


def load(name, shape, moves, *sources, after=()):
    return call(
        functools.partial(load_kernel, moves),
        name,
        pltpu.VMEM(shape, sources[0].dtype),
        [in_hbm(source) for source in sources] + list(after),
        in_specs=[IN_HBM] * len(sources) + [pl.BlockSpec(memory_space=pl.ANY)] * len(after),
        scratch=[pltpu.SemaphoreType.DMA((len(moves),))],
        limit=MIB,
        moved=2 * shape[0] * shape[1],
    )


def boxes(rows, columns, pieces, at_row=0, source=0):
    step = rows.size // pieces
    return [
        (
            source,
            (pl.ds(rows.start + at * step, step), columns),
            (pl.ds(at_row + at * step, step), pl.ds(0, columns.size)),
        )
        for at in range(pieces)
    ]


def sums_kernel(tokens, out):
    rows = tokens.shape[0]
    lanes = out.shape[1]
    values = tokens[...].astype(jnp.float32)
    at_lane = lax.broadcasted_iota(jnp.int32, (rows, lanes), 1)
    at_row = lax.broadcasted_iota(jnp.int32, (rows, lanes), 0)
    out[...] = jnp.zeros_like(out)
    for row, column in enumerate(
        (
            jnp.sum(values, axis=1, keepdims=True),
            jnp.sum(values * values, axis=1, keepdims=True),
        )
    ):
        out[row : row + 1, :] = jnp.sum(
            jnp.where(at_lane == at_row, column, 0.0), axis=0, keepdims=True
        )


def payload_kernel(tokens, gain, mine, theirs, out, extra):
    rows, width = tokens.shape
    lanes = out.shape[1]
    parts = width // lanes
    extra[...] = jnp.zeros_like(extra)
    for at in range(parts):
        span = slice(at * lanes, (at + 1) * lanes)
        extra[at : at + 1, :] = gain[:, span].astype(jnp.float32)
        out[at * rows : (at + 1) * rows, :] = tokens[:, span]
    for at in range(2):
        left = mine[at : at + 1, :] + theirs[at : at + 1, :]
        for piece in range(3):
            row = parts + 3 * at + piece
            part = left.astype(jnp.bfloat16).astype(jnp.float32)
            extra[row : row + 1, :] = part
            left = left - part
    out[parts * rows :, :] = extra[...].astype(jnp.bfloat16)


class Stream:
    def __init__(self, copies, flight=5):
        self.copies, self.started, self.done = copies, 0, 0
        self.start(flight)

    def start(self, count):
        for copy in self.copies[self.started : self.started + count]:
            copy.start()
        self.started = min(self.started + count, len(self.copies))

    def take(self, at):
        while self.done <= at:
            self.copies[self.done].wait()
            self.done += 1
            self.start(1)


def project_kernel(steps, width_total, place, w_keyval_far, w_query, early, *refs):
    *blocks, keep, send, result, normed, late, w_keyval, sems = refs
    wide_at, narrow_at = place[0], place[1]
    rows = result.shape[0]
    width, part = w_keyval.shape[0], early.shape[1]
    columns = w_query.shape[1]
    lanes = blocks[0].shape[1]
    parts = width // lanes
    spots = [
        pl.ds(pl.multiple_of(jnp.bitwise_xor(wide_at, k) * width, width), width)
        for k in range(len(blocks))
    ]
    stream = Stream(
        [pltpu.make_async_copy(w_keyval_far, w_keyval, sems.at[len(blocks)])]
        + [
            pltpu.make_async_copy(
                w_query.at[spot, pl.ds(part, columns - part)], late.at[spot], sems.at[k]
            )
            for k, spot in enumerate(spots)
        ]
    )
    tail = pl.ds(parts * rows, blocks[0].shape[0] - parts * rows)
    sums = blocks[0][tail, :].astype(jnp.float32)
    for block in blocks[1:]:
        sums = sums + block[tail, :].astype(jnp.float32)
    totals = [
        sums[at : at + 1] + sums[at + 1 : at + 2] + sums[at + 2 : at + 3]
        for at in (parts, parts + 3)
    ]
    average = totals[0] / width_total
    spread = totals[1] / width_total - average * average
    scale = lax.rsqrt(spread + epsilon)
    at_lane = lax.broadcasted_iota(jnp.int32, (rows, lanes), 1)
    at_row = lax.broadcasted_iota(jnp.int32, (rows, lanes), 0)

    def stand(flat):
        return jnp.sum(jnp.where(at_lane == at_row, flat, 0.0), axis=1, keepdims=True)

    average, scale = stand(average), stand(scale)
    for weights, span in ((early, slice(0, part)), (late, slice(part, columns))):
        for k, block in enumerate(blocks):
            if weights is early:
                gains = block[tail, :].astype(jnp.float32)
                for at in range(parts):
                    values = block[at * rows : (at + 1) * rows, :].astype(jnp.float32)
                    normed[k, :, at * lanes : (at + 1) * lanes] = (
                        (values - average) * scale * gains[at : at + 1]
                    ).astype(jnp.bfloat16)
            else:
                stream.take(k + 1)
            product = jnp.dot(normed[k], weights[spots[k], :], preferred_element_type=jnp.float32)
            if k == 0:
                result[:, span] = product
            else:
                result[:, span] += product
            if weights is early and k in (2, 4, 6):
                stream.take(k // 2 - 1)
    result[:, columns:] = jnp.dot(normed[0], w_keyval[...], preferred_element_type=jnp.float32)
    half = rows // steps // 2
    for step in range(steps):
        for out, core in ((keep, narrow_at), (send, 1 - narrow_at)):
            start = pl.multiple_of(step * 2 * half + core * half, half)
            out[step * half : (step + 1) * half, :] = result[pl.ds(start, half), :]


def combine_kernel(columns, mine, theirs, out, held):
    wide, steps, _ = out.shape
    lanes = held.shape[2]
    extent = mine.shape[1]
    for at in range(0, extent, lanes):
        total = mine[:, at : at + lanes] + theirs[:, at : at + lanes]
        if at < columns:
            held[at // lanes] = total
        else:
            high = total.astype(jnp.bfloat16).astype(jnp.float32)
            held[at // lanes] = high
            held[(at + extent - columns) // lanes] = total - high
    for at in range(held.shape[0]):
        for to in range(wide):
            out[to, :, at * lanes : (at + 1) * lanes] = held[
                at, pl.ds(to, steps, stride=wide), :
            ].astype(jnp.bfloat16)


def attend_kernel(
    columns, length, cosine, sine, arrived, cache, out, queries, fresh_rows
):
    slots = cache.shape[0] // 2
    wide, steps, _ = arrived.shape
    size = cache.shape[1]
    half = size // 2
    heads = columns // size
    cos, sin = cosine[...], sine[...]

    def turn(vectors):
        first, second = vectors[:, :half], vectors[:, half:]
        return first * cos - second * sin, second * cos + first * sin

    for source in range(wide):
        for head in range(heads):
            at = (source * heads + head) * steps
            low, high = turn(
                arrived[source, :, head * size : (head + 1) * size].astype(jnp.float32)
            )
            queries[at : at + steps, :half] = low
            queries[at : at + steps, half:] = high
    keyval = jnp.zeros((steps, 2 * size), jnp.float32)
    for source in range(wide):
        high = arrived[source, :, columns : columns + 2 * size].astype(jnp.float32)
        low = arrived[source, :, columns + 2 * size :].astype(jnp.float32)
        keyval = keyval + (high + low)
    fresh_rows[...] = jnp.zeros_like(fresh_rows)
    low, high = turn(keyval[:, :size])
    fresh_rows[0, :steps, :half] = low
    fresh_rows[0, :steps, half:] = high
    fresh_rows[1, :steps, :] = keyval[:, size:]
    query = queries[...].astype(jnp.bfloat16)
    new_keys = fresh_rows[0].astype(jnp.bfloat16)
    new_values = fresh_rows[1].astype(jnp.bfloat16)
    score_scale = 1.0 / size**0.5
    by_row = (((1,), (1,)), ((), ()))
    scores = score_scale * lax.dot_general(
        query, cache[:slots, :], by_row, preferred_element_type=jnp.float32
    )
    fresh = score_scale * lax.dot_general(
        query, new_keys, by_row, preferred_element_type=jnp.float32
    )
    valid = lax.broadcasted_iota(jnp.int32, scores.shape, 1) < length[0]
    row_step = lax.rem(lax.broadcasted_iota(jnp.int32, fresh.shape, 0), steps)
    seen = lax.broadcasted_iota(jnp.int32, fresh.shape, 1) <= row_step
    scores = jnp.where(valid, scores, -1e30)
    fresh = jnp.where(seen, fresh, -1e30)
    highest = jnp.maximum(
        jnp.max(scores, axis=1, keepdims=True), jnp.max(fresh, axis=1, keepdims=True)
    )
    weights = jnp.where(valid, jnp.exp(scores - highest), 0.0)
    fresh_weights = jnp.where(seen, jnp.exp(fresh - highest), 0.0)
    share = 1.0 / (
        jnp.sum(weights, axis=1, keepdims=True) + jnp.sum(fresh_weights, axis=1, keepdims=True)
    )
    context = jnp.dot(
        (weights * share).astype(jnp.bfloat16),
        cache[slots:, :],
        preferred_element_type=jnp.float32,
    ) + jnp.dot(
        (fresh_weights * share).astype(jnp.bfloat16),
        new_values,
        preferred_element_type=jnp.float32,
    )
    queries[...] = context
    for head in range(wide * heads):
        out[:, head * size : (head + 1) * size] = queries[
            head * steps : (head + 1) * steps, :
        ].astype(jnp.bfloat16)


def output_kernel(steps, place, w_out, *refs):
    *blocks, out, joined, result, ordered, late, sems = refs
    parts, blocks = [*blocks[:2], late], blocks[2:]
    wide_at, narrow_at = place[0], place[1]
    batch = len(blocks)
    count = batch // 2
    deep, depth = late.shape[0], joined.shape[1]
    piece = deep // OUT_PIECES
    stream = Stream(
        [
            pltpu.make_async_copy(
                w_out.at[pl.ds(2 * deep + at * piece, piece)],
                late.at[pl.ds(at * piece, piece)],
                sems.at[at],
            )
            for at in range(OUT_PIECES)
        ]
    )
    for at in range(0, 3 * deep, depth):
        for k, block in enumerate(blocks):
            joined[k * steps : (k + 1) * steps, :] = block[:, at : at + depth].astype(jnp.float32)
        rows = joined[...].astype(jnp.bfloat16)
        inside = at % deep
        if at >= 2 * deep:
            stream.take((inside + depth) // piece - 1)
        product = jnp.dot(
            rows,
            parts[at // deep][inside : inside + depth, :],
            preferred_element_type=jnp.float32,
        )
        if at == 0:
            result[...] = product
        else:
            result[...] += product
        if at in (3 * depth, 5 * depth, 7 * depth):
            stream.take(at // depth // 2 - 1)
    for core in range(2):
        for k in range(count):
            sequence = jnp.bitwise_xor(narrow_at, core) * count + jnp.bitwise_xor(wide_at, k)
            for step in range(steps):
                row = core * count * steps + k * steps + step
                ordered[pl.ds(step * batch + sequence, 1), :] = result[row : row + 1, :]
    for step in range(steps):
        out[step] = ordered[step * batch : (step + 1) * batch, :].astype(jnp.bfloat16)


def swap(value, axis, bits):
    size = lax.axis_size(axis)
    return lax.ppermute(value, axis, [(at, at ^ bits) for at in range(size)])


def gather_tokens(block):
    near = {0: block}
    for bits in (4, 2, 1):
        near[bits] = swap(block, "wide", bits)
    near[4], near[2], near[1] = lax.optimization_barrier((near[4], near[2], near[1]))
    near[6] = swap(near[4], "wide", 2)
    near[5] = swap(near[4], "wide", 1)
    near[5], near[2] = lax.optimization_barrier((near[5], near[2]))
    near[7] = swap(near[5], "wide", 2)
    near[3] = swap(near[2], "wide", 1)
    return [near[k] for k in range(8)]


def gather_contexts(block, loader):
    near = {0: block}
    for bits in (4, 2, 1):
        near[bits] = swap(block, "wide", bits)
    first = loader(0, block)
    near[1], near[2], near[4], first = lax.optimization_barrier((near[1], near[2], near[4], first))
    near[6] = swap(near[4], "wide", 2)
    near[5] = swap(near[4], "wide", 1)
    near[3] = swap(near[2], "wide", 1)
    near[7] = swap(near[5], "wide", 2)
    second = loader(1, near[4])
    near[3], near[6], near[7], second = lax.optimization_barrier(
        (near[3], near[6], near[7], second)
    )
    return [near[k] for k in range(8)], [first, second]


def local_fast(tokens, norm_gain, w_query, w_keyval, w_out, cache_keys, cache_values, lengths):
    wide_count = lax.axis_size("wide")
    narrow_count = lax.axis_size("narrow")
    steps, batch, width = tokens.shape
    rows = steps * batch
    columns, tail = w_query.shape[1], w_keyval.shape[1]
    size = cache_keys.shape[2]
    f32, bf16 = jnp.float32, jnp.bfloat16
    place = jnp.stack([lax.axis_index("wide"), lax.axis_index("narrow")]).astype(jnp.int32)

    own = tokens.reshape(rows, width)
    sums = call(sums_kernel, "row_sums", jax.ShapeDtypeStruct((8, 128), f32), [own])
    payload = call(
        payload_kernel,
        "payload",
        jax.ShapeDtypeStruct((width // 128 * rows + EXTRA, 128), bf16),
        [own, norm_gain[None], sums, swap(sums, "narrow", 1)],
        scratch=[pltpu.VMEM((EXTRA, 128), f32)],
    )
    blocks = gather_tokens(payload)
    part = columns // 3 * 2
    deep = w_query.shape[0]
    early_weights = load(
        "load_query_weights",
        (deep, part),
        boxes(pl.ds(0, deep), pl.ds(0, part), 8),
        w_query,
    )
    keep, send = call(
        functools.partial(project_kernel, steps, width * wide_count * narrow_count),
        "norm_and_project",
        [jax.ShapeDtypeStruct((rows // 2, columns + tail), f32)] * 2,
        [place, in_hbm(w_keyval), in_hbm(w_query), early_weights, *blocks],
        in_specs=[IN_SMEM, IN_HBM, IN_HBM] + [IN_VMEM] * (wide_count + 1),
        scratch=[
            pltpu.VMEM((rows, columns + tail), f32),
            pltpu.VMEM((wide_count, rows, width), bf16),
            pltpu.VMEM((deep, columns - part), bf16),
            pltpu.VMEM(w_keyval.shape, bf16),
            pltpu.SemaphoreType.DMA((wide_count + 1,)),
        ],
        limit=24 * MIB,
        flops=2 * rows * width * wide_count * columns,
    )
    outgoing = call(
        functools.partial(combine_kernel, columns),
        "sum_of_cores",
        jax.ShapeDtypeStruct((wide_count, steps, columns + 2 * tail), bf16),
        [keep, swap(send, "narrow", 1)],
        scratch=[pltpu.VMEM(((columns + 2 * tail) // 128, rows // 2, 128), f32)],
    )
    arrived = lax.all_to_all(outgoing, "wide", 0, 0, tiled=True)
    slots = cache_keys.shape[1]
    cache = load(
        "load_cache",
        (2 * slots, size),
        boxes(pl.ds(0, slots), pl.ds(0, size), 4)
        + boxes(pl.ds(0, slots), pl.ds(0, size), 4, at_row=slots, source=1),
        cache_keys.reshape(slots, size),
        cache_values.reshape(slots, size),
        after=[outgoing],
    )
    ladder = jnp.arange(size // 2, dtype=f32)
    frequency = jnp.exp(ladder * (-2.0 / size) * jnp.log(10000.0))
    angles = (lengths + jnp.arange(steps)).astype(f32)[:, None] * frequency
    context = call(
        functools.partial(attend_kernel, columns),
        "attention",
        jax.ShapeDtypeStruct((steps, H * size), bf16),
        [lengths, jnp.cos(angles), jnp.sin(angles), arrived, cache],
        in_specs=[IN_SMEM] + [IN_VMEM] * 4,
        scratch=[
            pltpu.VMEM((steps * H, size), f32),
            pltpu.VMEM((2, 128, size), f32),
        ],
        limit=16 * MIB,
        flops=4 * steps * H * size * slots,
    )
    deep = w_out.shape[0] // 3
    contexts, early_weights = gather_contexts(
        context,
        lambda at, block: load(
            "load_out_weights",
            (deep, w_out.shape[1]),
            boxes(pl.ds(at * deep, deep), pl.ds(0, w_out.shape[1]), 8),
            w_out,
            after=[block],
        ),
    )
    contexts = contexts + [swap(block, "narrow", 1) for block in contexts]
    return call(
        functools.partial(output_kernel, steps),
        "project_out",
        jax.ShapeDtypeStruct((steps, batch, w_out.shape[1]), bf16),
        [place, in_hbm(w_out), *early_weights, *contexts],
        in_specs=[IN_SMEM, IN_HBM] + [IN_VMEM] * (2 + batch),
        scratch=[
            pltpu.VMEM((rows, deep // 4), f32),
            pltpu.VMEM((rows, w_out.shape[1]), f32),
            pltpu.VMEM((rows, w_out.shape[1]), f32),
            pltpu.VMEM((deep, w_out.shape[1]), bf16),
            pltpu.SemaphoreType.DMA((OUT_PIECES,)),
        ],
        limit=28 * MIB,
        flops=2 * rows * w_out.size,
    )


def local(tokens, norm_gain, w_query, w_keyval, w_out, cache_keys, cache_values, lengths):
    fits = (
        lengths.shape[0] == 1
        and lax.axis_size("narrow") == 2
        and lax.axis_size("wide") == 8
        and tokens.shape[1] == 16
        and tokens.shape[2] % 128 == 0
        and tokens.shape[2] // 128 + 6 <= EXTRA
        and tokens.shape[0] * 16 <= 128
    )
    return (local_fast if fits else local_plain)(
        tokens, norm_gain, w_query, w_keyval, w_out, cache_keys, cache_values, lengths
    )


def solution(mesh):
    placed = (
        P(None, "groups", ("narrow", "wide")),
        P(("narrow", "wide")),
        P("narrow", "wide"),
        P(("narrow", "wide"), None),
        P(None, ("narrow", "wide")),
        P(("groups", "narrow", "wide"), None, None),
        P(("groups", "narrow", "wide"), None, None),
        P(("groups", "narrow", "wide")),
    )
    return jax.shard_map(
        local,
        mesh=mesh,
        in_specs=placed,
        out_specs=P(None, "groups", ("narrow", "wide")),
        check_vma=False,
    )
```

```python
import functools

import jax
import jax.numpy as jnp
from jax import lax
from jax.experimental import pallas as pl
from jax.experimental.pallas import tpu as pltpu
from jax.sharding import PartitionSpec as P

H = 48
DH = 256


epsilon = 1e-06


def rotate(vectors, positions):
    half_size = vectors.shape[-1] // 2
    ladder = jnp.arange(half_size, dtype=jnp.float32)
    frequency = jnp.exp(ladder * (-2.0 / vectors.shape[-1]) * jnp.log(10000.0))
    angles = positions[..., None] * frequency
    cosine = jnp.cos(angles)
    sine = jnp.sin(angles)
    first_half = vectors[..., :half_size]
    second_half = vectors[..., half_size:]
    return jnp.concatenate(
        [first_half * cosine - second_half * sine, second_half * cosine + first_half * sine],
        axis=-1,
    )


def attend(rot_query, cache_keys, cache_values, new_keys, new_values, lengths):
    count, steps, heads, size = rot_query.shape
    score_scale = 1.0 / jnp.sqrt(jnp.float32(DH))
    flat = rot_query.reshape(count, steps * heads, size)
    cache_scores = (
        jnp.einsum("bhd,bsd->bhs", flat, cache_keys, preferred_element_type=jnp.float32)
        * score_scale
    )
    valid = jnp.arange(cache_keys.shape[1])[None, None, :] < lengths[:, None, None]
    masked = jnp.where(valid, cache_scores, -1e30)
    fresh = (
        jnp.einsum("bhd,bjd->bhj", flat, new_keys, preferred_element_type=jnp.float32)
        * score_scale
    )
    row_step = jnp.arange(steps * heads) // heads
    seen = (jnp.arange(steps)[None, :] <= row_step[:, None])[None]
    fresh = jnp.where(seen, fresh, -1e30)
    highest = jnp.maximum(jnp.max(masked, axis=-1), jnp.max(fresh, axis=-1))[..., None]
    cache_weights = jnp.where(valid, jnp.exp(masked - highest), 0.0)
    fresh_weights = jnp.where(seen, jnp.exp(fresh - highest), 0.0)
    total = jnp.sum(cache_weights, axis=-1, keepdims=True) + jnp.sum(
        fresh_weights, axis=-1, keepdims=True
    )
    cache_probs = (cache_weights / total).astype(jnp.bfloat16)
    fresh_probs = (fresh_weights / total).astype(jnp.bfloat16)
    context = jnp.einsum(
        "bhs,bsd->bhd", cache_probs, cache_values, preferred_element_type=jnp.float32
    )
    context = context + jnp.einsum(
        "bhj,bjd->bhd", fresh_probs, new_values, preferred_element_type=jnp.float32
    )
    return context.astype(jnp.bfloat16).reshape(count, steps, heads, size)


def local_plain(tokens, norm_gain, w_query, w_keyval, w_out, cache_keys, cache_values, lengths):
    wide_count = lax.axis_size("wide")
    narrow_count = lax.axis_size("narrow")
    steps, batch, width = tokens.shape
    count = lengths.shape[0]
    rows_all = steps * batch
    width_total = width * wide_count * narrow_count
    rows_float = tokens.reshape(rows_all, width).astype(jnp.float32)
    row_sum, row_squares = lax.psum(
        (jnp.sum(rows_float, axis=1), jnp.sum(rows_float * rows_float, axis=1)),
        ("wide", "narrow"),
    )
    average = (row_sum / width_total)[:, None]
    spread = (row_squares / width_total)[:, None] - average * average
    normed = (
        (rows_float - average) * lax.rsqrt(spread + epsilon) * norm_gain.astype(jnp.float32)
    ).astype(jnp.bfloat16)
    query_part = jnp.dot(
        lax.all_gather(normed, "wide", axis=1, tiled=True),
        w_query,
        preferred_element_type=jnp.float32,
    ).reshape(steps, narrow_count, batch // narrow_count, w_query.shape[1])
    keyval_part = jnp.dot(normed, w_keyval, preferred_element_type=jnp.float32)
    keyval_part = keyval_part.reshape(steps, batch, w_keyval.shape[1])
    query_half = lax.psum_scatter(query_part, "narrow", scatter_dimension=1, tiled=False)
    query_local = lax.all_to_all(
        query_half.astype(jnp.bfloat16), "wide", split_axis=1, concat_axis=2, tiled=True
    )
    keyval_local = lax.psum_scatter(
        keyval_part, ("narrow", "wide"), scatter_dimension=1, tiled=True
    )
    positions = (lengths[:, None] + jnp.arange(steps)).astype(jnp.float32)
    query_local = query_local.astype(jnp.float32).reshape(steps, count, H, DH).transpose(1, 0, 2, 3)
    keyval_local = keyval_local.transpose(1, 0, 2)
    rot_query = rotate(query_local, positions[..., None]).astype(jnp.bfloat16)
    new_keys = rotate(keyval_local[..., :DH], positions).astype(jnp.bfloat16)
    new_values = keyval_local[..., DH:].astype(jnp.bfloat16)
    context = attend(rot_query, cache_keys, cache_values, new_keys, new_values, lengths)
    context = context.reshape(count * steps, H * DH)
    joined = jnp.dot(
        lax.all_gather(context, ("narrow", "wide"), axis=0, tiled=True),
        w_out,
        preferred_element_type=jnp.float32,
    ).astype(jnp.bfloat16)
    return joined.reshape(batch, steps, w_out.shape[1]).transpose(1, 0, 2)


MIB = 1 << 20
EXTRA = 16
OUT_CUTS = (4, 7)
IN_VMEM = pl.BlockSpec(memory_space=pltpu.VMEM)
IN_SMEM = pl.BlockSpec(memory_space=pltpu.SMEM)
IN_HBM = pl.BlockSpec(memory_space=pltpu.HBM)


def call(kernel, name, out_shape, args, in_specs=None, scratch=(), limit=12 * MIB, flops=0, moved=None, aliases=None):
    if moved is None:
        moved = sum(a.size * a.dtype.itemsize for a in args)
    return pl.pallas_call(
        kernel,
        out_shape=out_shape,
        in_specs=in_specs or [IN_VMEM] * len(args),
        out_specs=jax.tree.map(lambda _: IN_VMEM, out_shape),
        scratch_shapes=list(scratch),
        compiler_params=pltpu.CompilerParams(vmem_limit_bytes=limit),
        input_output_aliases=aliases or {},
        cost_estimate=pl.CostEstimate(flops=flops, bytes_accessed=moved, transcendentals=0),
        name=name,
    )(*args)


def in_hbm(array):
    return pltpu.with_memory_space_constraint(array, pltpu.HBM)


def load_kernel(moves, *refs):
    target, sems = refs[-2], refs[-1]
    copies = [
        pltpu.make_async_copy(refs[source].at[box], target.at[to], sems.at[at])
        for at, (source, box, to) in enumerate(moves)
    ]
    for copy in copies:
        copy.start()
    for copy in copies:
        copy.wait()


def load(name, shape, moves, *sources, after=()):
    return call(
        functools.partial(load_kernel, moves),
        name,
        pltpu.VMEM(shape, sources[0].dtype),
        [in_hbm(source) for source in sources] + list(after),
        in_specs=[IN_HBM] * len(sources) + [pl.BlockSpec(memory_space=pl.ANY)] * len(after),
        scratch=[pltpu.SemaphoreType.DMA((len(moves),))],
        limit=MIB,
        moved=2 * shape[0] * shape[1],
    )


def boxes(rows, columns, pieces, at_row=0, source=0):
    step = rows.size // pieces
    return [
        (
            source,
            (pl.ds(rows.start + at * step, step), columns),
            (pl.ds(at_row + at * step, step), pl.ds(0, columns.size)),
        )
        for at in range(pieces)
    ]


def sums_kernel(tokens, out):
    rows = tokens.shape[0]
    lanes = out.shape[1]
    values = tokens[...].astype(jnp.float32)
    at_lane = lax.broadcasted_iota(jnp.int32, (rows, lanes), 1)
    at_row = lax.broadcasted_iota(jnp.int32, (rows, lanes), 0)
    out[...] = jnp.zeros_like(out)
    for row, column in enumerate(
        (
            jnp.sum(values, axis=1, keepdims=True),
            jnp.sum(values * values, axis=1, keepdims=True),
        )
    ):
        out[row : row + 1, :] = jnp.sum(
            jnp.where(at_lane == at_row, column, 0.0), axis=0, keepdims=True
        )


def payload_kernel(tokens, gain, mine, theirs, out, extra):
    rows, width = tokens.shape
    lanes = out.shape[1]
    parts = width // lanes
    extra[...] = jnp.zeros_like(extra)
    for at in range(parts):
        span = slice(at * lanes, (at + 1) * lanes)
        extra[at : at + 1, :] = gain[:, span].astype(jnp.float32)
        out[at * rows : (at + 1) * rows, :] = tokens[:, span]
    for at in range(2):
        left = mine[at : at + 1, :] + theirs[at : at + 1, :]
        for piece in range(3):
            row = parts + 3 * at + piece
            part = left.astype(jnp.bfloat16).astype(jnp.float32)
            extra[row : row + 1, :] = part
            left = left - part
    out[parts * rows :, :] = extra[...].astype(jnp.bfloat16)


class Stream:
    def __init__(self, copies, flight=16):
        self.copies, self.started, self.done = copies, 0, 0
        self.start(flight)

    def start(self, count):
        for copy in self.copies[self.started : self.started + count]:
            copy.start()
        self.started = min(self.started + count, len(self.copies))

    def take(self, at):
        while self.done <= at:
            self.copies[self.done].wait()
            self.done += 1
            self.start(1)


def project_kernel(steps, width_total, place, w_keyval_far, w_query, early, *refs):
    *blocks, keep, send, result, normed, late, w_keyval, sems = refs
    wide_at, narrow_at = place[0], place[1]
    rows = result.shape[0]
    width, part = w_keyval.shape[0], early.shape[1]
    columns = w_query.shape[1]
    lanes = blocks[0].shape[1]
    parts = width // lanes
    spots = [
        pl.ds(pl.multiple_of(jnp.bitwise_xor(wide_at, k) * width, width), width)
        for k in range(len(blocks))
    ]
    stream = Stream(
        [pltpu.make_async_copy(w_keyval_far, w_keyval, sems.at[len(blocks)])]
        + [
            pltpu.make_async_copy(
                w_query.at[spot, pl.ds(part, columns - part)], late.at[spot], sems.at[k]
            )
            for k, spot in enumerate(spots)
        ]
    )
    tail = pl.ds(parts * rows, blocks[0].shape[0] - parts * rows)
    sums = blocks[0][tail, :].astype(jnp.float32)
    for block in blocks[1:]:
        sums = sums + block[tail, :].astype(jnp.float32)
    totals = [
        sums[at : at + 1] + sums[at + 1 : at + 2] + sums[at + 2 : at + 3]
        for at in (parts, parts + 3)
    ]
    average = totals[0] / width_total
    spread = totals[1] / width_total - average * average
    scale = lax.rsqrt(spread + epsilon)
    at_lane = lax.broadcasted_iota(jnp.int32, (rows, lanes), 1)
    at_row = lax.broadcasted_iota(jnp.int32, (rows, lanes), 0)

    def stand(flat):
        return jnp.sum(jnp.where(at_lane == at_row, flat, 0.0), axis=1, keepdims=True)

    average, scale = stand(average), stand(scale)
    for weights, span in ((early, slice(0, part)), (late, slice(part, columns))):
        for k, block in enumerate(blocks):
            if weights is early:
                gains = block[tail, :].astype(jnp.float32)
                for at in range(parts):
                    values = block[at * rows : (at + 1) * rows, :].astype(jnp.float32)
                    normed[k, :, at * lanes : (at + 1) * lanes] = (
                        (values - average) * scale * gains[at : at + 1]
                    ).astype(jnp.bfloat16)
            else:
                stream.take(k + 1)
            product = jnp.dot(normed[k], weights[spots[k], :], preferred_element_type=jnp.float32)
            if k == 0:
                result[:, span] = product
            else:
                result[:, span] += product
            if weights is early and k in (3, 6):
                stream.take(k // 3 - 1)
    result[:, columns:] = jnp.dot(normed[0], w_keyval[...], preferred_element_type=jnp.float32)
    half = rows // steps // 2
    for step in range(steps):
        for out, core in ((keep, narrow_at), (send, 1 - narrow_at)):
            start = pl.multiple_of(step * 2 * half + core * half, half)
            out[step * half : (step + 1) * half, :] = result[pl.ds(start, half), :]


def combine_kernel(columns, mine, theirs, out, held):
    wide, steps, _ = out.shape
    lanes = held.shape[2]
    extent = mine.shape[1]
    for at in range(0, extent, lanes):
        total = mine[:, at : at + lanes] + theirs[:, at : at + lanes]
        if at < columns:
            held[at // lanes] = total
        else:
            high = total.astype(jnp.bfloat16).astype(jnp.float32)
            held[at // lanes] = high
            held[(at + extent - columns) // lanes] = total - high
    for at in range(held.shape[0]):
        for to in range(wide):
            out[to, :, at * lanes : (at + 1) * lanes] = held[
                at, pl.ds(to, steps, stride=wide), :
            ].astype(jnp.bfloat16)


def attend_kernel(
    columns, length, cosine, sine, arrived, cache, out, queries, fresh_rows
):
    slots = cache.shape[0] // 2
    wide, steps, _ = arrived.shape
    size = cache.shape[1]
    half = size // 2
    heads = columns // size
    cos, sin = cosine[...], sine[...]

    def turn(vectors):
        first, second = vectors[:, :half], vectors[:, half:]
        return first * cos - second * sin, second * cos + first * sin

    for source in range(wide):
        for head in range(heads):
            at = (source * heads + head) * steps
            low, high = turn(
                arrived[source, :, head * size : (head + 1) * size].astype(jnp.float32)
            )
            queries[at : at + steps, :half] = low
            queries[at : at + steps, half:] = high
    keyval = jnp.zeros((steps, 2 * size), jnp.float32)
    for source in range(wide):
        high = arrived[source, :, columns : columns + 2 * size].astype(jnp.float32)
        low = arrived[source, :, columns + 2 * size :].astype(jnp.float32)
        keyval = keyval + (high + low)
    fresh_rows[...] = jnp.zeros_like(fresh_rows)
    low, high = turn(keyval[:, :size])
    fresh_rows[0, :steps, :half] = low
    fresh_rows[0, :steps, half:] = high
    fresh_rows[1, :steps, :] = keyval[:, size:]
    query = queries[...].astype(jnp.bfloat16)
    new_keys = fresh_rows[0].astype(jnp.bfloat16)
    new_values = fresh_rows[1].astype(jnp.bfloat16)
    score_scale = 1.0 / size**0.5
    by_row = (((1,), (1,)), ((), ()))
    scores = score_scale * lax.dot_general(
        query, cache[:slots, :], by_row, preferred_element_type=jnp.float32
    )
    fresh = score_scale * lax.dot_general(
        query, new_keys, by_row, preferred_element_type=jnp.float32
    )
    valid = lax.broadcasted_iota(jnp.int32, scores.shape, 1) < length[0]
    row_step = lax.rem(lax.broadcasted_iota(jnp.int32, fresh.shape, 0), steps)
    seen = lax.broadcasted_iota(jnp.int32, fresh.shape, 1) <= row_step
    scores = jnp.where(valid, scores, -1e30)
    fresh = jnp.where(seen, fresh, -1e30)
    highest = jnp.maximum(
        jnp.max(scores, axis=1, keepdims=True), jnp.max(fresh, axis=1, keepdims=True)
    )
    weights = jnp.where(valid, jnp.exp(scores - highest), 0.0)
    fresh_weights = jnp.where(seen, jnp.exp(fresh - highest), 0.0)
    share = 1.0 / (
        jnp.sum(weights, axis=1, keepdims=True) + jnp.sum(fresh_weights, axis=1, keepdims=True)
    )
    context = jnp.dot(
        (weights * share).astype(jnp.bfloat16),
        cache[slots:, :],
        preferred_element_type=jnp.float32,
    ) + jnp.dot(
        (fresh_weights * share).astype(jnp.bfloat16),
        new_values,
        preferred_element_type=jnp.float32,
    )
    queries[...] = context
    for head in range(wide * heads):
        out[:, head * size : (head + 1) * size] = queries[
            head * steps : (head + 1) * steps, :
        ].astype(jnp.bfloat16)


def output_kernel(steps, depth, place, w_out, *refs):
    *blocks, out, result, ordered, late, sems = refs
    parts, blocks = [*blocks[:2], late], blocks[2:]
    wide_at, narrow_at = place[0], place[1]
    batch = len(blocks)
    count = batch // 2
    pieces = sems.shape[0]
    size = late.shape[0] // pieces
    stream = Stream(
        [
            pltpu.make_async_copy(
                w_out.at[pl.ds(w_out.shape[0] - late.shape[0] + at * size, size)],
                late.at[pl.ds(at * size, size)],
                sems.at[at],
            )
            for at in range(pieces)
        ]
    )
    chunks = [(part, at) for part in parts for at in range(0, part.shape[0], depth)]
    for index, (part, inside) in enumerate(chunks):
        span = slice(index * depth, (index + 1) * depth)
        rows = jnp.concatenate([block[:, span] for block in blocks], axis=0)
        if part is late:
            stream.take((inside + depth) // size - 1)
        product = jnp.dot(rows, part[inside : inside + depth, :], preferred_element_type=jnp.float32)
        if index == 0:
            result[...] = product
        else:
            result[...] += product
        if index in (3, 5):
            stream.take(index // 2 - 1)
    for core in range(2):
        for k in range(count):
            sequence = jnp.bitwise_xor(narrow_at, core) * count + jnp.bitwise_xor(wide_at, k)
            for step in range(steps):
                row = core * count * steps + k * steps + step
                ordered[pl.ds(step * batch + sequence, 1), :] = result[row : row + 1, :]
    for step in range(steps):
        out[step] = ordered[step * batch : (step + 1) * batch, :].astype(jnp.bfloat16)


def swap(value, axis, bits):
    size = lax.axis_size(axis)
    return lax.ppermute(value, axis, [(at, at ^ bits) for at in range(size)])


def gather_tokens(block):
    near = {0: block}
    for bits in (4, 2, 1):
        near[bits] = swap(block, "wide", bits)
    near[4], near[2], near[1] = lax.optimization_barrier((near[4], near[2], near[1]))
    near[6] = swap(near[4], "wide", 2)
    near[5] = swap(near[4], "wide", 1)
    near[5], near[2] = lax.optimization_barrier((near[5], near[2]))
    near[7] = swap(near[5], "wide", 2)
    near[3] = swap(near[2], "wide", 1)
    return [near[k] for k in range(8)]


def gather_contexts(block, loader):
    near = {0: block}
    for bits in (4, 2, 1):
        near[bits] = swap(block, "wide", bits)
    first = loader(0, block)
    near[1], near[2], near[4], first = lax.optimization_barrier((near[1], near[2], near[4], first))
    near[6] = swap(near[4], "wide", 2)
    near[5] = swap(near[4], "wide", 1)
    near[3] = swap(near[2], "wide", 1)
    near[7] = swap(near[5], "wide", 2)
    second = loader(1, near[4])
    near[3], near[6], near[7], second = lax.optimization_barrier(
        (near[3], near[6], near[7], second)
    )
    return [near[k] for k in range(8)], [first, second]


def local_fast(tokens, norm_gain, w_query, w_keyval, w_out, cache_keys, cache_values, lengths):
    wide_count = lax.axis_size("wide")
    narrow_count = lax.axis_size("narrow")
    steps, batch, width = tokens.shape
    rows = steps * batch
    columns, tail = w_query.shape[1], w_keyval.shape[1]
    size = cache_keys.shape[2]
    f32, bf16 = jnp.float32, jnp.bfloat16
    place = jnp.stack([lax.axis_index("wide"), lax.axis_index("narrow")]).astype(jnp.int32)

    own = tokens.reshape(rows, width)
    sums = call(sums_kernel, "row_sums", jax.ShapeDtypeStruct((8, 128), f32), [own])
    payload = call(
        payload_kernel,
        "payload",
        jax.ShapeDtypeStruct((width // 128 * rows + EXTRA, 128), bf16),
        [own, norm_gain[None], sums, swap(sums, "narrow", 1)],
        scratch=[pltpu.VMEM((EXTRA, 128), f32)],
    )
    blocks = gather_tokens(payload)
    part = columns // 3 * 2
    deep = w_query.shape[0]
    early_weights = load(
        "load_query_weights",
        (deep, part),
        boxes(pl.ds(0, deep), pl.ds(0, part), 8),
        w_query,
    )
    keep, send = call(
        functools.partial(project_kernel, steps, width * wide_count * narrow_count),
        "norm_and_project",
        [jax.ShapeDtypeStruct((rows // 2, columns + tail), f32)] * 2,
        [place, in_hbm(w_keyval), in_hbm(w_query), early_weights, *blocks],
        in_specs=[IN_SMEM, IN_HBM, IN_HBM] + [IN_VMEM] * (wide_count + 1),
        scratch=[
            pltpu.VMEM((rows, columns + tail), f32),
            pltpu.VMEM((wide_count, rows, width), bf16),
            pltpu.VMEM((deep, columns - part), bf16),
            pltpu.VMEM(w_keyval.shape, bf16),
            pltpu.SemaphoreType.DMA((wide_count + 1,)),
        ],
        limit=24 * MIB,
        flops=2 * rows * width * wide_count * columns,
    )
    outgoing = call(
        functools.partial(combine_kernel, columns),
        "sum_of_cores",
        jax.ShapeDtypeStruct((wide_count, steps, columns + 2 * tail), bf16),
        [keep, swap(send, "narrow", 1)],
        scratch=[pltpu.VMEM(((columns + 2 * tail) // 128, rows // 2, 128), f32)],
    )
    arrived = lax.all_to_all(outgoing, "wide", 0, 0, tiled=True)
    slots = cache_keys.shape[1]
    cache = load(
        "load_cache",
        (2 * slots, size),
        boxes(pl.ds(0, slots), pl.ds(0, size), 4)
        + boxes(pl.ds(0, slots), pl.ds(0, size), 4, at_row=slots, source=1),
        cache_keys.reshape(slots, size),
        cache_values.reshape(slots, size),
        after=[outgoing],
    )
    ladder = jnp.arange(size // 2, dtype=f32)
    frequency = jnp.exp(ladder * (-2.0 / size) * jnp.log(10000.0))
    angles = (lengths + jnp.arange(steps)).astype(f32)[:, None] * frequency
    context = call(
        functools.partial(attend_kernel, columns),
        "attention",
        jax.ShapeDtypeStruct((steps, H * size), bf16),
        [lengths, jnp.cos(angles), jnp.sin(angles), arrived, cache],
        in_specs=[IN_SMEM] + [IN_VMEM] * 4,
        scratch=[
            pltpu.VMEM((steps * H, size), f32),
            pltpu.VMEM((2, 128, size), f32),
        ],
        limit=16 * MIB,
        flops=4 * steps * H * size * slots,
    )
    depth = w_out.shape[0] // 12
    bounds = (0, OUT_CUTS[0] * depth, OUT_CUTS[1] * depth, w_out.shape[0])

    def load_out(at, block):
        size = bounds[at + 1] - bounds[at]
        return load(
            "load_out_weights",
            (size, w_out.shape[1]),
            boxes(pl.ds(bounds[at], size), pl.ds(0, w_out.shape[1]), 8),
            w_out,
            after=[block],
        )

    contexts, early_weights = gather_contexts(context, load_out)
    deep = bounds[3] - bounds[2]
    contexts = contexts + [swap(block, "narrow", 1) for block in contexts]
    return call(
        functools.partial(output_kernel, steps, depth),
        "project_out",
        jax.ShapeDtypeStruct((steps, batch, w_out.shape[1]), bf16),
        [place, in_hbm(w_out), *early_weights, *contexts],
        in_specs=[IN_SMEM, IN_HBM] + [IN_VMEM] * (2 + batch),
        scratch=[
            pltpu.VMEM((rows, w_out.shape[1]), f32),
            pltpu.VMEM((rows, w_out.shape[1]), f32),
            pltpu.VMEM((deep, w_out.shape[1]), bf16),
            pltpu.SemaphoreType.DMA((deep // depth * 2,)),
        ],
        limit=28 * MIB,
        flops=2 * rows * w_out.size,
    )


def local(tokens, norm_gain, w_query, w_keyval, w_out, cache_keys, cache_values, lengths):
    fits = (
        lengths.shape[0] == 1
        and lax.axis_size("narrow") == 2
        and lax.axis_size("wide") == 8
        and tokens.shape[1] == 16
        and tokens.shape[2] % 128 == 0
        and tokens.shape[2] // 128 + 6 <= EXTRA
        and tokens.shape[0] * 16 <= 128
    )
    return (local_fast if fits else local_plain)(
        tokens, norm_gain, w_query, w_keyval, w_out, cache_keys, cache_values, lengths
    )


def solution(mesh):
    placed = (
        P(None, "groups", ("narrow", "wide")),
        P(("narrow", "wide")),
        P("narrow", "wide"),
        P(("narrow", "wide"), None),
        P(None, ("narrow", "wide")),
        P(("groups", "narrow", "wide"), None, None),
        P(("groups", "narrow", "wide"), None, None),
        P(("groups", "narrow", "wide")),
    )
    return jax.shard_map(
        local,
        mesh=mesh,
        in_specs=placed,
        out_specs=P(None, "groups", ("narrow", "wide")),
        check_vma=False,
    )
```

```python
import functools

import jax
import jax.numpy as jnp
from jax import lax
from jax.experimental import pallas as pl
from jax.experimental.pallas import tpu as pltpu
from jax.sharding import PartitionSpec as P

H = 48
DH = 256


epsilon = 1e-06


def rotate(vectors, positions):
    half_size = vectors.shape[-1] // 2
    ladder = jnp.arange(half_size, dtype=jnp.float32)
    frequency = jnp.exp(ladder * (-2.0 / vectors.shape[-1]) * jnp.log(10000.0))
    angles = positions[..., None] * frequency
    cosine = jnp.cos(angles)
    sine = jnp.sin(angles)
    first_half = vectors[..., :half_size]
    second_half = vectors[..., half_size:]
    return jnp.concatenate(
        [first_half * cosine - second_half * sine, second_half * cosine + first_half * sine],
        axis=-1,
    )


def attend(rot_query, cache_keys, cache_values, new_keys, new_values, lengths):
    count, steps, heads, size = rot_query.shape
    score_scale = 1.0 / jnp.sqrt(jnp.float32(DH))
    flat = rot_query.reshape(count, steps * heads, size)
    cache_scores = (
        jnp.einsum("bhd,bsd->bhs", flat, cache_keys, preferred_element_type=jnp.float32)
        * score_scale
    )
    valid = jnp.arange(cache_keys.shape[1])[None, None, :] < lengths[:, None, None]
    masked = jnp.where(valid, cache_scores, -1e30)
    fresh = (
        jnp.einsum("bhd,bjd->bhj", flat, new_keys, preferred_element_type=jnp.float32)
        * score_scale
    )
    row_step = jnp.arange(steps * heads) // heads
    seen = (jnp.arange(steps)[None, :] <= row_step[:, None])[None]
    fresh = jnp.where(seen, fresh, -1e30)
    highest = jnp.maximum(jnp.max(masked, axis=-1), jnp.max(fresh, axis=-1))[..., None]
    cache_weights = jnp.where(valid, jnp.exp(masked - highest), 0.0)
    fresh_weights = jnp.where(seen, jnp.exp(fresh - highest), 0.0)
    total = jnp.sum(cache_weights, axis=-1, keepdims=True) + jnp.sum(
        fresh_weights, axis=-1, keepdims=True
    )
    cache_probs = (cache_weights / total).astype(jnp.bfloat16)
    fresh_probs = (fresh_weights / total).astype(jnp.bfloat16)
    context = jnp.einsum(
        "bhs,bsd->bhd", cache_probs, cache_values, preferred_element_type=jnp.float32
    )
    context = context + jnp.einsum(
        "bhj,bjd->bhd", fresh_probs, new_values, preferred_element_type=jnp.float32
    )
    return context.astype(jnp.bfloat16).reshape(count, steps, heads, size)


def local_plain(tokens, norm_gain, w_query, w_keyval, w_out, cache_keys, cache_values, lengths):
    wide_count = lax.axis_size("wide")
    narrow_count = lax.axis_size("narrow")
    steps, batch, width = tokens.shape
    count = lengths.shape[0]
    rows_all = steps * batch
    width_total = width * wide_count * narrow_count
    rows_float = tokens.reshape(rows_all, width).astype(jnp.float32)
    row_sum, row_squares = lax.psum(
        (jnp.sum(rows_float, axis=1), jnp.sum(rows_float * rows_float, axis=1)),
        ("wide", "narrow"),
    )
    average = (row_sum / width_total)[:, None]
    spread = (row_squares / width_total)[:, None] - average * average
    normed = (
        (rows_float - average) * lax.rsqrt(spread + epsilon) * norm_gain.astype(jnp.float32)
    ).astype(jnp.bfloat16)
    query_part = jnp.dot(
        lax.all_gather(normed, "wide", axis=1, tiled=True),
        w_query,
        preferred_element_type=jnp.float32,
    ).reshape(steps, narrow_count, batch // narrow_count, w_query.shape[1])
    keyval_part = jnp.dot(normed, w_keyval, preferred_element_type=jnp.float32)
    keyval_part = keyval_part.reshape(steps, batch, w_keyval.shape[1])
    query_half = lax.psum_scatter(query_part, "narrow", scatter_dimension=1, tiled=False)
    query_local = lax.all_to_all(
        query_half.astype(jnp.bfloat16), "wide", split_axis=1, concat_axis=2, tiled=True
    )
    keyval_local = lax.psum_scatter(
        keyval_part, ("narrow", "wide"), scatter_dimension=1, tiled=True
    )
    positions = (lengths[:, None] + jnp.arange(steps)).astype(jnp.float32)
    query_local = query_local.astype(jnp.float32).reshape(steps, count, H, DH).transpose(1, 0, 2, 3)
    keyval_local = keyval_local.transpose(1, 0, 2)
    rot_query = rotate(query_local, positions[..., None]).astype(jnp.bfloat16)
    new_keys = rotate(keyval_local[..., :DH], positions).astype(jnp.bfloat16)
    new_values = keyval_local[..., DH:].astype(jnp.bfloat16)
    context = attend(rot_query, cache_keys, cache_values, new_keys, new_values, lengths)
    context = context.reshape(count * steps, H * DH)
    joined = jnp.dot(
        lax.all_gather(context, ("narrow", "wide"), axis=0, tiled=True),
        w_out,
        preferred_element_type=jnp.float32,
    ).astype(jnp.bfloat16)
    return joined.reshape(batch, steps, w_out.shape[1]).transpose(1, 0, 2)


MIB = 1 << 20
EXTRA = 16
OUT_CUTS = (4, 7)
IN_VMEM = pl.BlockSpec(memory_space=pltpu.VMEM)
IN_SMEM = pl.BlockSpec(memory_space=pltpu.SMEM)
IN_HBM = pl.BlockSpec(memory_space=pltpu.HBM)


def call(kernel, name, out_shape, args, in_specs=None, scratch=(), limit=12 * MIB, flops=0, moved=None, aliases=None):
    if moved is None:
        moved = sum(a.size * a.dtype.itemsize for a in args)
    return pl.pallas_call(
        kernel,
        out_shape=out_shape,
        in_specs=in_specs or [IN_VMEM] * len(args),
        out_specs=jax.tree.map(lambda _: IN_VMEM, out_shape),
        scratch_shapes=list(scratch),
        compiler_params=pltpu.CompilerParams(vmem_limit_bytes=limit),
        input_output_aliases=aliases or {},
        cost_estimate=pl.CostEstimate(flops=flops, bytes_accessed=moved, transcendentals=0),
        name=name,
    )(*args)


def in_hbm(array):
    return pltpu.with_memory_space_constraint(array, pltpu.HBM)


def load_kernel(moves, *refs):
    target, sems = refs[-2], refs[-1]
    copies = [
        pltpu.make_async_copy(refs[source].at[box], target.at[to], sems.at[at])
        for at, (source, box, to) in enumerate(moves)
    ]
    for copy in copies:
        copy.start()
    for copy in copies:
        copy.wait()


def load(name, shape, moves, *sources, after=()):
    return call(
        functools.partial(load_kernel, moves),
        name,
        pltpu.VMEM(shape, sources[0].dtype),
        [in_hbm(source) for source in sources] + list(after),
        in_specs=[IN_HBM] * len(sources) + [pl.BlockSpec(memory_space=pl.ANY)] * len(after),
        scratch=[pltpu.SemaphoreType.DMA((len(moves),))],
        limit=MIB,
        moved=2 * shape[0] * shape[1],
    )


def boxes(rows, columns, pieces, at_row=0, source=0):
    step = rows.size // pieces
    return [
        (
            source,
            (pl.ds(rows.start + at * step, step), columns),
            (pl.ds(at_row + at * step, step), pl.ds(0, columns.size)),
        )
        for at in range(pieces)
    ]


def sums_kernel(tokens, out):
    rows = tokens.shape[0]
    lanes = out.shape[1]
    values = tokens[...].astype(jnp.float32)
    at_lane = lax.broadcasted_iota(jnp.int32, (rows, lanes), 1)
    at_row = lax.broadcasted_iota(jnp.int32, (rows, lanes), 0)
    out[...] = jnp.zeros_like(out)
    for row, column in enumerate(
        (
            jnp.sum(values, axis=1, keepdims=True),
            jnp.sum(values * values, axis=1, keepdims=True),
        )
    ):
        out[row : row + 1, :] = jnp.sum(
            jnp.where(at_lane == at_row, column, 0.0), axis=0, keepdims=True
        )


def payload_kernel(tokens, gain, mine, theirs, out, extra):
    rows, width = tokens.shape
    lanes = out.shape[1]
    parts = width // lanes
    extra[...] = jnp.zeros_like(extra)
    for at in range(parts):
        span = slice(at * lanes, (at + 1) * lanes)
        extra[at : at + 1, :] = gain[:, span].astype(jnp.float32)
        out[at * rows : (at + 1) * rows, :] = tokens[:, span]
    for at in range(2):
        left = mine[at : at + 1, :] + theirs[at : at + 1, :]
        for piece in range(3):
            row = parts + 3 * at + piece
            part = left.astype(jnp.bfloat16).astype(jnp.float32)
            extra[row : row + 1, :] = part
            left = left - part
    out[parts * rows :, :] = extra[...].astype(jnp.bfloat16)


class Stream:
    def __init__(self, copies, flight=16):
        self.copies, self.started, self.done = copies, 0, 0
        self.start(flight)

    def start(self, count):
        for copy in self.copies[self.started : self.started + count]:
            copy.start()
        self.started = min(self.started + count, len(self.copies))

    def take(self, at):
        while self.done <= at:
            self.copies[self.done].wait()
            self.done += 1
            self.start(1)


def project_kernel(steps, width_total, place, w_keyval_far, w_query, early, *refs):
    *blocks, keep, send, result, normed, late, w_keyval, sems = refs
    wide_at, narrow_at = place[0], place[1]
    rows = result.shape[0]
    width, part = w_keyval.shape[0], early.shape[1]
    columns = w_query.shape[1]
    lanes = blocks[0].shape[1]
    parts = width // lanes
    spots = [
        pl.ds(pl.multiple_of(jnp.bitwise_xor(wide_at, k) * width, width), width)
        for k in range(len(blocks))
    ]
    stream = Stream(
        [pltpu.make_async_copy(w_keyval_far, w_keyval, sems.at[len(blocks)])]
        + [
            pltpu.make_async_copy(
                w_query.at[spot, pl.ds(part, columns - part)], late.at[spot], sems.at[k]
            )
            for k, spot in enumerate(spots)
        ]
    )
    tail = pl.ds(parts * rows, blocks[0].shape[0] - parts * rows)
    sums = blocks[0][tail, :].astype(jnp.float32)
    for block in blocks[1:]:
        sums = sums + block[tail, :].astype(jnp.float32)
    totals = [
        sums[at : at + 1] + sums[at + 1 : at + 2] + sums[at + 2 : at + 3]
        for at in (parts, parts + 3)
    ]
    average = totals[0] / width_total
    spread = totals[1] / width_total - average * average
    scale = lax.rsqrt(spread + epsilon)
    at_lane = lax.broadcasted_iota(jnp.int32, (rows, lanes), 1)
    at_row = lax.broadcasted_iota(jnp.int32, (rows, lanes), 0)

    def stand(flat):
        return jnp.sum(jnp.where(at_lane == at_row, flat, 0.0), axis=1, keepdims=True)

    average, scale = stand(average), stand(scale)
    for weights, span in ((early, slice(0, part)), (late, slice(part, columns))):
        for k, block in enumerate(blocks):
            if weights is early:
                gains = block[tail, :].astype(jnp.float32)
                for at in range(parts):
                    values = block[at * rows : (at + 1) * rows, :].astype(jnp.float32)
                    normed[k, :, at * lanes : (at + 1) * lanes] = (
                        (values - average) * scale * gains[at : at + 1]
                    ).astype(jnp.bfloat16)
            else:
                stream.take(k + 1)
            product = jnp.dot(normed[k], weights[spots[k], :], preferred_element_type=jnp.float32)
            if k == 0:
                result[:, span] = product
            else:
                result[:, span] += product
            if weights is early and k in (3, 6):
                stream.take(k // 3 - 1)
    result[:, columns:] = jnp.dot(normed[0], w_keyval[...], preferred_element_type=jnp.float32)
    half = rows // steps // 2
    for step in range(steps):
        for out, core in ((keep, narrow_at), (send, 1 - narrow_at)):
            start = pl.multiple_of(step * 2 * half + core * half, half)
            out[step * half : (step + 1) * half, :] = result[pl.ds(start, half), :]


def combine_kernel(columns, mine, theirs, out, held):
    wide, steps, _ = out.shape
    lanes = held.shape[2]
    extent = mine.shape[1]
    for at in range(0, extent, lanes):
        total = mine[:, at : at + lanes] + theirs[:, at : at + lanes]
        if at < columns:
            held[at // lanes] = total
        else:
            high = total.astype(jnp.bfloat16).astype(jnp.float32)
            held[at // lanes] = high
            held[(at + extent - columns) // lanes] = total - high
    for at in range(held.shape[0]):
        for to in range(wide):
            out[to, :, at * lanes : (at + 1) * lanes] = held[
                at, pl.ds(to, steps, stride=wide), :
            ].astype(jnp.bfloat16)


def attend_kernel(
    columns, length, cosine, sine, arrived, cache, out, queries, fresh_rows
):
    slots = cache.shape[0] // 2
    wide, steps, _ = arrived.shape
    size = cache.shape[1]
    half = size // 2
    heads = columns // size
    cos, sin = cosine[...], sine[...]

    def turn(vectors):
        first, second = vectors[:, :half], vectors[:, half:]
        return first * cos - second * sin, second * cos + first * sin

    for source in range(wide):
        for head in range(heads):
            at = (source * heads + head) * steps
            low, high = turn(
                arrived[source, :, head * size : (head + 1) * size].astype(jnp.float32)
            )
            queries[at : at + steps, :half] = low
            queries[at : at + steps, half:] = high
    keyval = jnp.zeros((steps, 2 * size), jnp.float32)
    for source in range(wide):
        high = arrived[source, :, columns : columns + 2 * size].astype(jnp.float32)
        low = arrived[source, :, columns + 2 * size :].astype(jnp.float32)
        keyval = keyval + (high + low)
    fresh_rows[...] = jnp.zeros_like(fresh_rows)
    low, high = turn(keyval[:, :size])
    fresh_rows[0, :steps, :half] = low
    fresh_rows[0, :steps, half:] = high
    fresh_rows[1, :steps, :] = keyval[:, size:]
    query = queries[...].astype(jnp.bfloat16)
    new_keys = fresh_rows[0].astype(jnp.bfloat16)
    new_values = fresh_rows[1].astype(jnp.bfloat16)
    score_scale = 1.0 / size**0.5
    by_row = (((1,), (1,)), ((), ()))
    scores = score_scale * lax.dot_general(
        query, cache[:slots, :], by_row, preferred_element_type=jnp.float32
    )
    fresh = score_scale * lax.dot_general(
        query, new_keys, by_row, preferred_element_type=jnp.float32
    )
    valid = lax.broadcasted_iota(jnp.int32, scores.shape, 1) < length[0]
    row_step = lax.rem(lax.broadcasted_iota(jnp.int32, fresh.shape, 0), steps)
    seen = lax.broadcasted_iota(jnp.int32, fresh.shape, 1) <= row_step
    scores = jnp.where(valid, scores, -1e30)
    fresh = jnp.where(seen, fresh, -1e30)
    highest = jnp.maximum(
        jnp.max(scores, axis=1, keepdims=True), jnp.max(fresh, axis=1, keepdims=True)
    )
    weights = jnp.where(valid, jnp.exp(scores - highest), 0.0)
    fresh_weights = jnp.where(seen, jnp.exp(fresh - highest), 0.0)
    share = 1.0 / (
        jnp.sum(weights, axis=1, keepdims=True) + jnp.sum(fresh_weights, axis=1, keepdims=True)
    )
    context = jnp.dot(
        (weights * share).astype(jnp.bfloat16),
        cache[slots:, :],
        preferred_element_type=jnp.float32,
    ) + jnp.dot(
        (fresh_weights * share).astype(jnp.bfloat16),
        new_values,
        preferred_element_type=jnp.float32,
    )
    queries[...] = context
    for head in range(wide * heads):
        out[:, head * size : (head + 1) * size] = queries[
            head * steps : (head + 1) * steps, :
        ].astype(jnp.bfloat16)


def output_kernel(steps, depth, place, w_out, *refs):
    *blocks, out, result, ordered, late, sems = refs
    parts, blocks = [*blocks[:2], late], blocks[2:]
    wide_at, narrow_at = place[0], place[1]
    batch = len(blocks)
    count = batch // 2
    pieces = sems.shape[0]
    size = late.shape[0] // pieces
    stream = Stream(
        [
            pltpu.make_async_copy(
                w_out.at[pl.ds(w_out.shape[0] - late.shape[0] + at * size, size)],
                late.at[pl.ds(at * size, size)],
                sems.at[at],
            )
            for at in range(pieces)
        ]
    )
    chunks = [(part, at) for part in parts for at in range(0, part.shape[0], depth)]
    for index, (part, inside) in enumerate(chunks):
        span = slice(index * depth, (index + 1) * depth)
        rows = jnp.concatenate([block[:, span] for block in blocks], axis=0)
        if part is late:
            stream.take((inside + depth) // size - 1)
        product = jnp.dot(rows, part[inside : inside + depth, :], preferred_element_type=jnp.float32)
        if index == 0:
            result[...] = product
        else:
            result[...] += product
        if index in (3, 5):
            stream.take(index // 2 - 1)
    for core in range(2):
        for k in range(count):
            sequence = jnp.bitwise_xor(narrow_at, core) * count + jnp.bitwise_xor(wide_at, k)
            for step in range(steps):
                row = core * count * steps + k * steps + step
                ordered[pl.ds(step * batch + sequence, 1), :] = result[row : row + 1, :]
    for step in range(steps):
        out[step] = ordered[step * batch : (step + 1) * batch, :].astype(jnp.bfloat16)


def swap(value, axis, bits):
    size = lax.axis_size(axis)
    return lax.ppermute(value, axis, [(at, at ^ bits) for at in range(size)])


def gather_tokens(block):
    near = {0: block}
    for bits in (4, 2, 1):
        near[bits] = swap(block, "wide", bits)
    near[4], near[2], near[1] = lax.optimization_barrier((near[4], near[2], near[1]))
    near[6] = swap(near[4], "wide", 2)
    near[5] = swap(near[4], "wide", 1)
    near[5], near[2] = lax.optimization_barrier((near[5], near[2]))
    near[7] = swap(near[5], "wide", 2)
    near[3] = swap(near[2], "wide", 1)
    return [near[k] for k in range(8)]


def gather_contexts(block, loader):
    near = {0: block}
    for bits in (4, 2, 1):
        near[bits] = swap(block, "wide", bits)
    first = loader(0, block)
    near[2], near[4], near[1], first = lax.optimization_barrier((near[2], near[4], near[1], first))
    near[6] = swap(near[4], "wide", 2)
    near[5] = swap(near[4], "wide", 1)
    near[3] = swap(near[2], "wide", 1)
    near[7] = swap(near[5], "wide", 2)
    second = loader(1, near[4])
    near[3], near[6], near[7], second = lax.optimization_barrier(
        (near[3], near[6], near[7], second)
    )
    return [near[k] for k in range(8)], [first, second]


def local_fast(tokens, norm_gain, w_query, w_keyval, w_out, cache_keys, cache_values, lengths):
    wide_count = lax.axis_size("wide")
    narrow_count = lax.axis_size("narrow")
    steps, batch, width = tokens.shape
    rows = steps * batch
    columns, tail = w_query.shape[1], w_keyval.shape[1]
    size = cache_keys.shape[2]
    f32, bf16 = jnp.float32, jnp.bfloat16
    place = jnp.stack([lax.axis_index("wide"), lax.axis_index("narrow")]).astype(jnp.int32)

    own = tokens.reshape(rows, width)
    sums = call(sums_kernel, "row_sums", jax.ShapeDtypeStruct((8, 128), f32), [own])
    payload = call(
        payload_kernel,
        "payload",
        jax.ShapeDtypeStruct((width // 128 * rows + EXTRA, 128), bf16),
        [own, norm_gain[None], sums, swap(sums, "narrow", 1)],
        scratch=[pltpu.VMEM((EXTRA, 128), f32)],
    )
    blocks = gather_tokens(payload)
    part = columns // 3 * 2
    deep = w_query.shape[0]
    early_weights = load(
        "load_query_weights",
        (deep, part),
        boxes(pl.ds(0, deep), pl.ds(0, part), 4),
        w_query,
    )
    keep, send = call(
        functools.partial(project_kernel, steps, width * wide_count * narrow_count),
        "norm_and_project",
        [jax.ShapeDtypeStruct((rows // 2, columns + tail), f32)] * 2,
        [place, in_hbm(w_keyval), in_hbm(w_query), early_weights, *blocks],
        in_specs=[IN_SMEM, IN_HBM, IN_HBM] + [IN_VMEM] * (wide_count + 1),
        scratch=[
            pltpu.VMEM((rows, columns + tail), f32),
            pltpu.VMEM((wide_count, rows, width), bf16),
            pltpu.VMEM((deep, columns - part), bf16),
            pltpu.VMEM(w_keyval.shape, bf16),
            pltpu.SemaphoreType.DMA((wide_count + 1,)),
        ],
        limit=24 * MIB,
        flops=2 * rows * width * wide_count * columns,
    )
    outgoing = call(
        functools.partial(combine_kernel, columns),
        "sum_of_cores",
        jax.ShapeDtypeStruct((wide_count, steps, columns + 2 * tail), bf16),
        [keep, swap(send, "narrow", 1)],
        scratch=[pltpu.VMEM(((columns + 2 * tail) // 128, rows // 2, 128), f32)],
    )
    arrived = lax.all_to_all(outgoing, "wide", 0, 0, tiled=True)
    slots = cache_keys.shape[1]
    cache = load(
        "load_cache",
        (2 * slots, size),
        boxes(pl.ds(0, slots), pl.ds(0, size), 4)
        + boxes(pl.ds(0, slots), pl.ds(0, size), 4, at_row=slots, source=1),
        cache_keys.reshape(slots, size),
        cache_values.reshape(slots, size),
        after=[outgoing],
    )
    ladder = jnp.arange(size // 2, dtype=f32)
    frequency = jnp.exp(ladder * (-2.0 / size) * jnp.log(10000.0))
    angles = (lengths + jnp.arange(steps)).astype(f32)[:, None] * frequency
    context = call(
        functools.partial(attend_kernel, columns),
        "attention",
        jax.ShapeDtypeStruct((steps, H * size), bf16),
        [lengths, jnp.cos(angles), jnp.sin(angles), arrived, cache],
        in_specs=[IN_SMEM] + [IN_VMEM] * 4,
        scratch=[
            pltpu.VMEM((steps * H, size), f32),
            pltpu.VMEM((2, 128, size), f32),
        ],
        limit=16 * MIB,
        flops=4 * steps * H * size * slots,
    )
    depth = w_out.shape[0] // 12
    bounds = (0, OUT_CUTS[0] * depth, OUT_CUTS[1] * depth, w_out.shape[0])

    def load_out(at, block):
        size = bounds[at + 1] - bounds[at]
        return load(
            "load_out_weights",
            (size, w_out.shape[1]),
            boxes(pl.ds(bounds[at], size), pl.ds(0, w_out.shape[1]), 4),
            w_out,
            after=[block],
        )

    contexts, early_weights = gather_contexts(context, load_out)
    deep = bounds[3] - bounds[2]
    contexts = contexts + [swap(block, "narrow", 1) for block in contexts]
    return call(
        functools.partial(output_kernel, steps, depth),
        "project_out",
        jax.ShapeDtypeStruct((steps, batch, w_out.shape[1]), bf16),
        [place, in_hbm(w_out), *early_weights, *contexts],
        in_specs=[IN_SMEM, IN_HBM] + [IN_VMEM] * (2 + batch),
        scratch=[
            pltpu.VMEM((rows, w_out.shape[1]), f32),
            pltpu.VMEM((rows, w_out.shape[1]), f32),
            pltpu.VMEM((deep, w_out.shape[1]), bf16),
            pltpu.SemaphoreType.DMA((deep // depth * 2,)),
        ],
        limit=28 * MIB,
        flops=2 * rows * w_out.size,
    )


def local(tokens, norm_gain, w_query, w_keyval, w_out, cache_keys, cache_values, lengths):
    fits = (
        lengths.shape[0] == 1
        and lax.axis_size("narrow") == 2
        and lax.axis_size("wide") == 8
        and tokens.shape[1] == 16
        and tokens.shape[2] % 128 == 0
        and tokens.shape[2] // 128 + 6 <= EXTRA
        and tokens.shape[0] * 16 <= 128
    )
    return (local_fast if fits else local_plain)(
        tokens, norm_gain, w_query, w_keyval, w_out, cache_keys, cache_values, lengths
    )


def solution(mesh):
    placed = (
        P(None, "groups", ("narrow", "wide")),
        P(("narrow", "wide")),
        P("narrow", "wide"),
        P(("narrow", "wide"), None),
        P(None, ("narrow", "wide")),
        P(("groups", "narrow", "wide"), None, None),
        P(("groups", "narrow", "wide"), None, None),
        P(("groups", "narrow", "wide")),
    )
    return jax.shard_map(
        local,
        mesh=mesh,
        in_specs=placed,
        out_specs=P(None, "groups", ("narrow", "wide")),
        check_vma=False,
    )
```

```python
import functools

import jax
import jax.numpy as jnp
from jax import lax
from jax.experimental import pallas as pl
from jax.experimental.pallas import tpu as pltpu
from jax.sharding import PartitionSpec as P

H = 48
DH = 256


epsilon = 1e-06


def rotate(vectors, positions):
    half_size = vectors.shape[-1] // 2
    ladder = jnp.arange(half_size, dtype=jnp.float32)
    frequency = jnp.exp(ladder * (-2.0 / vectors.shape[-1]) * jnp.log(10000.0))
    angles = positions[..., None] * frequency
    cosine = jnp.cos(angles)
    sine = jnp.sin(angles)
    first_half = vectors[..., :half_size]
    second_half = vectors[..., half_size:]
    return jnp.concatenate(
        [first_half * cosine - second_half * sine, second_half * cosine + first_half * sine],
        axis=-1,
    )


def attend(rot_query, cache_keys, cache_values, new_keys, new_values, lengths):
    count, steps, heads, size = rot_query.shape
    score_scale = 1.0 / jnp.sqrt(jnp.float32(DH))
    flat = rot_query.reshape(count, steps * heads, size)
    cache_scores = (
        jnp.einsum("bhd,bsd->bhs", flat, cache_keys, preferred_element_type=jnp.float32)
        * score_scale
    )
    valid = jnp.arange(cache_keys.shape[1])[None, None, :] < lengths[:, None, None]
    masked = jnp.where(valid, cache_scores, -1e30)
    fresh = (
        jnp.einsum("bhd,bjd->bhj", flat, new_keys, preferred_element_type=jnp.float32)
        * score_scale
    )
    row_step = jnp.arange(steps * heads) // heads
    seen = (jnp.arange(steps)[None, :] <= row_step[:, None])[None]
    fresh = jnp.where(seen, fresh, -1e30)
    highest = jnp.maximum(jnp.max(masked, axis=-1), jnp.max(fresh, axis=-1))[..., None]
    cache_weights = jnp.where(valid, jnp.exp(masked - highest), 0.0)
    fresh_weights = jnp.where(seen, jnp.exp(fresh - highest), 0.0)
    total = jnp.sum(cache_weights, axis=-1, keepdims=True) + jnp.sum(
        fresh_weights, axis=-1, keepdims=True
    )
    cache_probs = (cache_weights / total).astype(jnp.bfloat16)
    fresh_probs = (fresh_weights / total).astype(jnp.bfloat16)
    context = jnp.einsum(
        "bhs,bsd->bhd", cache_probs, cache_values, preferred_element_type=jnp.float32
    )
    context = context + jnp.einsum(
        "bhj,bjd->bhd", fresh_probs, new_values, preferred_element_type=jnp.float32
    )
    return context.astype(jnp.bfloat16).reshape(count, steps, heads, size)


def local_plain(tokens, norm_gain, w_query, w_keyval, w_out, cache_keys, cache_values, lengths):
    wide_count = lax.axis_size("wide")
    narrow_count = lax.axis_size("narrow")
    steps, batch, width = tokens.shape
    count = lengths.shape[0]
    rows_all = steps * batch
    width_total = width * wide_count * narrow_count
    rows_float = tokens.reshape(rows_all, width).astype(jnp.float32)
    row_sum, row_squares = lax.psum(
        (jnp.sum(rows_float, axis=1), jnp.sum(rows_float * rows_float, axis=1)),
        ("wide", "narrow"),
    )
    average = (row_sum / width_total)[:, None]
    spread = (row_squares / width_total)[:, None] - average * average
    normed = (
        (rows_float - average) * lax.rsqrt(spread + epsilon) * norm_gain.astype(jnp.float32)
    ).astype(jnp.bfloat16)
    query_part = jnp.dot(
        lax.all_gather(normed, "wide", axis=1, tiled=True),
        w_query,
        preferred_element_type=jnp.float32,
    ).reshape(steps, narrow_count, batch // narrow_count, w_query.shape[1])
    keyval_part = jnp.dot(normed, w_keyval, preferred_element_type=jnp.float32)
    keyval_part = keyval_part.reshape(steps, batch, w_keyval.shape[1])
    query_half = lax.psum_scatter(query_part, "narrow", scatter_dimension=1, tiled=False)
    query_local = lax.all_to_all(
        query_half.astype(jnp.bfloat16), "wide", split_axis=1, concat_axis=2, tiled=True
    )
    keyval_local = lax.psum_scatter(
        keyval_part, ("narrow", "wide"), scatter_dimension=1, tiled=True
    )
    positions = (lengths[:, None] + jnp.arange(steps)).astype(jnp.float32)
    query_local = query_local.astype(jnp.float32).reshape(steps, count, H, DH).transpose(1, 0, 2, 3)
    keyval_local = keyval_local.transpose(1, 0, 2)
    rot_query = rotate(query_local, positions[..., None]).astype(jnp.bfloat16)
    new_keys = rotate(keyval_local[..., :DH], positions).astype(jnp.bfloat16)
    new_values = keyval_local[..., DH:].astype(jnp.bfloat16)
    context = attend(rot_query, cache_keys, cache_values, new_keys, new_values, lengths)
    context = context.reshape(count * steps, H * DH)
    joined = jnp.dot(
        lax.all_gather(context, ("narrow", "wide"), axis=0, tiled=True),
        w_out,
        preferred_element_type=jnp.float32,
    ).astype(jnp.bfloat16)
    return joined.reshape(batch, steps, w_out.shape[1]).transpose(1, 0, 2)


MIB = 1 << 20
EXTRA = 16
OUT_CUTS = (5, 7)
IN_VMEM = pl.BlockSpec(memory_space=pltpu.VMEM)
IN_SMEM = pl.BlockSpec(memory_space=pltpu.SMEM)
IN_HBM = pl.BlockSpec(memory_space=pltpu.HBM)


def call(kernel, name, out_shape, args, in_specs=None, scratch=(), limit=12 * MIB, flops=0, moved=None, aliases=None):
    if moved is None:
        moved = sum(a.size * a.dtype.itemsize for a in args)
    return pl.pallas_call(
        kernel,
        out_shape=out_shape,
        in_specs=in_specs or [IN_VMEM] * len(args),
        out_specs=jax.tree.map(lambda _: IN_VMEM, out_shape),
        scratch_shapes=list(scratch),
        compiler_params=pltpu.CompilerParams(vmem_limit_bytes=limit),
        input_output_aliases=aliases or {},
        cost_estimate=pl.CostEstimate(flops=flops, bytes_accessed=moved, transcendentals=0),
        name=name,
    )(*args)


def in_hbm(array):
    return pltpu.with_memory_space_constraint(array, pltpu.HBM)


def load_kernel(moves, *refs):
    target, sems = refs[-2], refs[-1]
    copies = [
        pltpu.make_async_copy(refs[source].at[box], target.at[to], sems.at[at])
        for at, (source, box, to) in enumerate(moves)
    ]
    for copy in copies:
        copy.start()
    for copy in copies:
        copy.wait()


def load(name, shape, moves, *sources, after=()):
    return call(
        functools.partial(load_kernel, moves),
        name,
        pltpu.VMEM(shape, sources[0].dtype),
        [in_hbm(source) for source in sources] + list(after),
        in_specs=[IN_HBM] * len(sources) + [pl.BlockSpec(memory_space=pl.ANY)] * len(after),
        scratch=[pltpu.SemaphoreType.DMA((len(moves),))],
        limit=MIB,
        moved=2 * shape[0] * shape[1],
    )


def boxes(rows, columns, pieces, at_row=0, source=0):
    step = rows.size // pieces
    return [
        (
            source,
            (pl.ds(rows.start + at * step, step), columns),
            (pl.ds(at_row + at * step, step), pl.ds(0, columns.size)),
        )
        for at in range(pieces)
    ]


def sums_kernel(tokens, out):
    rows = tokens.shape[0]
    lanes = out.shape[1]
    values = tokens[...].astype(jnp.float32)
    at_lane = lax.broadcasted_iota(jnp.int32, (rows, lanes), 1)
    at_row = lax.broadcasted_iota(jnp.int32, (rows, lanes), 0)
    out[...] = jnp.zeros_like(out)
    for row, column in enumerate(
        (
            jnp.sum(values, axis=1, keepdims=True),
            jnp.sum(values * values, axis=1, keepdims=True),
        )
    ):
        out[row : row + 1, :] = jnp.sum(
            jnp.where(at_lane == at_row, column, 0.0), axis=0, keepdims=True
        )


def payload_kernel(tokens, gain, mine, theirs, out, extra):
    rows, width = tokens.shape
    lanes = out.shape[1]
    parts = width // lanes
    extra[...] = jnp.zeros_like(extra)
    for at in range(parts):
        span = slice(at * lanes, (at + 1) * lanes)
        extra[at : at + 1, :] = gain[:, span].astype(jnp.float32)
        out[at * rows : (at + 1) * rows, :] = tokens[:, span]
    for at in range(2):
        left = mine[at : at + 1, :] + theirs[at : at + 1, :]
        for piece in range(3):
            row = parts + 3 * at + piece
            part = left.astype(jnp.bfloat16).astype(jnp.float32)
            extra[row : row + 1, :] = part
            left = left - part
    out[parts * rows :, :] = extra[...].astype(jnp.bfloat16)


class Stream:
    def __init__(self, copies, flight=16):
        self.copies, self.started, self.done = copies, 0, 0
        self.start(flight)

    def start(self, count):
        for copy in self.copies[self.started : self.started + count]:
            copy.start()
        self.started = min(self.started + count, len(self.copies))

    def take(self, at):
        while self.done <= at:
            self.copies[self.done].wait()
            self.done += 1
            self.start(1)


def project_kernel(steps, width_total, place, w_keyval_far, w_query, early, *refs):
    *blocks, keep, send, result, normed, late, w_keyval, sems = refs
    wide_at, narrow_at = place[0], place[1]
    rows = result.shape[0]
    width, part = w_keyval.shape[0], early.shape[1]
    columns = w_query.shape[1]
    lanes = blocks[0].shape[1]
    parts = width // lanes
    spots = [
        pl.ds(pl.multiple_of(jnp.bitwise_xor(wide_at, k) * width, width), width)
        for k in range(len(blocks))
    ]
    stream = Stream(
        [pltpu.make_async_copy(w_keyval_far, w_keyval, sems.at[len(blocks)])]
        + [
            pltpu.make_async_copy(
                w_query.at[spot, pl.ds(part, columns - part)], late.at[spot], sems.at[k]
            )
            for k, spot in enumerate(spots)
        ]
    )
    tail = pl.ds(parts * rows, blocks[0].shape[0] - parts * rows)
    sums = blocks[0][tail, :].astype(jnp.float32)
    for block in blocks[1:]:
        sums = sums + block[tail, :].astype(jnp.float32)
    totals = [
        sums[at : at + 1] + sums[at + 1 : at + 2] + sums[at + 2 : at + 3]
        for at in (parts, parts + 3)
    ]
    average = totals[0] / width_total
    spread = totals[1] / width_total - average * average
    scale = lax.rsqrt(spread + epsilon)
    at_lane = lax.broadcasted_iota(jnp.int32, (rows, lanes), 1)
    at_row = lax.broadcasted_iota(jnp.int32, (rows, lanes), 0)

    def stand(flat):
        return jnp.sum(jnp.where(at_lane == at_row, flat, 0.0), axis=1, keepdims=True)

    average, scale = stand(average), stand(scale)
    for weights, span in ((early, slice(0, part)), (late, slice(part, columns))):
        for k, block in enumerate(blocks):
            if weights is early:
                gains = block[tail, :].astype(jnp.float32)
                for at in range(parts):
                    values = block[at * rows : (at + 1) * rows, :].astype(jnp.float32)
                    normed[k, :, at * lanes : (at + 1) * lanes] = (
                        (values - average) * scale * gains[at : at + 1]
                    ).astype(jnp.bfloat16)
            else:
                stream.take(k + 1)
            product = jnp.dot(normed[k], weights[spots[k], :], preferred_element_type=jnp.float32)
            if k == 0:
                result[:, span] = product
            else:
                result[:, span] += product
            if weights is early and k in (3, 6):
                stream.take(k // 3 - 1)
    result[:, columns:] = jnp.dot(normed[0], w_keyval[...], preferred_element_type=jnp.float32)
    half = rows // steps // 2
    for step in range(steps):
        for out, core in ((keep, narrow_at), (send, 1 - narrow_at)):
            start = pl.multiple_of(step * 2 * half + core * half, half)
            out[step * half : (step + 1) * half, :] = result[pl.ds(start, half), :]


def combine_kernel(columns, mine, theirs, out, held):
    wide, steps, _ = out.shape
    lanes = held.shape[2]
    extent = mine.shape[1]
    for at in range(0, extent, lanes):
        total = mine[:, at : at + lanes] + theirs[:, at : at + lanes]
        if at < columns:
            held[at // lanes] = total
        else:
            high = total.astype(jnp.bfloat16).astype(jnp.float32)
            held[at // lanes] = high
            held[(at + extent - columns) // lanes] = total - high
    for at in range(held.shape[0]):
        for to in range(wide):
            out[to, :, at * lanes : (at + 1) * lanes] = held[
                at, pl.ds(to, steps, stride=wide), :
            ].astype(jnp.bfloat16)


def attend_kernel(
    columns, length, cosine, sine, arrived, cache, out, queries, fresh_rows
):
    slots = cache.shape[0] // 2
    wide, steps, _ = arrived.shape
    size = cache.shape[1]
    half = size // 2
    heads = columns // size
    cos, sin = cosine[...], sine[...]

    def turn(vectors):
        first, second = vectors[:, :half], vectors[:, half:]
        return first * cos - second * sin, second * cos + first * sin

    for source in range(wide):
        for head in range(heads):
            at = (source * heads + head) * steps
            low, high = turn(
                arrived[source, :, head * size : (head + 1) * size].astype(jnp.float32)
            )
            queries[at : at + steps, :half] = low
            queries[at : at + steps, half:] = high
    keyval = jnp.zeros((steps, 2 * size), jnp.float32)
    for source in range(wide):
        high = arrived[source, :, columns : columns + 2 * size].astype(jnp.float32)
        low = arrived[source, :, columns + 2 * size :].astype(jnp.float32)
        keyval = keyval + (high + low)
    fresh_rows[...] = jnp.zeros_like(fresh_rows)
    low, high = turn(keyval[:, :size])
    fresh_rows[0, :steps, :half] = low
    fresh_rows[0, :steps, half:] = high
    fresh_rows[1, :steps, :] = keyval[:, size:]
    query = queries[...].astype(jnp.bfloat16)
    new_keys = fresh_rows[0].astype(jnp.bfloat16)
    new_values = fresh_rows[1].astype(jnp.bfloat16)
    score_scale = 1.0 / size**0.5
    by_row = (((1,), (1,)), ((), ()))
    scores = score_scale * lax.dot_general(
        query, cache[:slots, :], by_row, preferred_element_type=jnp.float32
    )
    fresh = score_scale * lax.dot_general(
        query, new_keys, by_row, preferred_element_type=jnp.float32
    )
    valid = lax.broadcasted_iota(jnp.int32, scores.shape, 1) < length[0]
    row_step = lax.rem(lax.broadcasted_iota(jnp.int32, fresh.shape, 0), steps)
    seen = lax.broadcasted_iota(jnp.int32, fresh.shape, 1) <= row_step
    scores = jnp.where(valid, scores, -1e30)
    fresh = jnp.where(seen, fresh, -1e30)
    highest = jnp.maximum(
        jnp.max(scores, axis=1, keepdims=True), jnp.max(fresh, axis=1, keepdims=True)
    )
    weights = jnp.where(valid, jnp.exp(scores - highest), 0.0)
    fresh_weights = jnp.where(seen, jnp.exp(fresh - highest), 0.0)
    share = 1.0 / (
        jnp.sum(weights, axis=1, keepdims=True) + jnp.sum(fresh_weights, axis=1, keepdims=True)
    )
    context = jnp.dot(
        (weights * share).astype(jnp.bfloat16),
        cache[slots:, :],
        preferred_element_type=jnp.float32,
    ) + jnp.dot(
        (fresh_weights * share).astype(jnp.bfloat16),
        new_values,
        preferred_element_type=jnp.float32,
    )
    queries[...] = context
    for head in range(wide * heads):
        out[:, head * size : (head + 1) * size] = queries[
            head * steps : (head + 1) * steps, :
        ].astype(jnp.bfloat16)


def output_kernel(steps, depth, place, w_out, *refs):
    *blocks, out, result, ordered, late, sems = refs
    parts, blocks = [*blocks[:2], late], blocks[2:]
    wide_at, narrow_at = place[0], place[1]
    batch = len(blocks)
    count = batch // 2
    pieces = sems.shape[0]
    size = late.shape[0] // pieces
    stream = Stream(
        [
            pltpu.make_async_copy(
                w_out.at[pl.ds(w_out.shape[0] - late.shape[0] + at * size, size)],
                late.at[pl.ds(at * size, size)],
                sems.at[at],
            )
            for at in range(pieces)
        ]
    )
    chunks = [(part, at) for part in parts for at in range(0, part.shape[0], depth)]
    for index, (part, inside) in enumerate(chunks):
        span = slice(index * depth, (index + 1) * depth)
        rows = jnp.concatenate([block[:, span] for block in blocks], axis=0)
        if part is late:
            stream.take((inside + depth) // size - 1)
        product = jnp.dot(rows, part[inside : inside + depth, :], preferred_element_type=jnp.float32)
        if index == 0:
            result[...] = product
        else:
            result[...] += product
        if index in (3, 5):
            stream.take(index // 2 - 1)
    for core in range(2):
        for k in range(count):
            sequence = jnp.bitwise_xor(narrow_at, core) * count + jnp.bitwise_xor(wide_at, k)
            for step in range(steps):
                row = core * count * steps + k * steps + step
                ordered[pl.ds(step * batch + sequence, 1), :] = result[row : row + 1, :]
    for step in range(steps):
        out[step] = ordered[step * batch : (step + 1) * batch, :].astype(jnp.bfloat16)


def swap(value, axis, bits):
    size = lax.axis_size(axis)
    return lax.ppermute(value, axis, [(at, at ^ bits) for at in range(size)])


def gather_tokens(block):
    near = {0: block}
    for bits in (4, 2, 1):
        near[bits] = swap(block, "wide", bits)
    near[4], near[2], near[1] = lax.optimization_barrier((near[4], near[2], near[1]))
    near[6] = swap(near[4], "wide", 2)
    near[5] = swap(near[4], "wide", 1)
    near[5], near[2] = lax.optimization_barrier((near[5], near[2]))
    near[7] = swap(near[5], "wide", 2)
    near[3] = swap(near[2], "wide", 1)
    return [near[k] for k in range(8)]


def gather_contexts(block, loader):
    near = {0: block}
    for bits in (4, 2, 1):
        near[bits] = swap(block, "wide", bits)
    first = loader(0, block)
    near[2], near[4], near[1], first = lax.optimization_barrier((near[2], near[4], near[1], first))
    near[6] = swap(near[4], "wide", 2)
    near[5] = swap(near[4], "wide", 1)
    near[3] = swap(near[2], "wide", 1)
    near[7] = swap(near[5], "wide", 2)
    second = loader(1, near[4])
    near[3], near[6], near[7], second = lax.optimization_barrier(
        (near[3], near[6], near[7], second)
    )
    return [near[k] for k in range(8)], [first, second]


def local_fast(tokens, norm_gain, w_query, w_keyval, w_out, cache_keys, cache_values, lengths):
    wide_count = lax.axis_size("wide")
    narrow_count = lax.axis_size("narrow")
    steps, batch, width = tokens.shape
    rows = steps * batch
    columns, tail = w_query.shape[1], w_keyval.shape[1]
    size = cache_keys.shape[2]
    f32, bf16 = jnp.float32, jnp.bfloat16
    place = jnp.stack([lax.axis_index("wide"), lax.axis_index("narrow")]).astype(jnp.int32)

    own = tokens.reshape(rows, width)
    sums = call(sums_kernel, "row_sums", jax.ShapeDtypeStruct((8, 128), f32), [own])
    payload = call(
        payload_kernel,
        "payload",
        jax.ShapeDtypeStruct((width // 128 * rows + EXTRA, 128), bf16),
        [own, norm_gain[None], sums, swap(sums, "narrow", 1)],
        scratch=[pltpu.VMEM((EXTRA, 128), f32)],
    )
    blocks = gather_tokens(payload)
    part = columns // 3 * 2
    deep = w_query.shape[0]
    early_weights = load(
        "load_query_weights",
        (deep, part),
        boxes(pl.ds(0, deep), pl.ds(0, part), 4),
        w_query,
    )
    keep, send = call(
        functools.partial(project_kernel, steps, width * wide_count * narrow_count),
        "norm_and_project",
        [jax.ShapeDtypeStruct((rows // 2, columns + tail), f32)] * 2,
        [place, in_hbm(w_keyval), in_hbm(w_query), early_weights, *blocks],
        in_specs=[IN_SMEM, IN_HBM, IN_HBM] + [IN_VMEM] * (wide_count + 1),
        scratch=[
            pltpu.VMEM((rows, columns + tail), f32),
            pltpu.VMEM((wide_count, rows, width), bf16),
            pltpu.VMEM((deep, columns - part), bf16),
            pltpu.VMEM(w_keyval.shape, bf16),
            pltpu.SemaphoreType.DMA((wide_count + 1,)),
        ],
        limit=24 * MIB,
        flops=2 * rows * width * wide_count * columns,
    )
    outgoing = call(
        functools.partial(combine_kernel, columns),
        "sum_of_cores",
        jax.ShapeDtypeStruct((wide_count, steps, columns + 2 * tail), bf16),
        [keep, swap(send, "narrow", 1)],
        scratch=[pltpu.VMEM(((columns + 2 * tail) // 128, rows // 2, 128), f32)],
    )
    arrived = lax.all_to_all(outgoing, "wide", 0, 0, tiled=True)
    slots = cache_keys.shape[1]
    cache = load(
        "load_cache",
        (2 * slots, size),
        boxes(pl.ds(0, slots), pl.ds(0, size), 4)
        + boxes(pl.ds(0, slots), pl.ds(0, size), 4, at_row=slots, source=1),
        cache_keys.reshape(slots, size),
        cache_values.reshape(slots, size),
        after=[outgoing],
    )
    ladder = jnp.arange(size // 2, dtype=f32)
    frequency = jnp.exp(ladder * (-2.0 / size) * jnp.log(10000.0))
    angles = (lengths + jnp.arange(steps)).astype(f32)[:, None] * frequency
    context = call(
        functools.partial(attend_kernel, columns),
        "attention",
        jax.ShapeDtypeStruct((steps, H * size), bf16),
        [lengths, jnp.cos(angles), jnp.sin(angles), arrived, cache],
        in_specs=[IN_SMEM] + [IN_VMEM] * 4,
        scratch=[
            pltpu.VMEM((steps * H, size), f32),
            pltpu.VMEM((2, 128, size), f32),
        ],
        limit=16 * MIB,
        flops=4 * steps * H * size * slots,
    )
    depth = w_out.shape[0] // 12
    bounds = (0, OUT_CUTS[0] * depth, OUT_CUTS[1] * depth, w_out.shape[0])

    def load_out(at, block):
        size = bounds[at + 1] - bounds[at]
        return load(
            "load_out_weights",
            (size, w_out.shape[1]),
            boxes(pl.ds(bounds[at], size), pl.ds(0, w_out.shape[1]), 4),
            w_out,
            after=[block],
        )

    contexts, early_weights = gather_contexts(context, load_out)
    deep = bounds[3] - bounds[2]
    contexts = contexts + [swap(block, "narrow", 1) for block in contexts]
    return call(
        functools.partial(output_kernel, steps, depth),
        "project_out",
        jax.ShapeDtypeStruct((steps, batch, w_out.shape[1]), bf16),
        [place, in_hbm(w_out), *early_weights, *contexts],
        in_specs=[IN_SMEM, IN_HBM] + [IN_VMEM] * (2 + batch),
        scratch=[
            pltpu.VMEM((rows, w_out.shape[1]), f32),
            pltpu.VMEM((rows, w_out.shape[1]), f32),
            pltpu.VMEM((deep, w_out.shape[1]), bf16),
            pltpu.SemaphoreType.DMA((deep // depth * 2,)),
        ],
        limit=28 * MIB,
        flops=2 * rows * w_out.size,
    )


def local(tokens, norm_gain, w_query, w_keyval, w_out, cache_keys, cache_values, lengths):
    fits = (
        lengths.shape[0] == 1
        and lax.axis_size("narrow") == 2
        and lax.axis_size("wide") == 8
        and tokens.shape[1] == 16
        and tokens.shape[2] % 128 == 0
        and tokens.shape[2] // 128 + 6 <= EXTRA
        and tokens.shape[0] * 16 <= 128
    )
    return (local_fast if fits else local_plain)(
        tokens, norm_gain, w_query, w_keyval, w_out, cache_keys, cache_values, lengths
    )


def solution(mesh):
    placed = (
        P(None, "groups", ("narrow", "wide")),
        P(("narrow", "wide")),
        P("narrow", "wide"),
        P(("narrow", "wide"), None),
        P(None, ("narrow", "wide")),
        P(("groups", "narrow", "wide"), None, None),
        P(("groups", "narrow", "wide"), None, None),
        P(("groups", "narrow", "wide")),
    )
    return jax.shard_map(
        local,
        mesh=mesh,
        in_specs=placed,
        out_specs=P(None, "groups", ("narrow", "wide")),
        check_vma=False,
    )
```
